32 devices in a mesh: groups: 2 (over x), dp: 16 (over z, y, core).
Axes of the slice: x: 2, y: 2, z: 4, core: 2. Of those that a mesh axis runs over, the one named last changes fastest.
Arguments:
- activations: bfloat16 [8192, 8192], P(('groups', 'dp')), parts along dimension 0, may hold values from -6 to 6
- key_grad: bfloat16 [8192, 1024], P(('groups', 'dp')), parts along dimension 0
- proj_basis: bfloat16 [16384, 512], P(('groups', 'dp')), parts along dimension 0
- master_weight: float32 [16384, 1024], P(('groups', 'dp')), parts along dimension 0, may hold values from -0.0625 to 0.0625
- first_moment: float32 [1024, 1024], P(('groups', 'dp')), parts along dimension 0, may hold values from -3 to 3
- second_moment: float32 [1024, 1024], P(('groups', 'dp')), parts along dimension 0, may hold values from 0.1 to 1
Outputs:
- activation_grad: bfloat16 [8192, 8192], P(('groups', 'dp')), parts along dimension 0
- new_master: float32 [16384, 1024], P(('groups', 'dp')), parts along dimension 0
- new_first: float32 [1024, 1024], P(('groups', 'dp')), parts along dimension 0
- new_second: float32 [1024, 1024], P(('groups', 'dp')), parts along dimension 0
The draws below stay inside these ranges and needn't reach their ends.
There are 2 independent parts, one for each index of `groups`. The reference program is written for one: setup_inputs(seed, part) draws one part's arguments, and reference() takes and returns one part's arrays. A program takes and returns all parts, laid end to end along the dimension named above; each array names one. Nothing has to cross between parts.
All inputs are finite; a program needn't handle non-finite values.
Results may differ from the reference program's by a relative error of at most 0.0049.
Values may be sent and summed in bfloat16 or wider, within the bound.
No kernel may reach another device: no remote copies, remote signals or barrier semaphores. Data moves between devices by JAX's collectives and lax.ppermute only.
A program may use at most 128 MiB of HBM per device.

```python
import math
import jax
import jax.numpy as jnp
from jax import lax

D = 8192
KV = 1024
RANK = 512
TOKENS = 4096


def draw_proj_basis(key, part):
    key = jax.random.fold_in(key, 11)
    first_key, second_key = jax.random.split(key)
    ramp = jnp.arange(RANK, dtype=jnp.float32) / RANK * 0.5
    rough = jax.random.uniform(second_key, (RANK,), jnp.float32, 0.0, 0.5)
    scales = 10.0 ** (ramp + rough)
    values = jax.random.normal(first_key, (D, RANK), jnp.float32)
    return (values * scales[None, :] / jnp.sqrt(jnp.float32(D))).astype(jnp.bfloat16)


def draw_key_grad(key, part):
    key = jax.random.fold_in(key, 23)
    first_key, second_key = jax.random.split(key, 2)
    scales = 10.0 ** jax.random.uniform(second_key, (KV,), jnp.float32, 0.0, 1.0)
    values = jax.random.normal(first_key, (TOKENS, KV), jnp.float32)
    return (values * scales[None, :]).astype(jnp.bfloat16)


def block_levels(stream_key, extent, shards, smallest, high):
    loudness = 1.0
    for axis_at, parts in shards:
        heights = jax.random.uniform(jax.random.fold_in(jax.random.fold_in(stream_key, 6), axis_at), (parts,), jnp.float32, smallest / len(shards), high / len(shards))
        loudness = loudness * jnp.repeat(jnp.exp(heights), extent[axis_at] // parts).reshape((-1,) + (1,) * (len(extent) - 1 - axis_at))
    return loudness


def gaussian(key, shape, width, limit, shards=(), kind=jnp.bfloat16):
    values = jax.random.normal(key, shape, jnp.float32) * width
    if len(shards) > 0:
        values = block_levels(key, shape, shards, -0.22, 0.18) * values
    return jnp.clip(values, min=-limit, max=limit).astype(kind)


def setup_inputs(seed: int = 0, part: int = 0) -> dict:
    arg_keys = jax.random.split(jax.random.key(seed), 7)
    own_keys = jax.random.split(jax.random.fold_in(arg_keys[6], part), 7)
    return {
        "activations": gaussian(own_keys[0], (TOKENS, D), 1.0, 6.0, ((0, 16),)),
        "key_grad": draw_key_grad(jax.random.fold_in(jax.random.fold_in(arg_keys[6], part), 71), part),
        "proj_basis": draw_proj_basis(jax.random.fold_in(jax.random.fold_in(arg_keys[6], part), 71), part),
        "master_weight": gaussian(own_keys[3], (D, KV), D ** -0.5, 0.0625, ((0, 16),), jnp.float32),
        "first_moment": gaussian(own_keys[4], (RANK, KV), 0.5, 3.0, ((0, 16),), jnp.float32),
        "second_moment": jnp.clip(jnp.exp(math.log(1.0) - 2.3025851 * jax.random.uniform(own_keys[5], (RANK, KV), jnp.float32) ** block_levels(own_keys[5], (RANK, KV), ((0, 16),), -0.2, 0.2)), 0.1, 1.0),
    }


clip_total = 512.0
step_size = 0.01
first_fix = 1.0 - 0.9 ** 10
second_fix = 1.0 - 0.99 ** 10

def reference(activations, key_grad, proj_basis, master_weight, first_moment, second_moment):
    weight_bf16 = master_weight.astype(jnp.bfloat16)
    activation_grad = jnp.dot(key_grad, weight_bf16.T, preferred_element_type=jnp.float32).astype(jnp.bfloat16)
    projected = jnp.dot(activations, proj_basis, preferred_element_type=jnp.float32).astype(jnp.bfloat16)
    proj_grad = jnp.dot(projected.T, key_grad, preferred_element_type=jnp.float32)
    grad_norm = jnp.sqrt(jnp.sum(proj_grad * proj_grad))
    factor = jnp.minimum(1.0, clip_total / (grad_norm + 1e-06))
    clipped = proj_grad * factor
    new_first = 0.9 * first_moment + 0.1 * clipped
    new_second = 0.99 * second_moment + 0.01 * clipped * clipped
    update = new_first / first_fix / (jnp.sqrt(new_second / second_fix) + 1e-08)
    back_step = jnp.dot(proj_basis.astype(jnp.float32), update, precision=lax.Precision.HIGHEST)
    new_master = master_weight - step_size * back_step
    return (activation_grad, new_master, new_first, new_second)
```

```python
import jax
import jax.numpy as jnp
from jax import lax
from jax.sharding import PartitionSpec as P

clip_total = 512.0
step_size = 0.01
first_fix = 1.0 - 0.9**10
second_fix = 1.0 - 0.99**10

f32 = jnp.float32
bf16 = jnp.bfloat16


def after(value, *others):
    return lax.optimization_barrier((value,) + others)[0]


def make_per_device(n):
    members = 4 if n == 16 else 2
    ring = n // members
    order = [0, 1, 3, 2] if ring == 4 else list(range(ring))
    forward = [
        (order[k] * members + m, order[(k + 1) % ring] * members + m)
        for k in range(ring)
        for m in range(members)
    ]

    def send_xor(value, bit):
        return lax.ppermute(value, "dp", [(i, i ^ bit) for i in range(n)])

    def per_device(activations, key_grad, proj_basis, master_weight, first_moment, second_moment):
        tokens, width = activations.shape
        rows, rank = proj_basis.shape
        outs = key_grad.shape[1]
        index = lax.axis_index("dp")
        member = index % members
        place = jnp.asarray([order.index(z) for z in range(ring)], jnp.int32)[index // members]
        source = [
            jnp.asarray(order, jnp.int32)[(place - s + ring) % ring] for s in range(ring)
        ]

        if members == 4:
            far = send_xor(key_grad, 2)
            near = send_xor(jnp.concatenate([key_grad, far], axis=0), 1)
            plane_grad = jnp.concatenate(
                [key_grad, near[:tokens], far, near[tokens:]], axis=0
            )
        else:
            plane_grad = jnp.concatenate([key_grad, send_xor(key_grad, 1)], axis=0)

        def columns(m):
            return jnp.concatenate(
                [
                    lax.dynamic_slice(
                        activations, (0, (source[s] * members + m) * rows), (tokens, rows)
                    )
                    for s in range(ring)
                ],
                axis=1,
            )

        plane_act = [columns(member)]
        for x in range(1, members):
            plane_act.append(send_xor(columns(member ^ x), x))
        plane_act = jnp.concatenate(plane_act, axis=0)

        basis = [proj_basis]
        for s in range(1, ring):
            basis.append(lax.ppermute(basis[-1], "dp", forward))
        ring_basis = jnp.concatenate(basis, axis=0)

        projected = jnp.dot(plane_act, ring_basis, preferred_element_type=f32).astype(bf16)
        partial_grad = lax.dot_general(
            projected, plane_grad, (((0,), (0,)), ((), ())), preferred_element_type=f32
        )

        weight = master_weight.astype(bf16)
        weight = after(weight, basis[ring - 2])
        activation_grad = jnp.zeros((tokens, width), bf16)
        for s in range(ring):
            if s > 0:
                weight = lax.ppermute(weight, "dp", forward)
            block = lax.dot_general(
                plane_grad, weight, (((1,), (1,)), ((), ())), preferred_element_type=f32
            ).astype(bf16)
            for x in range(members):
                piece = block[x * tokens : (x + 1) * tokens]
                if x > 0:
                    piece = send_xor(piece, x)
                activation_grad = lax.dynamic_update_slice(
                    activation_grad, piece, (0, (source[s] * members + (member ^ x)) * rows)
                )

        owned = rank // n
        bits = [1 << b for b in range(n.bit_length() - 1)]
        total = partial_grad.reshape(n, owned, outs)
        for bit in bits:
            mine = (index // bit) % 2
            total = total.reshape(total.shape[0] // 2, 2, owned, outs)
            kept = lax.dynamic_index_in_dim(total, mine, 1, keepdims=False)
            given = lax.dynamic_index_in_dim(total, 1 - mine, 1, keepdims=False)
            total = kept + send_xor(given.astype(bf16), bit).astype(f32)
        owned_rows = total.reshape(owned, outs)

        square_sum = jnp.broadcast_to(jnp.sum(owned_rows * owned_rows), (8, 128))
        for bit in reversed(bits):
            square_sum = square_sum + send_xor(square_sum, bit)
        grad_norm = jnp.sqrt(square_sum[0, 0])
        factor = jnp.minimum(1.0, clip_total / (grad_norm + 1e-06))
        clipped = owned_rows * factor
        new_first = 0.9 * first_moment + 0.1 * clipped
        new_second = 0.99 * second_moment + 0.01 * clipped * clipped
        update = new_first / first_fix / (jnp.sqrt(new_second / second_fix) + 1e-08)

        whole = update.astype(bf16).reshape(1, owned, outs)
        for bit in reversed(bits):
            other = send_xor(whole, bit)
            pair = jnp.where(
                (index // bit) % 2 == 0,
                jnp.stack([whole, other], axis=1),
                jnp.stack([other, whole], axis=1),
            )
            whole = pair.reshape(2 * whole.shape[0], owned, outs)
        back_step = jnp.dot(
            proj_basis, whole.reshape(rank, outs), preferred_element_type=f32
        )
        new_master = master_weight - step_size * back_step
        return (activation_grad, new_master, new_first, new_second)

    return per_device


def solution(mesh):
    spec = P(("groups", "dp"), None)
    return jax.shard_map(
        make_per_device(mesh.shape["dp"]),
        mesh=mesh,
        in_specs=(spec,) * 6,
        out_specs=(spec,) * 4,
        check_vma=False,
    )
```

```python
import jax
import jax.numpy as jnp
from jax import lax
from jax.sharding import PartitionSpec as P

clip_total = 512.0
step_size = 0.01
first_fix = 1.0 - 0.9**10
second_fix = 1.0 - 0.99**10

f32 = jnp.float32
bf16 = jnp.bfloat16


def after(value, *others):
    return lax.optimization_barrier((value,) + others)[0]


def make_per_device(n):
    sides = 2 if n == 16 else 1
    ring = n // (2 * sides)
    order = [0, 1, 3, 2] if ring == 4 else list(range(ring))
    forward = [
        ((order[k] * 2 * sides) + m, order[(k + 1) % ring] * 2 * sides + m)
        for k in range(ring)
        for m in range(2 * sides)
    ]
    rounds = [(1, 2)]
    bit = 2
    if sides == 2:
        rounds.append((2, 2))
        bit = 4
    while bit < n:
        radix = 4 if 2 * bit < n else 2
        rounds.append((bit, radix))
        bit *= radix

    def swap(value, bit):
        return lax.ppermute(value, "dp", [(i, i ^ bit) for i in range(n)])

    def onward(value):
        return lax.ppermute(value, "dp", forward)

    def per_device(activations, key_grad, proj_basis, master_weight, first_moment, second_moment):
        tokens = activations.shape[0]
        rows, rank = proj_basis.shape
        outs = key_grad.shape[1]
        half = rows // 2
        index = lax.axis_index("dp")
        core = index & 1
        side = (index >> 1) & (sides - 1)
        zplace = lax.shift_right_logical(index, 1 if sides == 1 else 2)
        if ring == 4:
            place = zplace ^ (zplace >> 1)
        else:
            place = zplace

        def source(s):
            k = (place - s) & (ring - 1)
            return k ^ (k >> 1) if ring == 4 else k

        def block_at(s, side_):
            return (source(s) * sides + side_) * (2 * rows)

        def pair(mine, theirs):
            return jnp.where(
                core == 0,
                jnp.concatenate([mine, theirs], axis=0),
                jnp.concatenate([theirs, mine], axis=0),
            )

        def act_columns(s, side_):
            return lax.dynamic_slice(activations, (0, block_at(s, side_)), (tokens, 2 * rows))

        basis = [proj_basis]
        for s in range(1, ring):
            basis.append(onward(basis[-1]))
        basis_pair = [pair(b, swap(b, 1)) for b in basis]

        weight = master_weight.astype(bf16)
        low, high = [weight[:half]], [weight[half:]]
        for s in range(1, ring):
            low.append(onward(after(low[-1], basis[ring - 1]) if s == 2 else low[-1]))
        for s in range(1, ring):
            high.append(onward(after(high[-1], basis[ring - 2]) if s == 1 else high[-1]))

        grads = [key_grad]
        acts = [[act_columns(s, side) for s in range(ring)]]
        if sides == 2:
            acts.append([swap(act_columns(s, 1 - side), 2) for s in range(ring)])
            grads.append(swap(key_grad, 2))

        partial_grad = 0.0
        for x in range(sides):
            projected = 0.0
            for s in range(ring):
                projected = projected + jnp.dot(
                    acts[x][s], basis_pair[s], preferred_element_type=f32
                )
            partial_grad = partial_grad + lax.dot_general(
                projected.astype(bf16),
                grads[x],
                (((0,), (0,)), ((), ())),
                preferred_element_type=f32,
            )

        activation_grad = jnp.zeros(activations.shape, bf16)
        for s in range(ring):
            wide = pair(
                jnp.concatenate([low[s], high[s]], axis=0),
                jnp.concatenate([swap(low[s], 1), swap(high[s], 1)], axis=0),
            )
            for x in reversed(range(sides)):
                block = lax.dot_general(
                    grads[x], wide, (((1,), (1,)), ((), ())), preferred_element_type=f32
                ).astype(bf16)
                if x > 0:
                    block = swap(block, 2)
                activation_grad = lax.dynamic_update_slice(
                    activation_grad, block, (0, block_at(s, side ^ x))
                )

        owned = rank // n
        total = partial_grad.reshape(n, owned, outs)
        for bit, radix in rounds:
            digit = (index // bit) & (radix - 1)
            total = total.reshape(total.shape[0] // radix, radix, owned, outs)
            kept = lax.dynamic_index_in_dim(total, digit, 1, keepdims=False)
            for j in range(1, radix):
                given = lax.dynamic_index_in_dim(total, digit ^ j, 1, keepdims=False)
                kept = kept + swap(given.astype(bf16), j * bit).astype(f32)
            total = kept
        owned_rows = total.reshape(owned, outs)

        square_sum = jnp.broadcast_to(jnp.sum(owned_rows * owned_rows), (8, 128))
        for bit, radix in reversed(rounds):
            square_sum = sum([swap(square_sum, j * bit) for j in range(1, radix)], square_sum)
        grad_norm = jnp.sqrt(square_sum[0, 0])
        factor = jnp.minimum(1.0, clip_total / (grad_norm + 1e-06))
        clipped = owned_rows * factor
        new_first = 0.9 * first_moment + 0.1 * clipped
        new_second = 0.99 * second_moment + 0.01 * clipped * clipped
        update = new_first / first_fix / (jnp.sqrt(new_second / second_fix) + 1e-08)

        whole = update.astype(bf16).reshape(1, owned, outs)
        for bit, radix in reversed(rounds):
            digit = (index // bit) & (radix - 1)
            found = [whole] + [swap(whole, j * bit) for j in range(1, radix)]
            ordered = []
            for d in range(radix):
                pick = found[d]
                for j in range(radix):
                    if j != d:
                        pick = jnp.where(digit == (d ^ j), found[j], pick)
                ordered.append(pick)
            whole = jnp.stack(ordered, axis=1).reshape(radix * whole.shape[0], owned, outs)
        back_step = jnp.dot(
            proj_basis, whole.reshape(rank, outs), preferred_element_type=f32
        )
        new_master = master_weight - step_size * back_step
        return (activation_grad, new_master, new_first, new_second)

    return per_device


def solution(mesh):
    spec = P(("groups", "dp"), None)
    return jax.shard_map(
        make_per_device(mesh.shape["dp"]),
        mesh=mesh,
        in_specs=(spec,) * 6,
        out_specs=(spec,) * 4,
        check_vma=False,
    )
```

```python
import functools
import jax
import jax.numpy as jnp
from jax import lax
from jax.experimental import pallas as pl
from jax.experimental.pallas import tpu as pltpu
from jax.sharding import PartitionSpec as P

clip_total = 512.0
step_size = 0.01
first_fix = 1.0 - 0.9**10
second_fix = 1.0 - 0.99**10

f32 = jnp.float32
bf16 = jnp.bfloat16
HBM = pl.BlockSpec(memory_space=pl.ANY)
VMEM = pl.BlockSpec(memory_space=pltpu.VMEM)
PARAMS = pltpu.CompilerParams(vmem_limit_bytes=40 * 2**20)


def after(value, *others):
    return lax.optimization_barrier((value,) + others)[0]


class Layout:
    def __init__(self, n):
        self.n = n
        self.sides = 2 if n == 16 else 1
        self.members = 2 * self.sides
        self.ring = n // self.members
        ring, members = self.ring, self.members
        order = [0, 1, 3, 2] if ring == 4 else list(range(ring))
        self.forward = [
            (order[k] * members + m, order[(k + 1) % ring] * members + m)
            for k in range(ring)
            for m in range(members)
        ]
        self.rounds = [(1, 2)]
        bit = 2
        if self.sides == 2:
            self.rounds.append((2, 2))
            bit = 4
        while bit < n:
            radix = 4 if 2 * bit < n else 2
            self.rounds.append((bit, radix))
            bit *= radix

    def swap(self, value, bit):
        return lax.ppermute(value, "dp", [(i, i ^ bit) for i in range(self.n)])

    def onward(self, value):
        return lax.ppermute(value, "dp", self.forward)

    def source(self, index, s):
        z = index // self.members
        if self.ring != 4:
            return (z - s + self.ring) % self.ring
        k = (z + z // 2 * (5 - 2 * z) - s + 4) % 4
        return k + k // 2 * (5 - 2 * k)


def flip(value, bit):
    return value + bit - 2 * bit * ((value // bit) % 2)


def cut_kernel(lay, rows, act, *refs):
    pieces, sems = refs[:-1], refs[-1]
    index = lax.axis_index("dp")
    member = index % lay.members
    copies = []
    for x in reversed(range(lay.members)):
        owner = member
        for bit in (1, 2):
            if x & bit:
                owner = flip(owner, bit)
        for s in range(lay.ring):
            start = pl.multiple_of((lay.source(index, s) * lay.members + owner) * rows, rows)
            copies.append(
                pltpu.make_async_copy(
                    act.at[:, pl.ds(start, rows)],
                    pieces[x].at[:, pl.ds(s * rows, rows)],
                    sems.at[x * lay.ring + s],
                )
            )
    for copy in copies:
        copy.start()
    for copy in copies:
        copy.wait()


def project_kernel(lay, owned, *refs):
    members, ring = lay.members, lay.ring
    acts, refs = refs[:members], refs[members:]
    basis, refs = refs[:ring], refs[ring:]
    grads, refs = refs[:members], refs[members:]
    kept, given, grad = refs
    rows = basis[0].shape[0]
    core = lax.axis_index("dp") % 2
    for x in range(members):
        total = jnp.dot(acts[x][:, :rows], basis[0][...], preferred_element_type=f32)
        for s in range(1, ring):
            total += jnp.dot(
                acts[x][:, s * rows : (s + 1) * rows],
                basis[s][...],
                preferred_element_type=f32,
            )
        term = lax.dot_general(
            total.astype(bf16),
            grads[x][...],
            (((0,), (0,)), ((), ())),
            preferred_element_type=f32,
        )
        if x == 0:
            grad[...] = term
        else:
            grad[...] += term
    for i in range(lay.n // 2):
        kept[i] = grad[pl.ds(pl.multiple_of((2 * i + core) * owned, owned), owned), :]
        given[i] = grad[pl.ds(pl.multiple_of((2 * i + 1 - core) * owned, owned), owned), :].astype(bf16)


def place(lay, s, side, low, width, rows, source, out, sems):
    index = lax.axis_index("dp")
    core = index % 2
    chip = lay.source(index, s) * lay.sides + side
    copies = []
    for k, owner in enumerate((core, 1 - core)):
        start = pl.multiple_of((chip * 2 + owner) * rows + low, width)
        copies.append(
            pltpu.make_async_copy(
                source.at[:, pl.ds(k * width, width)],
                out.at[:, pl.ds(start, width)],
                sems.at[k],
            )
        )
    return copies


def weight_kernel(lay, rows, s, low, parts, came, first, *refs):
    sides = lay.sides
    mine, refs = refs[:parts], refs[parts:]
    theirs, refs = refs[:parts], refs[parts:]
    grads, refs = refs[:sides], refs[sides:]
    if came is not None:
        arrived, refs = refs[0], refs[1:]
    if not first:
        refs = refs[1:]
    out, refs = refs[0], refs[1:]
    if sides == 2:
        far, refs = refs[0], refs[1:]
    own, sems, came_sems = refs
    height = mine[0].shape[0]
    width = parts * height
    side = (lax.axis_index("dp") // 2) % sides
    copies = []
    if came is not None:
        copies = place(
            lay, came[0], 1 - side, came[1], arrived.shape[1] // 2, rows, arrived, out, came_sems
        )
        for copy in copies:
            copy.start()
    for x in reversed(range(sides)):
        target = own if x == 0 else far
        for k, group in enumerate((mine, theirs)):
            for p, piece in enumerate(group):
                target[:, k * width + p * height : k * width + (p + 1) * height] = lax.dot_general(
                    grads[x][...],
                    piece[...],
                    (((1,), (1,)), ((), ())),
                    preferred_element_type=f32,
                ).astype(bf16)
    owns = place(lay, s, side, low, width, rows, own, out, sems)
    for copy in owns:
        copy.start()
    for copy in owns + copies:
        copy.wait()


def last_kernel(lay, rows, s, low, arrived, before, out, sems):
    side = (lax.axis_index("dp") // 2) % lay.sides
    copies = place(lay, s, 1 - side, low, arrived.shape[1] // 2, rows, arrived, out, sems)
    for copy in copies:
        copy.start()
    for copy in copies:
        copy.wait()


def back_kernel(lay, owned, basis, near, other, master, out, update):
    index = lax.axis_index("dp")
    half = lay.n // 2
    for j in range(lay.n):
        owner = index
        for bit in [1 << b for b in range(lay.n.bit_length() - 1)]:
            if slot_to_xor(lay, j) & bit:
                owner = flip(owner, bit)
        piece = near[j] if j < half else other[j - half]
        update[pl.ds(pl.multiple_of(owner * owned, owned), owned), :] = piece.astype(f32)
    out[...] = master[...] - step_size * jnp.dot(
        basis[...], update[...].astype(bf16), preferred_element_type=f32
    )


def slot_to_xor(lay, j):
    xor = 0
    for bit, radix in reversed(lay.rounds):
        xor += (j % radix) * bit
        j //= radix
    return xor


def make_per_device(n):
    lay = Layout(n)
    sides, members, ring, rounds = lay.sides, lay.members, lay.ring, lay.rounds
    swap, onward = lay.swap, lay.onward

    def per_device(activations, key_grad, proj_basis, master_weight, first_moment, second_moment):
        tokens = activations.shape[0]
        rows, rank = proj_basis.shape
        outs = key_grad.shape[1]
        index = lax.axis_index("dp")
        owned = rank // n
        parts = 2 if rows % 256 == 0 else 1
        height = rows // parts

        cut = pl.pallas_call(
            functools.partial(cut_kernel, lay, rows),
            name="cut",
            out_shape=[jax.ShapeDtypeStruct((tokens, ring * rows), bf16)] * members,
            in_specs=[HBM],
            out_specs=[VMEM] * members,
            scratch_shapes=[pltpu.SemaphoreType.DMA((members * ring,))],
            compiler_params=PARAMS,
            cost_estimate=pl.CostEstimate(
                flops=0, bytes_accessed=4 * tokens * ring * rows * members, transcendentals=0
            ),
        )(activations)
        acts = [cut[0]] + [swap(cut[x], x) for x in range(1, members)]

        weight = master_weight.astype(bf16)
        basis = [proj_basis]
        mine = [[weight[p * height : (p + 1) * height] for p in range(parts)]]
        for s in range(1, ring):
            value = basis[-1]
            if s == 2:
                value = started = after(value, cut[1])
            if s == 3:
                value = after(value, first_part)
            basis.append(onward(value))
            if s == 1:
                first_part = onward(mine[0][0])
        for s in range(1, ring):
            step = []
            for p in range(parts):
                value = mine[-1][p]
                if s == 1 and p == 0:
                    step.append(first_part)
                    continue
                if s == 1:
                    value = after(value, basis[ring - 2])
                if s == 2 and p == 0:
                    value = after(value, basis[ring - 1])
                step.append(onward(value))
            mine.append(step)
        theirs = [[swap(piece, 1) for piece in step] for step in mine]

        grads = [key_grad]
        if sides == 2:
            far_grad = swap(key_grad, 2)
            near = swap(
                jnp.concatenate([key_grad, after(far_grad, started)], axis=0), 1
            )
            grads = [key_grad, near[:tokens], far_grad, near[tokens:]]
        else:
            grads = [key_grad, swap(key_grad, 1)]

        total, given = pl.pallas_call(
            functools.partial(project_kernel, lay, owned),
            name="project",
            out_shape=[
                jax.ShapeDtypeStruct((n // 2, owned, outs), f32),
                jax.ShapeDtypeStruct((n // 2, owned, outs), bf16),
            ],
            in_specs=[VMEM] * (2 * members + ring),
            out_specs=[VMEM] * 2,
            scratch_shapes=[pltpu.VMEM((rank, outs), f32)],
            compiler_params=PARAMS,
            cost_estimate=pl.CostEstimate(
                flops=2 * tokens * members * rank * (ring * rows + outs),
                bytes_accessed=12 * 2**20,
                transcendentals=0,
            ),
        )(*acts, *basis, *grads)

        side_grads = [key_grad, far_grad] if sides == 2 else [key_grad]
        activation_grad = None
        waiting = None
        for s in range(ring):
            groups = [range(parts)] if s < ring - 1 else [[p] for p in range(parts)]
            for group in groups:
                low = group[0] * height
                width = len(group) * height
                args = [mine[s][p] for p in group] + [theirs[s][p] for p in group] + side_grads
                specs = [VMEM] * len(args)
                came = None
                if waiting is not None:
                    came = waiting[:2]
                    args.append(waiting[2])
                    specs.append(VMEM)
                first = activation_grad is None
                if not first:
                    args.append(activation_grad)
                    specs.append(HBM)
                shapes = [jax.ShapeDtypeStruct(activations.shape, bf16)]
                out_specs = [HBM]
                if sides == 2:
                    shapes.append(jax.ShapeDtypeStruct((tokens, 2 * width), bf16))
                    out_specs.append(VMEM)
                result = pl.pallas_call(
                    functools.partial(
                        weight_kernel, lay, rows, s, low, len(group), came, first
                    ),
                    name="weight",
                    out_shape=shapes,
                    in_specs=specs,
                    out_specs=out_specs,
                    scratch_shapes=[
                        pltpu.VMEM((tokens, 2 * width), bf16),
                        pltpu.SemaphoreType.DMA((2,)),
                        pltpu.SemaphoreType.DMA((2,)),
                    ],
                    input_output_aliases={} if first else {len(args) - 1: 0},
                    compiler_params=PARAMS,
                    cost_estimate=pl.CostEstimate(
                        flops=4 * sides * tokens * width * outs,
                        bytes_accessed=8 * 2**20,
                        transcendentals=0,
                    ),
                )(*args)
                activation_grad = result[0]
                if sides == 2:
                    waiting = (s, low, swap(result[1], 2))
        if waiting is not None:
            activation_grad = pl.pallas_call(
                functools.partial(last_kernel, lay, rows, waiting[0], waiting[1]),
                name="last",
                out_shape=jax.ShapeDtypeStruct(activations.shape, bf16),
                in_specs=[VMEM, HBM],
                out_specs=HBM,
                scratch_shapes=[pltpu.SemaphoreType.DMA((2,))],
                input_output_aliases={1: 0},
                compiler_params=PARAMS,
            )(waiting[2], activation_grad)

        for bit, radix in rounds:
            digit = (index // bit) % radix
            if bit == 1:
                total = total + swap(after(given, mine[1][-1]), 1).astype(f32)
                continue
            if bit == members:
                total = after(total, mine[2][0])
            total = total.reshape(total.shape[0] // radix, radix, owned, outs)
            kept = lax.dynamic_index_in_dim(total, digit, 1, keepdims=False)
            for j in range(1, radix):
                give = lax.dynamic_index_in_dim(total, digit ^ j, 1, keepdims=False)
                kept = kept + swap(give.astype(bf16), j * bit).astype(f32)
            total = kept
        owned_rows = total.reshape(owned, outs)

        square_sum = jnp.broadcast_to(jnp.sum(owned_rows * owned_rows), (8, 128))
        for bit, radix in reversed(rounds):
            square_sum = sum([swap(square_sum, j * bit) for j in range(1, radix)], square_sum)
        grad_norm = jnp.sqrt(square_sum[0, 0])
        factor = jnp.minimum(1.0, clip_total / (grad_norm + 1e-06))
        clipped = owned_rows * factor
        new_first = 0.9 * first_moment + 0.1 * clipped
        new_second = 0.99 * second_moment + 0.01 * clipped * clipped
        update = new_first / first_fix / (jnp.sqrt(new_second / second_fix) + 1e-08)

        whole = after(update.astype(bf16).reshape(1, owned, outs), mine[2][-1])
        for bit, radix in reversed(rounds[1:]):
            whole = jnp.concatenate(
                [whole] + [swap(whole, j * bit) for j in range(1, radix)], axis=0
            )
        new_master = pl.pallas_call(
            functools.partial(back_kernel, lay, owned),
            name="back",
            out_shape=jax.ShapeDtypeStruct(master_weight.shape, f32),
            in_specs=[VMEM] * 4,
            out_specs=VMEM,
            scratch_shapes=[pltpu.VMEM((rank, outs), f32)],
            compiler_params=PARAMS,
            cost_estimate=pl.CostEstimate(
                flops=2 * rows * rank * outs, bytes_accessed=8 * 2**20, transcendentals=0
            ),
        )(proj_basis, whole, swap(whole, 1), master_weight)
        return (activation_grad, new_master, new_first, new_second)

    return per_device


def solution(mesh):
    spec = P(("groups", "dp"), None)
    return jax.shard_map(
        make_per_device(mesh.shape["dp"]),
        mesh=mesh,
        in_specs=(spec,) * 6,
        out_specs=(spec,) * 4,
        check_vma=False,
    )
```

```python
import functools
import jax
import jax.numpy as jnp
from jax import lax
from jax.experimental import pallas as pl
from jax.experimental.pallas import tpu as pltpu
from jax.sharding import PartitionSpec as P

clip_total = 512.0
step_size = 0.01
first_fix = 1.0 - 0.9**10
second_fix = 1.0 - 0.99**10

f32 = jnp.float32
bf16 = jnp.bfloat16
HBM = pl.BlockSpec(memory_space=pl.ANY)
VMEM = pl.BlockSpec(memory_space=pltpu.VMEM)
PARAMS = pltpu.CompilerParams(vmem_limit_bytes=40 * 2**20)


def after(value, *others):
    return lax.optimization_barrier((value,) + others)[0]


class Layout:
    def __init__(self, n):
        self.n = n
        self.sides = 2 if n == 16 else 1
        self.members = 2 * self.sides
        self.ring = n // self.members
        ring, members = self.ring, self.members
        order = [0, 1, 3, 2] if ring == 4 else list(range(ring))
        self.forward = [
            (order[k] * members + m, order[(k + 1) % ring] * members + m)
            for k in range(ring)
            for m in range(members)
        ]
        self.rounds = [(1, 2)]
        bit = 2
        if self.sides == 2:
            self.rounds.append((2, 2))
            bit = 4
        while bit < n:
            radix = 4 if 2 * bit < n else 2
            self.rounds.append((bit, radix))
            bit *= radix

    def swap(self, value, bit):
        return lax.ppermute(value, "dp", [(i, i ^ bit) for i in range(self.n)])

    def onward(self, value):
        return lax.ppermute(value, "dp", self.forward)

    def source(self, index, s):
        z = index // self.members
        if self.ring != 4:
            return (z - s + self.ring) % self.ring
        k = (z + z // 2 * (5 - 2 * z) - s + 4) % 4
        return k + k // 2 * (5 - 2 * k)


def flip(value, bit):
    return value + bit - 2 * bit * ((value // bit) % 2)


def cut_kernel(lay, rows, plan, act, *refs):
    pieces, sems = refs[:-1], refs[-1]
    index = lax.axis_index("dp")
    member = index % lay.members
    copies = []
    for (x, first, count), piece in zip(plan, pieces):
        owner = member
        for bit in (1, 2):
            if x & bit:
                owner = flip(owner, bit)
        for s in range(first, first + count):
            start = pl.multiple_of((lay.source(index, s) * lay.members + owner) * rows, rows)
            copies.append(
                pltpu.make_async_copy(
                    act.at[:, pl.ds(start, rows)],
                    piece.at[:, pl.ds((s - first) * rows, rows)],
                    sems.at[len(copies)],
                )
            )
    for copy in copies:
        copy.start()
    for copy in copies:
        copy.wait()


def project_kernel(lay, owned, plan, *refs):
    members, ring = lay.members, lay.ring
    acts, refs = refs[: len(plan)], refs[len(plan) :]
    basis, refs = refs[:ring], refs[ring:]
    grads, refs = refs[:members], refs[members:]
    kept, given, grad = refs
    rows = basis[0].shape[0]
    core = lax.axis_index("dp") % 2
    for x in range(members):
        total = None
        for (x_, first, count), piece in zip(plan, acts):
            if x_ != x:
                continue
            for s in range(first, first + count):
                term = jnp.dot(
                    piece[:, (s - first) * rows : (s - first + 1) * rows],
                    basis[s][...],
                    preferred_element_type=f32,
                )
                total = term if total is None else total + term
        term = lax.dot_general(
            total.astype(bf16),
            grads[x][...],
            (((0,), (0,)), ((), ())),
            preferred_element_type=f32,
        )
        if x == 0:
            grad[...] = term
        else:
            grad[...] += term
    for i in range(lay.n // 2):
        kept[i] = grad[pl.ds(pl.multiple_of((2 * i + core) * owned, owned), owned), :]
        given[i] = grad[pl.ds(pl.multiple_of((2 * i + 1 - core) * owned, owned), owned), :].astype(bf16)


def fold_kernel(bit, radix, came, *refs):
    kept, arrived, outs = refs[0], refs[1 : 1 + came], refs[1 + came :]
    digit = (lax.axis_index("dp") // bit) % radix

    def block(i):
        total = kept[i]
        for piece in arrived:
            total = total + piece[i].astype(f32)
        return total

    for i in range(kept.shape[0] // radix):
        for j in range(radix):
            other = digit
            for b in (1, 2):
                if j & b:
                    other = flip(other, b)
            value = block(i * radix + other)
            outs[j][i] = value.astype(outs[j].dtype)


def square_kernel(came, *refs):
    kept, arrived, (owned, square) = refs[0], refs[1 : 1 + came], refs[1 + came :]
    total = kept[0]
    for piece in arrived:
        total = total + piece[0].astype(f32)
    owned[...] = total
    square[...] = jnp.full(square.shape, jnp.sum(total * total), f32)


def moment_kernel(count, *refs):
    squares, (owned, first, second, new_first, new_second, update) = refs[:count], refs[count:]
    total = squares[0][...]
    for square in squares[1:]:
        total = total + square[...]
    factor = jnp.minimum(1.0, clip_total / (jnp.sqrt(total) + 1e-06))[0:1, 0:1]
    clipped = owned[...] * factor
    one = 0.9 * first[...] + 0.1 * clipped
    two = 0.99 * second[...] + 0.01 * clipped * clipped
    new_first[...] = one
    new_second[...] = two
    update[0] = (one / first_fix / (jnp.sqrt(two / second_fix) + 1e-08)).astype(bf16)


def place(lay, s, side, low, width, rows, source, out, sems):
    index = lax.axis_index("dp")
    core = index % 2
    chip = lay.source(index, s) * lay.sides + side
    copies = []
    for k, owner in enumerate((core, 1 - core)):
        start = pl.multiple_of((chip * 2 + owner) * rows + low, width)
        copies.append(
            pltpu.make_async_copy(
                source.at[:, pl.ds(k * width, width)],
                out.at[:, pl.ds(start, width)],
                sems.at[k],
            )
        )
    return copies


def weight_kernel(lay, rows, s, low, parts, came, first, *refs):
    sides = lay.sides
    mine, refs = refs[:parts], refs[parts:]
    theirs, refs = refs[:parts], refs[parts:]
    grads, refs = refs[:sides], refs[sides:]
    if came is not None:
        arrived, refs = refs[0], refs[1:]
    if not first:
        refs = refs[1:]
    out, refs = refs[0], refs[1:]
    if sides == 2:
        far, refs = refs[0], refs[1:]
    own, sems, came_sems = refs
    height = mine[0].shape[0]
    width = parts * height
    side = (lax.axis_index("dp") // 2) % sides
    copies = []
    if came is not None:
        copies = place(
            lay, came[0], 1 - side, came[1], arrived.shape[1] // 2, rows, arrived, out, came_sems
        )
        for copy in copies:
            copy.start()
    for x in reversed(range(sides)):
        target = own if x == 0 else far
        for k, group in enumerate((mine, theirs)):
            for p, piece in enumerate(group):
                target[:, k * width + p * height : k * width + (p + 1) * height] = lax.dot_general(
                    grads[x][...],
                    piece[...],
                    (((1,), (1,)), ((), ())),
                    preferred_element_type=f32,
                ).astype(bf16)
    owns = place(lay, s, side, low, width, rows, own, out, sems)
    for copy in owns:
        copy.start()
    for copy in owns + copies:
        copy.wait()


def last_kernel(lay, rows, s, low, arrived, before, out, sems):
    side = (lax.axis_index("dp") // 2) % lay.sides
    copies = place(lay, s, 1 - side, low, arrived.shape[1] // 2, rows, arrived, out, sems)
    for copy in copies:
        copy.start()
    for copy in copies:
        copy.wait()


def back_kernel(lay, owned, basis, near, other, master, out, update):
    index = lax.axis_index("dp")
    half = lay.n // 2
    for j in range(lay.n):
        owner = index
        for bit in [1 << b for b in range(lay.n.bit_length() - 1)]:
            if slot_to_xor(lay, j) & bit:
                owner = flip(owner, bit)
        piece = near[j] if j < half else other[j - half]
        update[pl.ds(pl.multiple_of(owner * owned, owned), owned), :] = piece.astype(f32)
    out[...] = master[...] - step_size * jnp.dot(
        basis[...], update[...].astype(bf16), preferred_element_type=f32
    )


def slot_to_xor(lay, j):
    xor = 0
    for bit, radix in reversed(lay.rounds):
        xor += (j % radix) * bit
        j //= radix
    return xor


class Queue:
    def __init__(self):
        self.results = []

    def send(self, move, value):
        if len(self.results) >= 2:
            value = after(value, self.results[-2])
        self.results.append(move(value))
        return self.results[-1]


def call(kernel, name, shapes, args, in_specs=None, out_specs=None, scratch=(), flops=0, moved=2**20, **more):
    return pl.pallas_call(
        kernel,
        name=name,
        out_shape=[jax.ShapeDtypeStruct(shape, dtype) for shape, dtype in shapes],
        in_specs=in_specs or [VMEM] * len(args),
        out_specs=out_specs or [VMEM] * len(shapes),
        scratch_shapes=list(scratch),
        compiler_params=PARAMS,
        cost_estimate=pl.CostEstimate(flops=flops, bytes_accessed=moved, transcendentals=0),
        **more,
    )(*args)


def make_per_device(n):
    lay = Layout(n)
    sides, members, ring, rounds = lay.sides, lay.members, lay.ring, lay.rounds
    swap, onward = lay.swap, lay.onward

    def per_device(activations, key_grad, proj_basis, master_weight, first_moment, second_moment):
        tokens, width = activations.shape
        rows, rank = proj_basis.shape
        outs = key_grad.shape[1]
        owned = rank // n
        parts = 2 if rows % 256 == 0 else 1
        height = rows // parts
        z_queue, y_queue = Queue(), Queue()

        def swap_side(value):
            return y_queue.send(lambda v: swap(v, 2), value)

        def go_on(value):
            return z_queue.send(onward, value)

        plan = [(0, 0, ring), (1, 0, ring)]
        for x in range(2, members):
            plan += [(x, 0, ring // 2), (x, ring // 2, ring // 2)]
        cut = call(
            functools.partial(cut_kernel, lay, rows, plan),
            "cut",
            [((tokens, count * rows), bf16) for x, first, count in plan],
            [activations],
            in_specs=[HBM],
            scratch=[pltpu.SemaphoreType.DMA((members * ring,))],
            moved=4 * tokens * ring * rows * members,
        )

        weight = master_weight.astype(bf16)
        basis = [proj_basis]
        mine = [[weight[p * height : (p + 1) * height] for p in range(parts)]]
        mine += [[None] * parts for s in range(1, ring)]
        far_grad = swap_side(key_grad) if sides == 2 else None
        sends = []
        for s in range(1, ring):
            sends.append((s, None))
            if s <= parts:
                sends.append((1, s - 1))
        sends += [(s, p) for s in range(2, ring) for p in range(parts)]
        early = [send for send in sends if send[1] is None or send[0] <= 2]
        for s, p in early:
            if p is None:
                basis.append(go_on(basis[-1]))
            else:
                mine[s][p] = go_on(mine[s - 1][p])

        acts = list(cut)
        for k, (x, first, count) in enumerate(plan):
            if x >= 2:
                swap_x = functools.partial(swap, bit=x)
                acts[k] = y_queue.send(swap_x, cut[k])
        acts[1] = swap(after(cut[1], basis[1]), 1)
        if sides == 2:
            near = swap(jnp.concatenate([key_grad, after(far_grad, basis[1])], axis=0), 1)
            grads = [key_grad, near[:tokens], far_grad, near[tokens:]]
        else:
            grads = [key_grad, swap(key_grad, 1)]

        side_grads = [key_grad, far_grad] if sides == 2 else [key_grad]
        state = {"out": None, "waiting": None}

        def multiply(s, group, gate=None):
            low = group[0] * height
            wide = len(group) * height
            args = [mine[s][p] for p in group] + [swap(mine[s][p], 1) for p in group] + side_grads
            if gate is not None:
                args[0] = after(args[0], gate)
            in_specs = [VMEM] * len(args)
            came = None
            if state["waiting"] is not None:
                came = state["waiting"][:2]
                args.append(state["waiting"][2])
                in_specs.append(VMEM)
            first = state["out"] is None
            if not first:
                args.append(state["out"])
                in_specs.append(HBM)
            shapes, out_specs = [((tokens, width), bf16)], [HBM]
            if sides == 2:
                shapes.append(((tokens, 2 * wide), bf16))
                out_specs.append(VMEM)
            result = call(
                functools.partial(weight_kernel, lay, rows, s, low, len(group), came, first),
                "weight",
                shapes,
                args,
                in_specs,
                out_specs,
                scratch=[
                    pltpu.VMEM((tokens, 2 * wide), bf16),
                    pltpu.SemaphoreType.DMA((2,)),
                    pltpu.SemaphoreType.DMA((2,)),
                ],
                flops=4 * sides * tokens * wide * outs,
                moved=6 * 2**20,
                input_output_aliases={} if first else {len(args) - 1: 0},
            )
            state["out"] = result[0]
            state["waiting"] = None
            return result[1] if sides == 2 else None

        def give_back(s, group, block, gate=None):
            if sides == 2:
                if gate is not None:
                    block = after(block, gate)
                state["waiting"] = (s, group[0] * height, swap_side(block))

        everything = list(range(parts))
        block = multiply(0, everything)
        give_back(0, everything, block)
        block = multiply(1, everything)

        total, *gives = call(
            functools.partial(project_kernel, lay, owned, plan),
            "project",
            [((n // 2, owned, outs), f32), ((n // 2, owned, outs), bf16)],
            [after(acts[0], state["out"])] + acts[1:] + basis + grads,
            scratch=[pltpu.VMEM((rank, outs), f32)],
            flops=2 * tokens * members * rank * (ring * rows + outs),
            moved=12 * 2**20,
        )

        for k, (bit, radix) in enumerate(rounds):
            if bit == members:
                gives = [after(give, mine[2][0]) for give in gives]
            came = [swap(give, j * bit) for j, give in zip(range(1, radix), gives)]
            if k == len(rounds) - 1:
                break
            next_bit, next_radix = rounds[k + 1]
            shape = (total.shape[0] // next_radix, owned, outs)
            total, *gives = call(
                functools.partial(fold_kernel, next_bit, next_radix, len(came)),
                "fold",
                [(shape, f32)] + [(shape, bf16)] * (next_radix - 1),
                [total] + came,
                moved=4 * total.size,
            )
            if bit == 2 and sides == 2:
                give_back(1, everything, block, total)
        owned_rows, square = call(
            functools.partial(square_kernel, len(came)),
            "square",
            [((owned, outs), f32), ((8, 128), f32)],
            [total] + came,
        )
        for bit, radix in reversed(rounds):
            if bit >= members:
                square = sum([swap(square, j * bit) for j in range(1, radix)], square)
        squares = [square] + [swap(square, x) for x in range(1, members)]
        if sides == 1:
            give_back(1, everything, block)
        for s, p in sends:
            if (s, p) not in early and p == 0 and s == 3:
                mine[s][p] = go_on(after(mine[s - 1][p], square))
        if ring > 2:
            block = multiply(2, everything, square)
        new_first, new_second, update = call(
            functools.partial(moment_kernel, members),
            "moment",
            [((owned, outs), f32), ((owned, outs), f32), ((1, owned, outs), bf16)],
            squares + [owned_rows, first_moment, second_moment],
        )
        if ring > 2:
            give_back(2, everything, block, squares[-1])
        for s, p in sends:
            if p is not None and mine[s][p] is None:
                mine[s][p] = go_on(after(mine[s - 1][p], update))

        whole = update
        for bit, radix in reversed(rounds[1:]):
            whole = jnp.concatenate(
                [whole] + [swap(whole, j * bit) for j in range(1, radix)], axis=0
            )
        (new_master,) = call(
            functools.partial(back_kernel, lay, owned),
            "back",
            [(master_weight.shape, f32)],
            [proj_basis, whole, swap(whole, 1), master_weight],
            scratch=[pltpu.VMEM((rank, outs), f32)],
            flops=2 * rows * rank * outs,
            moved=8 * 2**20,
        )

        for s in range(3, ring):
            groups = [everything] if s < ring - 1 else [[p] for p in everything]
            for group in groups:
                block = multiply(s, group)
                give_back(s, group, block, whole if s == 3 and group[0] == 0 else None)
        activation_grad = state["out"]
        if state["waiting"] is not None:
            s, low, arrived = state["waiting"]
            (activation_grad,) = call(
                functools.partial(last_kernel, lay, rows, s, low),
                "last",
                [((tokens, width), bf16)],
                [arrived, activation_grad],
                [VMEM, HBM],
                [HBM],
                scratch=[pltpu.SemaphoreType.DMA((2,))],
                input_output_aliases={1: 0},
            )
        return (activation_grad, new_master, new_first, new_second)

    return per_device


def solution(mesh):
    spec = P(("groups", "dp"), None)
    return jax.shard_map(
        make_per_device(mesh.shape["dp"]),
        mesh=mesh,
        in_specs=(spec,) * 6,
        out_specs=(spec,) * 4,
        check_vma=False,
    )
```

```python
import functools
import jax
import jax.numpy as jnp
from jax import lax
from jax.experimental import pallas as pl
from jax.experimental.pallas import tpu as pltpu
from jax.sharding import PartitionSpec as P

clip_total = 512.0
step_size = 0.01
first_fix = 1.0 - 0.9**10
second_fix = 1.0 - 0.99**10

f32 = jnp.float32
bf16 = jnp.bfloat16
HBM = pl.BlockSpec(memory_space=pl.ANY)
VMEM = pl.BlockSpec(memory_space=pltpu.VMEM)
PARAMS = pltpu.CompilerParams(vmem_limit_bytes=40 * 2**20)


def after(value, *others):
    return lax.optimization_barrier((value,) + others)[0]


class Layout:
    def __init__(self, n):
        self.n = n
        self.sides = 2 if n == 16 else 1
        self.members = 2 * self.sides
        self.ring = n // self.members
        ring, members = self.ring, self.members
        order = [0, 1, 3, 2] if ring == 4 else list(range(ring))
        self.forward = [
            (order[k] * members + m, order[(k + 1) % ring] * members + m)
            for k in range(ring)
            for m in range(members)
        ]
        self.rounds = [(1, 2)]
        bit = 2
        if self.sides == 2:
            self.rounds.append((2, 2))
            bit = 4
        while bit < n:
            radix = 4 if 2 * bit < n else 2
            self.rounds.append((bit, radix))
            bit *= radix

    def swap(self, value, bit):
        return lax.ppermute(value, "dp", [(i, i ^ bit) for i in range(self.n)])

    def onward(self, value):
        return lax.ppermute(value, "dp", self.forward)

    def source(self, index, s):
        z = index // self.members
        if self.ring != 4:
            return (z - s + self.ring) % self.ring
        k = (z + z // 2 * (5 - 2 * z) - s + 4) % 4
        return k + k // 2 * (5 - 2 * k)


def flip(value, bit):
    return value + bit - 2 * bit * ((value // bit) % 2)


def cut_kernel(lay, rows, plan, act, *refs):
    pieces, sems = refs[:-1], refs[-1]
    index = lax.axis_index("dp")
    member = index % lay.members
    copies = []
    for (x, first, count), piece in zip(plan, pieces):
        owner = member
        for bit in (1, 2):
            if x & bit:
                owner = flip(owner, bit)
        for s in range(first, first + count):
            start = pl.multiple_of((lay.source(index, s) * lay.members + owner) * rows, rows)
            copies.append(
                pltpu.make_async_copy(
                    act.at[:, pl.ds(start, rows)],
                    piece.at[:, pl.ds((s - first) * rows, rows)],
                    sems.at[len(copies)],
                )
            )
    for copy in copies:
        copy.start()
    for copy in copies:
        copy.wait()


def project_kernel(lay, owned, plan, *refs):
    members, ring = lay.members, lay.ring
    acts, refs = refs[: len(plan)], refs[len(plan) :]
    basis, refs = refs[:ring], refs[ring:]
    grads, refs = refs[:members], refs[members:]
    kept, given, grad = refs
    rows = basis[0].shape[0]
    core = lax.axis_index("dp") % 2
    for x in range(members):
        total = None
        for (x_, first, count), piece in zip(plan, acts):
            if x_ != x:
                continue
            for s in range(first, first + count):
                term = jnp.dot(
                    piece[:, (s - first) * rows : (s - first + 1) * rows],
                    basis[s][...],
                    preferred_element_type=f32,
                )
                total = term if total is None else total + term
        term = lax.dot_general(
            total.astype(bf16),
            grads[x][...],
            (((0,), (0,)), ((), ())),
            preferred_element_type=f32,
        )
        if x == 0:
            grad[...] = term
        else:
            grad[...] += term
    for i in range(lay.n // 2):
        kept[i] = grad[pl.ds(pl.multiple_of((2 * i + core) * owned, owned), owned), :]
        given[i] = grad[pl.ds(pl.multiple_of((2 * i + 1 - core) * owned, owned), owned), :].astype(bf16)


def fold_kernel(bit, radix, came, *refs):
    kept, arrived, outs = refs[0], refs[1 : 1 + came], refs[1 + came :]
    digit = (lax.axis_index("dp") // bit) % radix

    def block(i):
        total = kept[i]
        for piece in arrived:
            total = total + piece[i].astype(f32)
        return total

    for i in range(kept.shape[0] // radix):
        for j in range(radix):
            other = digit
            for b in (1, 2):
                if j & b:
                    other = flip(other, b)
            value = block(i * radix + other)
            outs[j][i] = value.astype(outs[j].dtype)


def square_kernel(came, *refs):
    kept, arrived, (owned, square) = refs[0], refs[1 : 1 + came], refs[1 + came :]
    total = kept[0]
    for piece in arrived:
        total = total + piece[0].astype(f32)
    owned[...] = total
    square[...] = jnp.full(square.shape, jnp.sum(total * total), f32)


def moment_kernel(count, *refs):
    squares, (owned, first, second, new_first, new_second, update) = refs[:count], refs[count:]
    total = squares[0][...]
    for square in squares[1:]:
        total = total + square[...]
    factor = jnp.minimum(1.0, clip_total / (jnp.sqrt(total) + 1e-06))[0:1, 0:1]
    clipped = owned[...] * factor
    one = 0.9 * first[...] + 0.1 * clipped
    two = 0.99 * second[...] + 0.01 * clipped * clipped
    new_first[...] = one
    new_second[...] = two
    update[0] = (one / first_fix / (jnp.sqrt(two / second_fix) + 1e-08)).astype(bf16)


def place(lay, side, rows, low, source, out, sems):
    height = source.shape[1] // (2 * lay.ring)
    copies = []
    for z in range(lay.ring):
        for core in range(2):
            k = 2 * z + core
            start = pl.multiple_of(((z * lay.sides + side) * 2 + core) * rows + low, height)
            copies.append(
                pltpu.make_async_copy(
                    source.at[:, pl.ds(k * height, height)],
                    out.at[:, pl.ds(start, height)],
                    sems.at[k],
                )
            )
    return copies


def weight_kernel(lay, rows, low, came, first, *refs):
    sides = lay.sides
    weight, grads, refs = refs[0], refs[1 : 1 + sides], refs[1 + sides :]
    if came is not None:
        arrived, refs = refs[0], refs[1:]
    if not first:
        refs = refs[1:]
    out, refs = refs[0], refs[1:]
    if sides == 2:
        far, refs = refs[0], refs[1:]
    own, sems, came_sems = refs
    side = (lax.axis_index("dp") // 2) % sides
    copies = []
    if came is not None:
        copies = place(lay, 1 - side, rows, came, arrived, out, came_sems)
        for copy in copies:
            copy.start()
    for x in reversed(range(sides)):
        target = own if x == 0 else far
        target[...] = lax.dot_general(
            grads[x][...], weight[...], (((1,), (1,)), ((), ())), preferred_element_type=f32
        ).astype(bf16)
    owns = place(lay, side, rows, low, own, out, sems)
    for copy in owns:
        copy.start()
    for copy in owns + copies:
        copy.wait()


def last_kernel(lay, rows, low, arrived, before, out, sems):
    side = (lax.axis_index("dp") // 2) % lay.sides
    copies = place(lay, 1 - side, rows, low, arrived, out, sems)
    for copy in copies:
        copy.start()
    for copy in copies:
        copy.wait()


def back_kernel(lay, owned, basis, near, other, master, out, update):
    index = lax.axis_index("dp")
    half = lay.n // 2
    for j in range(lay.n):
        owner = index
        for bit in [1 << b for b in range(lay.n.bit_length() - 1)]:
            if slot_to_xor(lay, j) & bit:
                owner = flip(owner, bit)
        piece = near[j] if j < half else other[j - half]
        update[pl.ds(pl.multiple_of(owner * owned, owned), owned), :] = piece.astype(f32)
    out[...] = master[...] - step_size * jnp.dot(
        basis[...], update[...].astype(bf16), preferred_element_type=f32
    )


def slot_to_xor(lay, j):
    xor = 0
    for bit, radix in reversed(lay.rounds):
        xor += (j % radix) * bit
        j //= radix
    return xor


def call(kernel, name, shapes, args, in_specs=None, out_specs=None, scratch=(), flops=0, moved=2**20, **more):
    return pl.pallas_call(
        kernel,
        name=name,
        out_shape=[jax.ShapeDtypeStruct(shape, dtype) for shape, dtype in shapes],
        in_specs=in_specs or [VMEM] * len(args),
        out_specs=out_specs or [VMEM] * len(shapes),
        scratch_shapes=list(scratch),
        compiler_params=PARAMS,
        cost_estimate=pl.CostEstimate(flops=flops, bytes_accessed=moved, transcendentals=0),
        **more,
    )(*args)


def make_per_device(n):
    lay = Layout(n)
    sides, members, ring, rounds = lay.sides, lay.members, lay.ring, lay.rounds
    swap, onward = lay.swap, lay.onward

    def per_device(activations, key_grad, proj_basis, master_weight, first_moment, second_moment):
        tokens, width = activations.shape
        rows, rank = proj_basis.shape
        outs = key_grad.shape[1]
        owned = rank // n
        height = 128 if rows % 128 == 0 else rows
        parts = rows // height

        plan = [(x, 0, ring) for x in range(min(members, 3))]
        if sides == 2:
            plan += [(3, 0, ring // 2), (3, ring // 2, ring // 2)]
        cut = call(
            functools.partial(cut_kernel, lay, rows, plan),
            "cut",
            [((tokens, count * rows), bf16) for x, first, count in plan],
            [activations],
            in_specs=[HBM],
            scratch=[pltpu.SemaphoreType.DMA((members * ring,))],
            moved=4 * tokens * ring * rows * members,
        )

        basis = [after(proj_basis, cut[0])]
        acts = list(cut)
        if sides == 2:
            far_grad = swap(key_grad, 2)
            acts[2] = swap(cut[2], 2)
            acts[3] = swap(after(cut[3], far_grad), 3)
            acts[4] = swap(after(cut[4], acts[2]), 3)
        for s in range(1, ring):
            value = basis[-1]
            if s == 2 and sides == 2:
                value = after(value, far_grad)
            basis.append(onward(value))
        acts[1] = swap(after(cut[1], basis[1]), 1)
        if sides == 2:
            near = swap(jnp.concatenate([key_grad, far_grad], axis=0), 1)
            grads = [key_grad, near[:tokens], far_grad, near[tokens:]]
        else:
            grads = [key_grad, swap(key_grad, 1)]

        weight = master_weight.astype(bf16)
        groups = None
        if sides == 2:
            groups = [
                [(z * sides + side) * 2 + core for z in range(ring) for core in range(2)]
                for side in range(sides)
            ]
        chunks = []
        for p in range(parts):
            chunk = weight[p * height : (p + 1) * height]
            if p > 0:
                chunk = after(chunk, basis[min(p + 1, ring - 1)], acts[p + 1])
            chunks.append(
                lax.all_gather(chunk, "dp", axis=0, tiled=True, axis_index_groups=groups)
            )

        side_grads = [key_grad, far_grad] if sides == 2 else [key_grad]
        state = {"out": None, "waiting": None}
        wide = 2 * ring * height

        def multiply(p, gate=None):
            args = [chunks[p] if gate is None else after(chunks[p], gate)] + side_grads
            in_specs = [VMEM] * len(args)
            came = None
            if state["waiting"] is not None:
                came = state["waiting"][0]
                args.append(state["waiting"][1])
                in_specs.append(VMEM)
            first = state["out"] is None
            if not first:
                args.append(state["out"])
                in_specs.append(HBM)
            shapes, out_specs = [((tokens, width), bf16)], [HBM]
            if sides == 2:
                shapes.append(((tokens, wide), bf16))
                out_specs.append(VMEM)
            result = call(
                functools.partial(weight_kernel, lay, rows, p * height, came, first),
                "weight",
                shapes,
                args,
                in_specs,
                out_specs,
                scratch=[
                    pltpu.VMEM((tokens, wide), bf16),
                    pltpu.SemaphoreType.DMA((2 * ring,)),
                    pltpu.SemaphoreType.DMA((2 * ring,)),
                ],
                flops=2 * sides * tokens * wide * outs,
                moved=6 * 2**20,
                input_output_aliases={} if first else {len(args) - 1: 0},
            )
            state["out"] = result[0]
            state["waiting"] = None
            return result[1] if sides == 2 else None

        def give_back(p, block, gate=None):
            if sides == 2:
                if gate is not None:
                    block = after(block, gate)
                state["waiting"] = (p * height, swap(block, 2))

        block = multiply(0)
        give_back(0, block, acts[-1])

        total, *gives = call(
            functools.partial(project_kernel, lay, owned, plan),
            "project",
            [((n // 2, owned, outs), f32), ((n // 2, owned, outs), bf16)],
            [after(acts[0], block if sides == 2 else acts[0])] + acts[1:] + basis + grads,
            scratch=[pltpu.VMEM((rank, outs), f32)],
            flops=2 * tokens * members * rank * (ring * rows + outs),
            moved=12 * 2**20,
        )

        for k, (bit, radix) in enumerate(rounds):
            came = [swap(give, j * bit) for j, give in zip(range(1, radix), gives)]
            if k == len(rounds) - 1:
                break
            next_bit, next_radix = rounds[k + 1]
            shape = (total.shape[0] // next_radix, owned, outs)
            total, *gives = call(
                functools.partial(fold_kernel, next_bit, next_radix, len(came)),
                "fold",
                [(shape, f32)] + [(shape, bf16)] * (next_radix - 1),
                [total] + came,
                moved=4 * total.size,
            )
        if parts > 1:
            block = multiply(1, total)
            give_back(1, block)
        owned_rows, square = call(
            functools.partial(square_kernel, len(came)),
            "square",
            [((owned, outs), f32), ((8, 128), f32)],
            [total] + came,
        )
        for bit, radix in reversed(rounds):
            if bit >= members:
                square = sum([swap(square, j * bit) for j in range(1, radix)], square)
        squares = [square] + [swap(square, x) for x in range(1, members)]
        new_first, new_second, update = call(
            functools.partial(moment_kernel, members),
            "moment",
            [((owned, outs), f32), ((owned, outs), f32), ((1, owned, outs), bf16)],
            squares + [owned_rows, first_moment, second_moment],
        )
        if parts > 2:
            block = multiply(2, update)
            give_back(2, block)

        whole = update
        for bit, radix in reversed(rounds[1:]):
            whole = jnp.concatenate(
                [whole] + [swap(whole, j * bit) for j in range(1, radix)], axis=0
            )
        (new_master,) = call(
            functools.partial(back_kernel, lay, owned),
            "back",
            [(master_weight.shape, f32)],
            [proj_basis, whole, swap(whole, 1), master_weight],
            scratch=[pltpu.VMEM((rank, outs), f32)],
            flops=2 * rows * rank * outs,
            moved=8 * 2**20,
        )

        for p in range(3, parts):
            block = multiply(p, whole)
            give_back(p, block)
        activation_grad = state["out"]
        if state["waiting"] is not None:
            low, arrived = state["waiting"]
            (activation_grad,) = call(
                functools.partial(last_kernel, lay, rows, low),
                "last",
                [((tokens, width), bf16)],
                [arrived, activation_grad],
                [VMEM, HBM],
                [HBM],
                scratch=[pltpu.SemaphoreType.DMA((2 * ring,))],
                input_output_aliases={1: 0},
            )
        return (activation_grad, new_master, new_first, new_second)

    return per_device


def solution(mesh):
    spec = P(("groups", "dp"), None)
    return jax.shard_map(
        make_per_device(mesh.shape["dp"]),
        mesh=mesh,
        in_specs=(spec,) * 6,
        out_specs=(spec,) * 4,
        check_vma=False,
    )
```

```python
import functools
import jax
import jax.numpy as jnp
from jax import lax
from jax.experimental import pallas as pl
from jax.experimental.pallas import tpu as pltpu
from jax.sharding import PartitionSpec as P

clip_total = 512.0
step_size = 0.01
first_fix = 1.0 - 0.9**10
second_fix = 1.0 - 0.99**10

f32 = jnp.float32
bf16 = jnp.bfloat16
HBM = pl.BlockSpec(memory_space=pl.ANY)
VMEM = pl.BlockSpec(memory_space=pltpu.VMEM)
PARAMS = pltpu.CompilerParams(vmem_limit_bytes=40 * 2**20)


def after(value, *others):
    return lax.optimization_barrier((value,) + others)[0]


class Layout:
    def __init__(self, n):
        self.n = n
        self.sides = 2 if n == 16 else 1
        self.members = 2 * self.sides
        self.ring = n // self.members
        ring, members = self.ring, self.members
        order = [0, 1, 3, 2] if ring == 4 else list(range(ring))
        self.forward = [
            (order[k] * members + m, order[(k + 1) % ring] * members + m)
            for k in range(ring)
            for m in range(members)
        ]
        self.rounds = [(1, 2)]
        bit = 2
        if self.sides == 2:
            self.rounds.append((2, 2))
            bit = 4
        while bit < n:
            radix = 4 if 2 * bit < n else 2
            self.rounds.append((bit, radix))
            bit *= radix

    def swap(self, value, bit):
        return lax.ppermute(value, "dp", [(i, i ^ bit) for i in range(self.n)])

    def onward(self, value):
        return lax.ppermute(value, "dp", self.forward)

    def source(self, index, s):
        z = index // self.members
        if self.ring != 4:
            return (z - s + self.ring) % self.ring
        k = (z + z // 2 * (5 - 2 * z) - s + 4) % 4
        return k + k // 2 * (5 - 2 * k)


def flip(value, bit):
    return value + bit - 2 * bit * ((value // bit) % 2)


def cut_kernel(lay, rows, plan, act, *refs):
    pieces, sems = refs[:-1], refs[-1]
    index = lax.axis_index("dp")
    member = index % lay.members
    copies = []
    for (x, first, count), piece in zip(plan, pieces):
        owner = member
        for bit in (1, 2):
            if x & bit:
                owner = flip(owner, bit)
        for s in range(first, first + count):
            start = pl.multiple_of((lay.source(index, s) * lay.members + owner) * rows, rows)
            copies.append(
                pltpu.make_async_copy(
                    act.at[:, pl.ds(start, rows)],
                    piece.at[:, pl.ds((s - first) * rows, rows)],
                    sems.at[len(copies)],
                )
            )
    for copy in copies:
        copy.start()
    for copy in copies:
        copy.wait()


def project_kernel(lay, owned, plan, *refs):
    members, ring = lay.members, lay.ring
    acts, refs = refs[: len(plan)], refs[len(plan) :]
    basis, refs = refs[:ring], refs[ring:]
    grads, refs = refs[:members], refs[members:]
    kept, given, grad = refs
    rows = basis[0].shape[0]
    core = lax.axis_index("dp") % 2
    for x in range(members):
        total = None
        for (x_, first, count), piece in zip(plan, acts):
            if x_ != x:
                continue
            for s in range(first, first + count):
                term = jnp.dot(
                    piece[:, (s - first) * rows : (s - first + 1) * rows],
                    basis[s][...],
                    preferred_element_type=f32,
                )
                total = term if total is None else total + term
        term = lax.dot_general(
            total.astype(bf16),
            grads[x][...],
            (((0,), (0,)), ((), ())),
            preferred_element_type=f32,
        )
        if x == 0:
            grad[...] = term
        else:
            grad[...] += term
    for i in range(lay.n // 2):
        kept[i] = grad[pl.ds(pl.multiple_of((2 * i + core) * owned, owned), owned), :]
        given[i] = grad[pl.ds(pl.multiple_of((2 * i + 1 - core) * owned, owned), owned), :].astype(bf16)


def fold_kernel(bit, radix, came, *refs):
    kept, arrived, outs = refs[0], refs[1 : 1 + came], refs[1 + came :]
    digit = (lax.axis_index("dp") // bit) % radix

    def block(i):
        total = kept[i]
        for piece in arrived:
            total = total + piece[i].astype(f32)
        return total

    for i in range(kept.shape[0] // radix):
        for j in range(radix):
            other = digit
            for b in (1, 2):
                if j & b:
                    other = flip(other, b)
            value = block(i * radix + other)
            outs[j][i] = value.astype(outs[j].dtype)


def square_kernel(came, *refs):
    kept, arrived, (owned, square) = refs[0], refs[1 : 1 + came], refs[1 + came :]
    total = kept[0]
    for piece in arrived:
        total = total + piece[0].astype(f32)
    owned[...] = total
    square[...] = jnp.full(square.shape, jnp.sum(total * total), f32)


def moment_kernel(count, *refs):
    squares, (owned, first, second, new_first, new_second, update) = refs[:count], refs[count:]
    total = squares[0][...]
    for square in squares[1:]:
        total = total + square[...]
    factor = jnp.minimum(1.0, clip_total / (jnp.sqrt(total) + 1e-06))[0:1, 0:1]
    clipped = owned[...] * factor
    one = 0.9 * first[...] + 0.1 * clipped
    two = 0.99 * second[...] + 0.01 * clipped * clipped
    new_first[...] = one
    new_second[...] = two
    update[0] = (one / first_fix / (jnp.sqrt(two / second_fix) + 1e-08)).astype(bf16)


def place(lay, s, side, rows, source, out, sems):
    index = lax.axis_index("dp")
    core = index % 2
    chip = lay.source(index, s) * lay.sides + side
    copies = []
    for k, owner in enumerate((core, 1 - core)):
        start = pl.multiple_of((chip * 2 + owner) * rows, rows)
        copies.append(
            pltpu.make_async_copy(
                source.at[:, pl.ds(k * rows, rows)],
                out.at[:, pl.ds(start, rows)],
                sems.at[k],
            )
        )
    return copies


def weight_kernel(lay, rows, s, came, first, *refs):
    sides = lay.sides
    mine, theirs, grads, refs = refs[0], refs[1], refs[2 : 2 + sides], refs[2 + sides :]
    if came is not None:
        arrived, refs = refs[0], refs[1:]
    if not first:
        refs = refs[1:]
    out, refs = refs[0], refs[1:]
    if sides == 2:
        far, refs = refs[0], refs[1:]
    own, sems, came_sems = refs
    side = (lax.axis_index("dp") // 2) % sides
    copies = []
    if came is not None:
        copies = place(lay, came, 1 - side, rows, arrived, out, came_sems)
        for copy in copies:
            copy.start()
    for x in reversed(range(sides)):
        target = own if x == 0 else far
        for k, piece in enumerate((mine, theirs)):
            target[:, k * rows : (k + 1) * rows] = lax.dot_general(
                grads[x][...],
                piece[...],
                (((1,), (1,)), ((), ())),
                preferred_element_type=f32,
            ).astype(bf16)
    owns = place(lay, s, side, rows, own, out, sems)
    for copy in owns:
        copy.start()
    for copy in owns + copies:
        copy.wait()


def last_kernel(lay, rows, steps, *refs):
    arrived, (before, out, sems) = refs[: len(steps)], refs[len(steps) :]
    side = (lax.axis_index("dp") // 2) % lay.sides
    copies = []
    for k, s in enumerate(steps):
        copies += place(lay, s, 1 - side, rows, arrived[k], out, sems.at[k])
    for copy in copies:
        copy.start()
    for copy in copies:
        copy.wait()


def back_kernel(lay, owned, basis, near, other, master, out, update):
    index = lax.axis_index("dp")
    half = lay.n // 2
    for j in range(lay.n):
        owner = index
        for bit in [1 << b for b in range(lay.n.bit_length() - 1)]:
            if slot_to_xor(lay, j) & bit:
                owner = flip(owner, bit)
        piece = near[j] if j < half else other[j - half]
        update[pl.ds(pl.multiple_of(owner * owned, owned), owned), :] = piece.astype(f32)
    out[...] = master[...] - step_size * jnp.dot(
        basis[...], update[...].astype(bf16), preferred_element_type=f32
    )


def slot_to_xor(lay, j):
    xor = 0
    for bit, radix in reversed(lay.rounds):
        xor += (j % radix) * bit
        j //= radix
    return xor


def call(kernel, name, shapes, args, in_specs=None, out_specs=None, scratch=(), flops=0, moved=2**20, **more):
    return pl.pallas_call(
        kernel,
        name=name,
        out_shape=[jax.ShapeDtypeStruct(shape, dtype) for shape, dtype in shapes],
        in_specs=in_specs or [VMEM] * len(args),
        out_specs=out_specs or [VMEM] * len(shapes),
        scratch_shapes=list(scratch),
        compiler_params=PARAMS,
        cost_estimate=pl.CostEstimate(flops=flops, bytes_accessed=moved, transcendentals=0),
        **more,
    )(*args)


def make_per_device(n):
    lay = Layout(n)
    sides, members, ring, rounds = lay.sides, lay.members, lay.ring, lay.rounds
    swap, onward = lay.swap, lay.onward

    def per_device(activations, key_grad, proj_basis, master_weight, first_moment, second_moment):
        tokens, width = activations.shape
        rows, rank = proj_basis.shape
        outs = key_grad.shape[1]
        owned = rank // n

        plan = [(x, 0, ring) for x in range(min(members, 3))]
        if sides == 2:
            plan += [(3, 0, ring // 2), (3, ring // 2, ring // 2)]
        cut = call(
            functools.partial(cut_kernel, lay, rows, plan),
            "cut",
            [((tokens, count * rows), bf16) for x, first, count in plan],
            [activations],
            in_specs=[HBM],
            scratch=[pltpu.SemaphoreType.DMA((members * ring,))],
            moved=4 * tokens * ring * rows * members,
        )

        acts = list(cut)
        far_grad = None
        if sides == 2:
            far_grad = swap(key_grad, 2)
            acts[2] = swap(cut[2], 2)
            acts[3] = swap(after(cut[3], far_grad), 3)
            acts[4] = swap(after(cut[4], acts[2]), 3)
        weight = [master_weight.astype(bf16)]
        basis = [after(proj_basis, cut[0])]
        for s in range(1, ring):
            value = basis[-1]
            if s == 2 and sides == 2:
                value = after(value, far_grad)
            if s == 3:
                value = after(value, weight[1])
            basis.append(onward(value))
            if s == 1:
                weight.append(onward(weight[0]))
        acts[1] = swap(after(cut[1], basis[1]), 1)
        if sides == 2:
            near = swap(jnp.concatenate([key_grad, far_grad], axis=0), 1)
            grads = [key_grad, near[:tokens], far_grad, near[tokens:]]
        else:
            grads = [key_grad, swap(key_grad, 1)]
        weight.append(onward(after(weight[1], basis[-1])))

        side_grads = [key_grad, far_grad] if sides == 2 else [key_grad]
        state = {"out": None}
        waiting = []

        def multiply(s, gate=None):
            args = [weight[s] if gate is None else after(weight[s], gate), swap(weight[s], 1)]
            args += side_grads
            in_specs = [VMEM] * len(args)
            came = None
            if len(waiting) > 1:
                came, block = waiting.pop(0)
                args.append(block)
                in_specs.append(VMEM)
            first = state["out"] is None
            if not first:
                args.append(state["out"])
                in_specs.append(HBM)
            shapes, out_specs = [((tokens, width), bf16)], [HBM]
            if sides == 2:
                shapes.append(((tokens, 2 * rows), bf16))
                out_specs.append(VMEM)
            result = call(
                functools.partial(weight_kernel, lay, rows, s, came, first),
                "weight",
                shapes,
                args,
                in_specs,
                out_specs,
                scratch=[
                    pltpu.VMEM((tokens, 2 * rows), bf16),
                    pltpu.SemaphoreType.DMA((2,)),
                    pltpu.SemaphoreType.DMA((2,)),
                ],
                flops=4 * sides * tokens * rows * outs,
                moved=6 * 2**20,
                input_output_aliases={} if first else {len(args) - 1: 0},
            )
            state["out"] = result[0]
            return result[1] if sides == 2 else result[0]

        def give_back(s, block, *gates):
            if sides == 1:
                return block
            waiting.append((s, swap(after(block, *gates) if gates else block, 2)))
            return waiting[-1][1]

        first_block = multiply(0)

        total, *gives = call(
            functools.partial(project_kernel, lay, owned, plan),
            "project",
            [((n // 2, owned, outs), f32), ((n // 2, owned, outs), bf16)],
            [after(acts[0], first_block)] + acts[1:] + basis + grads,
            scratch=[pltpu.VMEM((rank, outs), f32)],
            flops=2 * tokens * members * rank * (ring * rows + outs),
            moved=12 * 2**20,
        )

        for k, (bit, radix) in enumerate(rounds):
            if bit == members:
                gives = [after(give, weight[2], block) for give in gives]
            came = [swap(give, j * bit) for j, give in zip(range(1, radix), gives)]
            if k == len(rounds) - 1:
                break
            next_bit, next_radix = rounds[k + 1]
            shape = (total.shape[0] // next_radix, owned, outs)
            total, *gives = call(
                functools.partial(fold_kernel, next_bit, next_radix, len(came)),
                "fold",
                [(shape, f32)] + [(shape, bf16)] * (next_radix - 1),
                [total] + came,
                moved=4 * total.size,
            )
            if bit == 1:
                block = multiply(1, total)
            if bit == 2:
                sent = give_back(0, first_block, total)
                later = give_back(1, block, total)
        owned_rows, square = call(
            functools.partial(square_kernel, len(came)),
            "square",
            [((owned, outs), f32), ((8, 128), f32)],
            [total] + came,
        )
        square = after(square, sent)
        for bit, radix in reversed(rounds):
            if bit >= members:
                square = sum([swap(square, j * bit) for j in range(1, radix)], square)
        if ring > 3:
            weight.append(onward(after(weight[2], square)))
        block = multiply(2, owned_rows)
        square = after(square, later)
        squares = [square] + [swap(square, x) for x in range(1, members)]
        new_first, new_second, update = call(
            functools.partial(moment_kernel, members),
            "moment",
            [((owned, outs), f32), ((owned, outs), f32), ((1, owned, outs), bf16)],
            squares + [after(owned_rows, block), first_moment, second_moment],
        )
        sent = give_back(2, block, update)
        if ring > 3:
            weight[3] = after(weight[3], update)

        whole = update
        for bit, radix in reversed(rounds[1:]):
            if bit >= members and 2 * bit >= n // 2 and ring > 3:
                whole = after(whole, weight[3])
            if bit == 2 and sides == 2:
                whole = after(whole, sent)
            whole = jnp.concatenate(
                [whole] + [swap(whole, j * bit) for j in range(1, radix)], axis=0
            )
        (new_master,) = call(
            functools.partial(back_kernel, lay, owned),
            "back",
            [(master_weight.shape, f32)],
            [proj_basis, whole, swap(whole, 1), master_weight],
            scratch=[pltpu.VMEM((rank, outs), f32)],
            flops=2 * rows * rank * outs,
            moved=8 * 2**20,
        )

        for s in range(3, ring):
            if s > 3:
                weight.append(onward(weight[s - 1]))
            give_back(s, multiply(s))
        activation_grad = state["out"]
        if waiting:
            (activation_grad,) = call(
                functools.partial(last_kernel, lay, rows, [s for s, block in waiting]),
                "last",
                [((tokens, width), bf16)],
                [block for s, block in waiting] + [activation_grad],
                [VMEM] * len(waiting) + [HBM],
                [HBM],
                scratch=[pltpu.SemaphoreType.DMA((len(waiting), 2))],
                input_output_aliases={len(waiting): 0},
            )
        return (activation_grad, new_master, new_first, new_second)

    return per_device


def solution(mesh):
    spec = P(("groups", "dp"), None)
    return jax.shard_map(
        make_per_device(mesh.shape["dp"]),
        mesh=mesh,
        in_specs=(spec,) * 6,
        out_specs=(spec,) * 4,
        check_vma=False,
    )
```

```python
import functools
import jax
import jax.numpy as jnp
from jax import lax
from jax.experimental import pallas as pl
from jax.experimental.pallas import tpu as pltpu
from jax.sharding import PartitionSpec as P

clip_total = 512.0
step_size = 0.01
first_fix = 1.0 - 0.9**10
second_fix = 1.0 - 0.99**10

f32 = jnp.float32
bf16 = jnp.bfloat16
HBM = pl.BlockSpec(memory_space=pl.ANY)
VMEM = pl.BlockSpec(memory_space=pltpu.VMEM)
PARAMS = pltpu.CompilerParams(vmem_limit_bytes=40 * 2**20)


def after(value, *others):
    return lax.optimization_barrier((value,) + others)[0]


class Layout:
    def __init__(self, n):
        self.n = n
        self.sides = 2 if n == 16 else 1
        self.members = 2 * self.sides
        self.ring = n // self.members
        ring, members = self.ring, self.members
        order = [0, 1, 3, 2] if ring == 4 else list(range(ring))
        self.forward = [
            (order[k] * members + m, order[(k + 1) % ring] * members + m)
            for k in range(ring)
            for m in range(members)
        ]
        self.rounds = [(1, 2)]
        bit = 2
        if self.sides == 2:
            self.rounds.append((2, 2))
            bit = 4
        while bit < n:
            radix = 4 if 2 * bit < n else 2
            self.rounds.append((bit, radix))
            bit *= radix

    def swap(self, value, bit):
        return lax.ppermute(value, "dp", [(i, i ^ bit) for i in range(self.n)])

    def onward(self, value):
        return lax.ppermute(value, "dp", self.forward)

    def source(self, index, s):
        z = index // self.members
        if self.ring != 4:
            return (z - s + self.ring) % self.ring
        k = (z + z // 2 * (5 - 2 * z) - s + 4) % 4
        return k + k // 2 * (5 - 2 * k)


def flip(value, bit):
    return value + bit - 2 * bit * ((value // bit) % 2)


def cut_kernel(lay, rows, plan, act, *refs):
    pieces, sems = refs[:-1], refs[-1]
    index = lax.axis_index("dp")
    member = index % lay.members
    copies = []
    for (x, first, count), piece in zip(plan, pieces):
        owner = member
        for bit in (1, 2):
            if x & bit:
                owner = flip(owner, bit)
        for s in range(first, first + count):
            start = pl.multiple_of((lay.source(index, s) * lay.members + owner) * rows, rows)
            copies.append(
                pltpu.make_async_copy(
                    act.at[:, pl.ds(start, rows)],
                    piece.at[:, pl.ds((s - first) * rows, rows)],
                    sems.at[len(copies)],
                )
            )
    for copy in copies:
        copy.start()
    for copy in copies:
        copy.wait()


def project_kernel(lay, owned, plan, *refs):
    members, ring = lay.members, lay.ring
    acts, refs = refs[: len(plan)], refs[len(plan) :]
    basis, refs = refs[:ring], refs[ring:]
    grads, refs = refs[:members], refs[members:]
    kept, given, grad = refs
    rows = acts[0].shape[1] // ring
    core = lax.axis_index("dp") % 2
    for x in range(members):
        total = None
        for (x_, first, count), piece in zip(plan, acts):
            if x_ != x:
                continue
            for s in range(first, first + count):
                term = jnp.dot(
                    piece[:, (s - first) * rows : (s - first + 1) * rows],
                    basis[s][:rows, :],
                    preferred_element_type=f32,
                )
                total = term if total is None else total + term
        term = lax.dot_general(
            total.astype(bf16),
            grads[x][...],
            (((0,), (0,)), ((), ())),
            preferred_element_type=f32,
        )
        if x == 0:
            grad[...] = term
        else:
            grad[...] += term
    for i in range(lay.n // 2):
        kept[i] = grad[pl.ds(pl.multiple_of((2 * i + core) * owned, owned), owned), :]
        given[i] = grad[pl.ds(pl.multiple_of((2 * i + 1 - core) * owned, owned), owned), :].astype(bf16)


def fold_kernel(bit, radix, came, *refs):
    kept, arrived, outs = refs[0], refs[1 : 1 + came], refs[1 + came :]
    digit = (lax.axis_index("dp") // bit) % radix

    def block(i):
        total = kept[i]
        for piece in arrived:
            total = total + piece[i].astype(f32)
        return total

    for i in range(kept.shape[0] // radix):
        for j in range(radix):
            other = digit
            for b in (1, 2):
                if j & b:
                    other = flip(other, b)
            value = block(i * radix + other)
            outs[j][i] = value.astype(outs[j].dtype)


def square_kernel(came, lines, *refs):
    kept, arrived, (owned, message) = refs[0], refs[1 : 1 + came], refs[1 + came :]
    total = kept[0]
    for piece in arrived:
        total = total + piece[0].astype(f32)
    owned[...] = total
    count = total.shape[0]
    square = jnp.full((16, total.shape[1]), jnp.sum(total * total), f32)
    first = square.astype(bf16).astype(f32)
    second = (square - first).astype(bf16).astype(f32)
    third = square - first - second
    row = lax.broadcasted_iota(jnp.int32, square.shape, 0)
    terms = jnp.where(row == 0, first, jnp.where(row == 1, second, jnp.where(row == 2, third, 0.0)))
    if count < lines:
        total = jnp.concatenate([total, jnp.zeros((lines - count, total.shape[1]), f32)], axis=0)
    message[0, :lines, :] = total.astype(bf16)
    message[0, lines:, :] = terms.astype(bf16)


def gathered_kernel(messages, square):
    lines = messages.shape[1] - 16
    total = jnp.zeros((16, 128), f32)
    for j in range(messages.shape[0]):
        total = total + messages[j, lines:, 0:128].astype(f32)
    square[...] = jnp.full(square.shape, jnp.sum(total[:, 0:1]), f32)


def moment_kernel(lay, rows, *refs):
    squares, refs = refs[: lay.members], refs[lay.members :]
    basis, refs = refs[: lay.ring], refs[lay.ring :]
    owned, first, second, messages, new_first, new_second, update = refs
    total = squares[0][...]
    for square in squares[1:]:
        total = total + square[...]
    factor = jnp.minimum(1.0, clip_total / (jnp.sqrt(total) + 1e-06))[0:1, 0:1]

    def advance(gradient, one, two):
        clipped = gradient * factor
        one = 0.9 * one + 0.1 * clipped
        two = 0.99 * two + 0.01 * clipped * clipped
        return one, two

    one, two = advance(owned[...], first[...], second[...])
    new_first[...] = one
    new_second[...] = two
    count = owned.shape[0]
    half = owned.shape[1] // 2
    index = lax.axis_index("dp")
    for s in range(lay.ring):
        xor = lax.bitwise_xor(lay.source(index, s), index // lay.members)
        slot = place_slot(lay, xor)
        for k in range(2):
            low = rows + k * 2 * count
            moments = basis[s][low : low + 2 * count, :].astype(f32)
            gradient = messages[slot, :, k * half : (k + 1) * half].astype(f32)[:count]
            one, two = advance(gradient, moments[:count], moments[count:])
            update[slot, :, k * half : (k + 1) * half] = (
                one / first_fix / (jnp.sqrt(two / second_fix) + 1e-08)
            ).astype(bf16)


def place_slot(lay, xor):
    slot, scale = 0, 1
    for bit, radix in reversed(lay.rounds):
        if bit >= lay.members:
            slot = slot + scale * ((xor // (bit // lay.members)) % radix)
            scale *= radix
    return slot


def place(lay, s, side, low, width, rows, source, out, sems):
    index = lax.axis_index("dp")
    core = index % 2
    chip = lay.source(index, s) * lay.sides + side
    copies = []
    for k, owner in enumerate((core, 1 - core)):
        start = pl.multiple_of((chip * 2 + owner) * rows + low, width)
        copies.append(
            pltpu.make_async_copy(
                source.at[:, pl.ds(k * width, width)],
                out.at[:, pl.ds(start, width)],
                sems.at[k],
            )
        )
    return copies


def weight_kernel(lay, rows, s, low, parts, came, first, *refs):
    sides = lay.sides
    mine, refs = refs[:parts], refs[parts:]
    theirs, refs = refs[:parts], refs[parts:]
    grads, refs = refs[:sides], refs[sides:]
    if came is not None:
        arrived, refs = refs[0], refs[1:]
    if not first:
        refs = refs[1:]
    out, refs = refs[0], refs[1:]
    if sides == 2:
        far, refs = refs[0], refs[1:]
    own, sems, came_sems = refs
    height = mine[0].shape[0]
    width = parts * height
    side = (lax.axis_index("dp") // 2) % sides
    copies = []
    if came is not None:
        copies = place(
            lay, came[0], 1 - side, came[1], arrived.shape[1] // 2, rows, arrived, out, came_sems
        )
        for copy in copies:
            copy.start()
    for x in reversed(range(sides)):
        target = own if x == 0 else far
        for k, group in enumerate((mine, theirs)):
            for p, piece in enumerate(group):
                target[:, k * width + p * height : k * width + (p + 1) * height] = lax.dot_general(
                    grads[x][...],
                    piece[...],
                    (((1,), (1,)), ((), ())),
                    preferred_element_type=f32,
                ).astype(bf16)
    owns = place(lay, s, side, low, width, rows, own, out, sems)
    for copy in owns:
        copy.start()
    for copy in owns + copies:
        copy.wait()


def last_kernel(lay, rows, blocks, *refs):
    arrived, (before, out, sems) = refs[: len(blocks)], refs[len(blocks) :]
    side = (lax.axis_index("dp") // 2) % lay.sides
    copies = []
    for k, (s, low) in enumerate(blocks):
        wide = arrived[k].shape[1] // 2
        copies += place(lay, s, 1 - side, low, wide, rows, arrived[k], out, sems.at[k])
    for copy in copies:
        copy.start()
    for copy in copies:
        copy.wait()


def back_kernel(lay, owned, basis, near, other, master, out, update):
    index = lax.axis_index("dp")
    half = lay.n // 2
    for j in range(lay.n):
        owner = index
        for bit in [1 << b for b in range(lay.n.bit_length() - 1)]:
            if slot_to_xor(lay, j) & bit:
                owner = flip(owner, bit)
        piece = near[j] if j < half else other[j - half]
        update[pl.ds(pl.multiple_of(owner * owned, owned), owned), :] = piece.astype(f32)
    out[...] = master[...] - step_size * jnp.dot(
        basis[...], update[...].astype(bf16), preferred_element_type=f32
    )


def slot_to_xor(lay, j):
    xor = 0
    for bit, radix in reversed(lay.rounds):
        xor += (j % radix) * bit
        j //= radix
    return xor


def call(kernel, name, shapes, args, in_specs=None, out_specs=None, scratch=(), flops=0, moved=2**20, **more):
    return pl.pallas_call(
        kernel,
        name=name,
        out_shape=[jax.ShapeDtypeStruct(shape, dtype) for shape, dtype in shapes],
        in_specs=in_specs or [VMEM] * len(args),
        out_specs=out_specs or [VMEM] * len(shapes),
        scratch_shapes=list(scratch),
        compiler_params=PARAMS,
        cost_estimate=pl.CostEstimate(flops=flops, bytes_accessed=moved, transcendentals=0),
        **more,
    )(*args)


def make_per_device(n):
    lay = Layout(n)
    sides, members, ring, rounds = lay.sides, lay.members, lay.ring, lay.rounds
    swap, onward = lay.swap, lay.onward

    def per_device(activations, key_grad, proj_basis, master_weight, first_moment, second_moment):
        tokens, width = activations.shape
        rows, rank = proj_basis.shape
        outs = key_grad.shape[1]
        owned = rank // n
        lines = -(-owned // 16) * 16
        parts = 2 if rows % 256 == 0 else 1
        height = rows // parts

        plan = [(x, 0, ring) for x in range(min(members, 3))]
        if sides == 2:
            plan += [(3, 0, ring // 2), (3, ring // 2, ring // 2)]
        cut = call(
            functools.partial(cut_kernel, lay, rows, plan),
            "cut",
            [((tokens, count * rows), bf16) for x, first, count in plan],
            [activations],
            in_specs=[HBM],
            scratch=[pltpu.SemaphoreType.DMA((members * ring,))],
            moved=4 * tokens * ring * rows * members,
        )

        acts = list(cut)
        far_grad = None
        if sides == 2:
            far_grad = swap(key_grad, 2)
            acts[2] = swap(cut[2], 2)
            acts[3] = swap(after(cut[3], far_grad), 3)
            acts[4] = swap(after(cut[4], acts[2]), 3)
        moments = jnp.concatenate([first_moment, second_moment], axis=0).astype(bf16)
        folded = [moments[:, k * rank : (k + 1) * rank] for k in range(outs // rank)]
        basis = [after(jnp.concatenate([proj_basis] + folded, axis=0), cut[0])]
        weight = [master_weight.astype(bf16)]
        for s in range(1, ring):
            value = basis[-1]
            if s == 2 and sides == 2:
                value = after(value, far_grad)
            if s == 3 and sides == 2:
                value = after(value, acts[2])
            basis.append(onward(value))
            if s == 1:
                weight.append(onward(after(weight[0], basis[1])))
        weight.append(onward(after(weight[1], basis[-1], acts[-1])))

        acts[1] = swap(cut[1], 1)
        if sides == 2:
            near = swap(jnp.concatenate([after(key_grad, acts[1]), far_grad], axis=0), 1)
            grads = [key_grad, near[:tokens], far_grad, near[tokens:]]
        else:
            near = swap(key_grad, 1)
            grads = [key_grad, near]
        theirs = [swap(after(weight[0], near, acts[min(members, 3) - 1]), 1)]

        side_grads = [key_grad, far_grad] if sides == 2 else [key_grad]
        state = {"out": None}
        waiting = []

        def multiply(s, mine, theirs, low=0, gate=None):
            args = [mine if gate is None else after(mine, gate), theirs] + side_grads
            in_specs = [VMEM] * len(args)
            wide = mine.shape[0]
            came = None
            if len(waiting) > 1:
                (came, block) = waiting.pop(0)
                args.append(block)
                in_specs.append(VMEM)
            first = state["out"] is None
            if not first:
                args.append(state["out"])
                in_specs.append(HBM)
            shapes, out_specs = [((tokens, width), bf16)], [HBM]
            if sides == 2:
                shapes.append(((tokens, 2 * wide), bf16))
                out_specs.append(VMEM)
            result = call(
                functools.partial(weight_kernel, lay, rows, s, low, 1, came, first),
                "weight",
                shapes,
                args,
                in_specs,
                out_specs,
                scratch=[
                    pltpu.VMEM((tokens, 2 * wide), bf16),
                    pltpu.SemaphoreType.DMA((2,)),
                    pltpu.SemaphoreType.DMA((2,)),
                ],
                flops=4 * sides * tokens * wide * outs,
                moved=6 * 2**20,
                input_output_aliases={} if first else {len(args) - 1: 0},
            )
            state["out"] = result[0]
            return result[1] if sides == 2 else result[0]

        def give_back(s, block, low=0, gate=None):
            if sides == 1:
                return block
            waiting.append(((s, low), swap(block if gate is None else after(block, gate), 2)))
            return waiting[-1][1]

        first_block = multiply(0, weight[0], theirs[0], gate=acts[-2])
        theirs.append(swap(after(weight[1], theirs[0]), 1))

        total, *gives = call(
            functools.partial(project_kernel, lay, owned, plan),
            "project",
            [((n // 2, owned, outs), f32), ((n // 2, owned, outs), bf16)],
            [after(acts[0], first_block)] + acts[1:] + basis + grads,
            scratch=[pltpu.VMEM((rank, outs), f32)],
            flops=2 * tokens * members * rank * (ring * rows + outs),
            moved=12 * 2**20,
        )
        sent = give_back(0, first_block, gate=acts[-1])

        for k, (bit, radix) in enumerate(rounds):
            if bit == 2 and sides == 2:
                gives = [after(give, sent) for give in gives]
            if bit == members:
                gives = [after(give, weight[2], block) for give in gives]
            came = [swap(give, j * bit) for j, give in zip(range(1, radix), gives)]
            if k == len(rounds) - 1:
                break
            next_bit, next_radix = rounds[k + 1]
            shape = (total.shape[0] // next_radix, owned, outs)
            total, *gives = call(
                functools.partial(fold_kernel, next_bit, next_radix, len(came)),
                "fold",
                [(shape, f32)] + [(shape, bf16)] * (next_radix - 1),
                [total] + came,
                moved=4 * total.size,
            )
            if bit == 1:
                block = multiply(1, weight[1], theirs[1], gate=total)
            if bit == 2:
                later = give_back(1, block, gate=total)

        split = [weight[2][p * height : (p + 1) * height] for p in range(parts)] if ring == 4 else []
        last = []
        if split:
            last.append(onward(after(split[0], *came)))
        owned_rows, message = call(
            functools.partial(square_kernel, len(came), lines),
            "square",
            [((owned, outs), f32), ((1, lines + 16, outs), bf16)],
            [total] + came,
        )
        block = multiply(2, weight[2], swap(weight[2], 1), gate=owned_rows)
        messages = after(message, last[0], block) if split else message
        for bit, radix in reversed(rounds):
            if bit >= members:
                came = [swap(messages, j * bit) for j in range(1, radix)]
                messages = jnp.concatenate([messages] + came, axis=0)
        for p in range(1, len(split)):
            last.append(onward(after(split[p], *came)))
        (square,) = call(gathered_kernel, "gathered", [((8, 128), f32)], [messages])
        if sides == 2:
            sent = give_back(2, block, gate=later)
            square = after(square, sent)
        squares = [square] + [swap(square, x) for x in range(1, members)]
        new_first, new_second, whole = call(
            functools.partial(moment_kernel, lay, rows),
            "moment",
            [((owned, outs), f32), ((owned, outs), f32), ((ring, owned, outs), bf16)],
            squares + basis + [owned_rows, first_moment, second_moment, messages],
        )
        blocks = []
        if split:
            block = multiply(3, last[0], swap(last[0], 1), 0, squares[0])
            sent = give_back(3, after(block, *squares), 0)

        for bit, radix in reversed(rounds[1:]):
            if bit < members:
                whole = after(whole, sent)
                whole = jnp.concatenate(
                    [whole] + [swap(whole, j * bit) for j in range(1, radix)], axis=0
                )
        (new_master,) = call(
            functools.partial(back_kernel, lay, owned),
            "back",
            [(master_weight.shape, f32)],
            [proj_basis, whole, swap(whole, 1), master_weight],
            scratch=[pltpu.VMEM((rank, outs), f32)],
            flops=2 * rows * rank * outs,
            moved=8 * 2**20,
        )

        for p in range(1, len(split)):
            give_back(3, multiply(3, last[p], swap(last[p], 1), p * height), p * height)
        if not split:
            for s in range(3, ring):
                weight.append(onward(weight[s - 1]))
                give_back(s, multiply(s, weight[s], swap(weight[s], 1)))
        activation_grad = state["out"]
        if waiting:
            (activation_grad,) = call(
                functools.partial(last_kernel, lay, rows, [spot for spot, block in waiting]),
                "last",
                [((tokens, width), bf16)],
                [block for spot, block in waiting] + [activation_grad],
                [VMEM] * len(waiting) + [HBM],
                [HBM],
                scratch=[pltpu.SemaphoreType.DMA((len(waiting), 2))],
                input_output_aliases={len(waiting): 0},
            )
        return (activation_grad, new_master, new_first, new_second)

    return per_device


def solution(mesh):
    spec = P(("groups", "dp"), None)
    return jax.shard_map(
        make_per_device(mesh.shape["dp"]),
        mesh=mesh,
        in_specs=(spec,) * 6,
        out_specs=(spec,) * 4,
        check_vma=False,
    )
```

```python
import functools
import jax
import jax.numpy as jnp
from jax import lax
from jax.experimental import pallas as pl
from jax.experimental.pallas import tpu as pltpu
from jax.sharding import PartitionSpec as P

clip_total = 512.0
step_size = 0.01
first_fix = 1.0 - 0.9**10
second_fix = 1.0 - 0.99**10

f32 = jnp.float32
bf16 = jnp.bfloat16
HBM = pl.BlockSpec(memory_space=pl.ANY)
VMEM = pl.BlockSpec(memory_space=pltpu.VMEM)
PARAMS = pltpu.CompilerParams(vmem_limit_bytes=40 * 2**20)


def after(value, *others):
    return lax.optimization_barrier((value,) + others)[0]


class Layout:
    def __init__(self, n):
        self.n = n
        self.sides = 2 if n == 16 else 1
        self.members = 2 * self.sides
        self.ring = n // self.members
        ring, members = self.ring, self.members
        order = [0, 1, 3, 2] if ring == 4 else list(range(ring))
        self.forward = [
            (order[k] * members + m, order[(k + 1) % ring] * members + m)
            for k in range(ring)
            for m in range(members)
        ]
        self.rounds = [(1, 2)]
        bit = 2
        if self.sides == 2:
            self.rounds.append((2, 2))
            bit = 4
        while bit < n:
            radix = 4 if 2 * bit < n else 2
            self.rounds.append((bit, radix))
            bit *= radix

    def swap(self, value, bit):
        return lax.ppermute(value, "dp", [(i, i ^ bit) for i in range(self.n)])

    def onward(self, value):
        return lax.ppermute(value, "dp", self.forward)

    def source(self, index, s):
        z = index // self.members
        if self.ring != 4:
            return (z - s + self.ring) % self.ring
        k = (z + z // 2 * (5 - 2 * z) - s + 4) % 4
        return k + k // 2 * (5 - 2 * k)


def flip(value, bit):
    return value + bit - 2 * bit * ((value // bit) % 2)


def cut_kernel(lay, rows, plan, act, *refs):
    pieces, sems = refs[:-1], refs[-1]
    index = lax.axis_index("dp")
    member = index % lay.members
    copies = []
    for (x, first, count), piece in zip(plan, pieces):
        owner = member
        for bit in (1, 2):
            if x & bit:
                owner = flip(owner, bit)
        for s in range(first, first + count):
            start = pl.multiple_of((lay.source(index, s) * lay.members + owner) * rows, rows)
            copies.append(
                pltpu.make_async_copy(
                    act.at[:, pl.ds(start, rows)],
                    piece.at[:, pl.ds((s - first) * rows, rows)],
                    sems.at[len(copies)],
                )
            )
    for copy in copies:
        copy.start()
    for copy in copies:
        copy.wait()


def project_kernel(lay, owned, plan, *refs):
    members, ring = lay.members, lay.ring
    acts, refs = refs[: len(plan)], refs[len(plan) :]
    basis, refs = refs[:ring], refs[ring:]
    grads, refs = refs[:members], refs[members:]
    kept, given, grad = refs
    rows = acts[0].shape[1] // ring
    core = lax.axis_index("dp") % 2
    for x in range(members):
        total = None
        for (x_, first, count), piece in zip(plan, acts):
            if x_ != x:
                continue
            for s in range(first, first + count):
                term = jnp.dot(
                    piece[:, (s - first) * rows : (s - first + 1) * rows],
                    basis[s][:rows, :],
                    preferred_element_type=f32,
                )
                total = term if total is None else total + term
        term = lax.dot_general(
            total.astype(bf16),
            grads[x][...],
            (((0,), (0,)), ((), ())),
            preferred_element_type=f32,
        )
        if x == 0:
            grad[...] = term
        else:
            grad[...] += term
    for i in range(lay.n // 2):
        kept[i] = grad[pl.ds(pl.multiple_of((2 * i + core) * owned, owned), owned), :]
        given[i] = grad[pl.ds(pl.multiple_of((2 * i + 1 - core) * owned, owned), owned), :].astype(bf16)


def fold_kernel(bit, radix, came, *refs):
    kept, arrived, outs = refs[0], refs[1 : 1 + came], refs[1 + came :]
    digit = (lax.axis_index("dp") // bit) % radix

    def block(i):
        total = kept[i]
        for piece in arrived:
            total = total + piece[i].astype(f32)
        return total

    for i in range(kept.shape[0] // radix):
        for j in range(radix):
            other = digit
            for b in (1, 2):
                if j & b:
                    other = flip(other, b)
            value = block(i * radix + other)
            outs[j][i] = value.astype(outs[j].dtype)


def square_kernel(came, lines, *refs):
    kept, arrived, (owned, message) = refs[0], refs[1 : 1 + came], refs[1 + came :]
    total = kept[0]
    for piece in arrived:
        total = total + piece[0].astype(f32)
    owned[...] = total
    count = total.shape[0]
    square = jnp.full((16, total.shape[1]), jnp.sum(total * total), f32)
    first = square.astype(bf16).astype(f32)
    second = (square - first).astype(bf16).astype(f32)
    third = square - first - second
    row = lax.broadcasted_iota(jnp.int32, square.shape, 0)
    terms = jnp.where(row == 0, first, jnp.where(row == 1, second, jnp.where(row == 2, third, 0.0)))
    if count < lines:
        total = jnp.concatenate([total, jnp.zeros((lines - count, total.shape[1]), f32)], axis=0)
    message[0, :lines, :] = total.astype(bf16)
    message[0, lines:, :] = terms.astype(bf16)


def gathered_kernel(messages, square):
    lines = messages.shape[1] - 16
    total = jnp.zeros((16, 128), f32)
    for j in range(messages.shape[0]):
        total = total + messages[j, lines:, 0:128].astype(f32)
    square[...] = jnp.full(square.shape, jnp.sum(total[:, 0:1]), f32)


def moment_kernel(lay, rows, *refs):
    squares, refs = refs[: lay.members], refs[lay.members :]
    basis, refs = refs[: lay.ring], refs[lay.ring :]
    owned, first, second, messages, new_first, new_second, update = refs
    total = squares[0][...]
    for square in squares[1:]:
        total = total + square[...]
    factor = jnp.minimum(1.0, clip_total / (jnp.sqrt(total) + 1e-06))[0:1, 0:1]

    def advance(gradient, one, two):
        clipped = gradient * factor
        one = 0.9 * one + 0.1 * clipped
        two = 0.99 * two + 0.01 * clipped * clipped
        return one, two

    one, two = advance(owned[...], first[...], second[...])
    new_first[...] = one
    new_second[...] = two
    count = owned.shape[0]
    half = owned.shape[1] // 2
    index = lax.axis_index("dp")
    for s in range(lay.ring):
        xor = lax.bitwise_xor(lay.source(index, s), index // lay.members)
        slot = place_slot(lay, xor)
        for k in range(2):
            low = rows + k * 2 * count
            moments = basis[s][low : low + 2 * count, :].astype(f32)
            gradient = messages[slot, :, k * half : (k + 1) * half].astype(f32)[:count]
            one, two = advance(gradient, moments[:count], moments[count:])
            update[slot, :, k * half : (k + 1) * half] = (
                one / first_fix / (jnp.sqrt(two / second_fix) + 1e-08)
            ).astype(bf16)


def place_slot(lay, xor):
    slot, scale = 0, 1
    for bit, radix in reversed(lay.rounds):
        if bit >= lay.members:
            slot = slot + scale * ((xor // (bit // lay.members)) % radix)
            scale *= radix
    return slot


def place(lay, s, side, low, width, rows, source, out, sems):
    index = lax.axis_index("dp")
    core = index % 2
    chip = lay.source(index, s) * lay.sides + side
    copies = []
    for k, owner in enumerate((core, 1 - core)):
        start = pl.multiple_of((chip * 2 + owner) * rows + low, width)
        copies.append(
            pltpu.make_async_copy(
                source.at[:, pl.ds(k * width, width)],
                out.at[:, pl.ds(start, width)],
                sems.at[k],
            )
        )
    return copies


def weight_kernel(lay, rows, s, low, parts, came, first, *refs):
    sides = lay.sides
    mine, refs = refs[:parts], refs[parts:]
    theirs, refs = refs[:parts], refs[parts:]
    grads, refs = refs[:sides], refs[sides:]
    if came is not None:
        arrived, refs = refs[0], refs[1:]
    if not first:
        refs = refs[1:]
    out, refs = refs[0], refs[1:]
    if sides == 2:
        far, refs = refs[0], refs[1:]
    own, sems, came_sems = refs
    height = mine[0].shape[0]
    width = parts * height
    side = (lax.axis_index("dp") // 2) % sides
    copies = []
    if came is not None:
        copies = place(
            lay, came[0], 1 - side, came[1], arrived.shape[1] // 2, rows, arrived, out, came_sems
        )
        for copy in copies:
            copy.start()
    for x in reversed(range(sides)):
        target = own if x == 0 else far
        for k, group in enumerate((mine, theirs)):
            for p, piece in enumerate(group):
                target[:, k * width + p * height : k * width + (p + 1) * height] = lax.dot_general(
                    grads[x][...],
                    piece[...],
                    (((1,), (1,)), ((), ())),
                    preferred_element_type=f32,
                ).astype(bf16)
    owns = place(lay, s, side, low, width, rows, own, out, sems)
    for copy in owns:
        copy.start()
    for copy in owns + copies:
        copy.wait()


def last_kernel(lay, rows, blocks, *refs):
    arrived, (before, out, sems) = refs[: len(blocks)], refs[len(blocks) :]
    side = (lax.axis_index("dp") // 2) % lay.sides
    copies = []
    for k, (s, low) in enumerate(blocks):
        wide = arrived[k].shape[1] // 2
        copies += place(lay, s, 1 - side, low, wide, rows, arrived[k], out, sems.at[k])
    for copy in copies:
        copy.start()
    for copy in copies:
        copy.wait()


def back_kernel(lay, owned, basis, near, other, master, out, update):
    index = lax.axis_index("dp")
    half = lay.n // 2
    for j in range(lay.n):
        owner = index
        for bit in [1 << b for b in range(lay.n.bit_length() - 1)]:
            if slot_to_xor(lay, j) & bit:
                owner = flip(owner, bit)
        piece = near[j] if j < half else other[j - half]
        update[pl.ds(pl.multiple_of(owner * owned, owned), owned), :] = piece.astype(f32)
    out[...] = master[...] - step_size * jnp.dot(
        basis[...], update[...].astype(bf16), preferred_element_type=f32
    )


def slot_to_xor(lay, j):
    xor = 0
    for bit, radix in reversed(lay.rounds):
        xor += (j % radix) * bit
        j //= radix
    return xor


def call(kernel, name, shapes, args, in_specs=None, out_specs=None, scratch=(), flops=0, moved=2**20, **more):
    return pl.pallas_call(
        kernel,
        name=name,
        out_shape=[jax.ShapeDtypeStruct(shape, dtype) for shape, dtype in shapes],
        in_specs=in_specs or [VMEM] * len(args),
        out_specs=out_specs or [VMEM] * len(shapes),
        scratch_shapes=list(scratch),
        compiler_params=PARAMS,
        cost_estimate=pl.CostEstimate(flops=flops, bytes_accessed=moved, transcendentals=0),
        **more,
    )(*args)


def make_per_device(n):
    lay = Layout(n)
    sides, members, ring, rounds = lay.sides, lay.members, lay.ring, lay.rounds
    swap, onward = lay.swap, lay.onward

    def per_device(activations, key_grad, proj_basis, master_weight, first_moment, second_moment):
        tokens, width = activations.shape
        rows, rank = proj_basis.shape
        outs = key_grad.shape[1]
        owned = rank // n
        lines = -(-owned // 16) * 16
        parts = 2 if rows % 256 == 0 else 1
        height = rows // parts

        plan = [(x, 0, ring) for x in range(min(members, 3))]
        if sides == 2:
            plan += [(3, 0, ring // 2), (3, ring // 2, ring // 2)]
        cut = call(
            functools.partial(cut_kernel, lay, rows, plan),
            "cut",
            [((tokens, count * rows), bf16) for x, first, count in plan],
            [activations],
            in_specs=[HBM],
            scratch=[pltpu.SemaphoreType.DMA((members * ring,))],
            moved=4 * tokens * ring * rows * members,
        )

        acts = list(cut)
        far_grad = None
        if sides == 2:
            far_grad = swap(key_grad, 2)
            acts[2] = swap(cut[2], 2)
            acts[3] = swap(after(cut[3], far_grad), 3)
            acts[4] = swap(after(cut[4], acts[2]), 3)
        moments = jnp.concatenate([first_moment, second_moment], axis=0).astype(bf16)
        folded = [moments[:, k * rank : (k + 1) * rank] for k in range(outs // rank)]
        basis = [after(jnp.concatenate([proj_basis] + folded, axis=0), cut[0])]
        weight = [master_weight.astype(bf16)]
        halves = [weight[0][p * height : (p + 1) * height] for p in range(parts)]
        for s in range(1, ring):
            value = basis[-1]
            if s == 2 and sides == 2:
                value = after(value, far_grad)
            basis.append(onward(value))
        halves = [onward(half if p == 0 else after(half, acts[-2])) for p, half in enumerate(halves)]

        acts[1] = swap(cut[1], 1)
        if sides == 2:
            near = swap(jnp.concatenate([after(key_grad, acts[1]), far_grad], axis=0), 1)
            grads = [key_grad, near[:tokens], far_grad, near[tokens:]]
        else:
            near = swap(key_grad, 1)
            grads = [key_grad, near]
        theirs = [swap(after(weight[0], near, acts[min(members, 3) - 1]), 1)]

        side_grads = [key_grad, far_grad] if sides == 2 else [key_grad]
        state = {"out": None}
        waiting = []

        def multiply(s, mine, theirs, low=0, gate=None):
            args = [mine if gate is None else after(mine, gate), theirs] + side_grads
            in_specs = [VMEM] * len(args)
            wide = mine.shape[0]
            came = None
            if len(waiting) > 1:
                (came, block) = waiting.pop(0)
                args.append(block)
                in_specs.append(VMEM)
            first = state["out"] is None
            if not first:
                args.append(state["out"])
                in_specs.append(HBM)
            shapes, out_specs = [((tokens, width), bf16)], [HBM]
            if sides == 2:
                shapes.append(((tokens, 2 * wide), bf16))
                out_specs.append(VMEM)
            result = call(
                functools.partial(weight_kernel, lay, rows, s, low, 1, came, first),
                "weight",
                shapes,
                args,
                in_specs,
                out_specs,
                scratch=[
                    pltpu.VMEM((tokens, 2 * wide), bf16),
                    pltpu.SemaphoreType.DMA((2,)),
                    pltpu.SemaphoreType.DMA((2,)),
                ],
                flops=4 * sides * tokens * wide * outs,
                moved=6 * 2**20,
                input_output_aliases={} if first else {len(args) - 1: 0},
            )
            state["out"] = result[0]
            return result[1] if sides == 2 else result[0]

        def give_back(s, block, low=0, gate=None):
            if sides == 1:
                return block
            waiting.append(((s, low), swap(block if gate is None else after(block, gate), 2)))
            return waiting[-1][1]

        first_block = multiply(0, weight[0], theirs[0], gate=acts[-2])
        total, *gives = call(
            functools.partial(project_kernel, lay, owned, plan),
            "project",
            [((n // 2, owned, outs), f32), ((n // 2, owned, outs), bf16)],
            [after(acts[0], first_block)] + acts[1:] + basis + grads,
            scratch=[pltpu.VMEM((rank, outs), f32)],
            flops=2 * tokens * members * rank * (ring * rows + outs),
            moved=12 * 2**20,
        )
        halves[-1] = after(halves[-1], total)
        weight.append(jnp.concatenate(halves, axis=0))
        weight.append(onward(weight[1]))
        theirs.append(swap(weight[1], 1))

        for k, (bit, radix) in enumerate(rounds):
            if bit == members:
                gives = [after(give, weight[2], sent if sides == 2 else block) for give in gives]
            came = [swap(give, j * bit) for j, give in zip(range(1, radix), gives)]
            if k == len(rounds) - 1:
                break
            next_bit, next_radix = rounds[k + 1]
            shape = (total.shape[0] // next_radix, owned, outs)
            total, *gives = call(
                functools.partial(fold_kernel, next_bit, next_radix, len(came)),
                "fold",
                [(shape, f32)] + [(shape, bf16)] * (next_radix - 1),
                [total] + came,
                moved=4 * total.size,
            )
            if bit == 1:
                block = multiply(1, weight[1], theirs[1], gate=total)
            if bit == 2:
                sent = give_back(0, first_block, gate=total)
                later = give_back(1, block, gate=total)
                weight[2] = after(weight[2], total)

        split = [weight[2][p * height : (p + 1) * height] for p in range(parts)] if ring == 4 else []
        last = []
        if split:
            last.append(onward(after(split[0], *came)))
        owned_rows, message = call(
            functools.partial(square_kernel, len(came), lines),
            "square",
            [((owned, outs), f32), ((1, lines + 16, outs), bf16)],
            [total] + came,
        )
        block = multiply(2, weight[2], swap(weight[2], 1), gate=owned_rows)
        messages = after(message, last[0], block) if split else message
        for bit, radix in reversed(rounds):
            if bit >= members:
                came = [swap(messages, j * bit) for j in range(1, radix)]
                messages = jnp.concatenate([messages] + came, axis=0)
        for p in range(1, len(split)):
            last.append(onward(after(split[p], *came)))
        (square,) = call(gathered_kernel, "gathered", [((8, 128), f32)], [messages])
        if sides == 2:
            sent = give_back(2, block, gate=later)
            square = after(square, sent)
        squares = [square] + [swap(square, x) for x in range(1, members)]
        new_first, new_second, whole = call(
            functools.partial(moment_kernel, lay, rows),
            "moment",
            [((owned, outs), f32), ((owned, outs), f32), ((ring, owned, outs), bf16)],
            squares + basis + [owned_rows, first_moment, second_moment, messages],
        )
        blocks = []
        if split:
            block = multiply(3, last[0], swap(last[0], 1), 0, squares[0])
            sent = give_back(3, after(block, *squares), 0)

        for bit, radix in reversed(rounds[1:]):
            if bit < members:
                whole = after(whole, sent)
                whole = jnp.concatenate(
                    [whole] + [swap(whole, j * bit) for j in range(1, radix)], axis=0
                )
        (new_master,) = call(
            functools.partial(back_kernel, lay, owned),
            "back",
            [(master_weight.shape, f32)],
            [proj_basis, whole, swap(whole, 1), master_weight],
            scratch=[pltpu.VMEM((rank, outs), f32)],
            flops=2 * rows * rank * outs,
            moved=8 * 2**20,
        )

        for p in range(1, len(split)):
            give_back(3, multiply(3, last[p], swap(last[p], 1), p * height), p * height)
        if not split:
            for s in range(3, ring):
                weight.append(onward(weight[s - 1]))
                give_back(s, multiply(s, weight[s], swap(weight[s], 1)))
        activation_grad = state["out"]
        if waiting:
            (activation_grad,) = call(
                functools.partial(last_kernel, lay, rows, [spot for spot, block in waiting]),
                "last",
                [((tokens, width), bf16)],
                [after(block, new_master) for spot, block in waiting] + [activation_grad],
                [VMEM] * len(waiting) + [HBM],
                [HBM],
                scratch=[pltpu.SemaphoreType.DMA((len(waiting), 2))],
                input_output_aliases={len(waiting): 0},
            )
        return (activation_grad, new_master, new_first, new_second)

    return per_device


def solution(mesh):
    spec = P(("groups", "dp"), None)
    return jax.shard_map(
        make_per_device(mesh.shape["dp"]),
        mesh=mesh,
        in_specs=(spec,) * 6,
        out_specs=(spec,) * 4,
        check_vma=False,
    )
```

```python
import functools
import jax
import jax.numpy as jnp
from jax import lax
from jax.experimental import pallas as pl
from jax.experimental.pallas import tpu as pltpu
from jax.sharding import PartitionSpec as P

clip_total = 512.0
step_size = 0.01
first_fix = 1.0 - 0.9**10
second_fix = 1.0 - 0.99**10

f32 = jnp.float32
bf16 = jnp.bfloat16
HBM = pl.BlockSpec(memory_space=pl.ANY)
VMEM = pl.BlockSpec(memory_space=pltpu.VMEM)
PARAMS = pltpu.CompilerParams(vmem_limit_bytes=40 * 2**20)


def after(value, *others):
    return lax.optimization_barrier((value,) + others)[0]


class Layout:
    def __init__(self, n):
        self.n = n
        self.sides = 2 if n == 16 else 1
        self.members = 2 * self.sides
        self.ring = n // self.members
        ring, members = self.ring, self.members
        order = [0, 1, 3, 2] if ring == 4 else list(range(ring))
        self.forward = [
            (order[k] * members + m, order[(k + 1) % ring] * members + m)
            for k in range(ring)
            for m in range(members)
        ]
        self.rounds = [(1, 2)]
        bit = 2
        if self.sides == 2:
            self.rounds.append((2, 2))
            bit = 4
        while bit < n:
            radix = 4 if 2 * bit < n else 2
            self.rounds.append((bit, radix))
            bit *= radix

    def swap(self, value, bit):
        return lax.ppermute(value, "dp", [(i, i ^ bit) for i in range(self.n)])

    def onward(self, value):
        return lax.ppermute(value, "dp", self.forward)

    def source(self, index, s):
        z = index // self.members
        if self.ring != 4:
            return (z - s + self.ring) % self.ring
        k = (z + z // 2 * (5 - 2 * z) - s + 4) % 4
        return k + k // 2 * (5 - 2 * k)


def flip(value, bit):
    return value + bit - 2 * bit * ((value // bit) % 2)


def cut_kernel(lay, rows, plan, act, key_grad, *refs):
    pieces, sems = refs[:-1], refs[-1]
    index = lax.axis_index("dp")
    member = index % lay.members
    copies = []
    for (x, first, count), piece in zip(plan, pieces):
        owner = member
        for bit in (1, 2):
            if x & bit:
                owner = flip(owner, bit)
        for s in range(first, first + count):
            start = pl.multiple_of((lay.source(index, s) * lay.members + owner) * rows, rows)
            copies.append(
                pltpu.make_async_copy(
                    act.at[:, pl.ds(start, rows)],
                    piece.at[:, pl.ds((s - first) * rows, rows)],
                    sems.at[len(copies)],
                )
            )
    if lay.sides == 2:
        copies.append(
            pltpu.make_async_copy(
                key_grad,
                pieces[2].at[:, pl.ds(lay.ring * rows, key_grad.shape[1])],
                sems.at[len(copies)],
            )
        )
    for copy in copies:
        copy.start()
    for copy in copies:
        copy.wait()


def project_kernel(lay, owned, plan, *refs):
    members, ring = lay.members, lay.ring
    acts, refs = refs[: len(plan)], refs[len(plan) :]
    basis, refs = refs[:ring], refs[ring:]
    grads, refs = refs[:members], refs[members:]
    kept, given, grad = refs
    rows = acts[0].shape[1] // ring
    core = lax.axis_index("dp") % 2
    for x in range(members):
        total = None
        for (x_, first, count), piece in zip(plan, acts):
            if x_ != x:
                continue
            for s in range(first, first + count):
                term = jnp.dot(
                    piece[:, (s - first) * rows : (s - first + 1) * rows],
                    basis[s][:rows, :],
                    preferred_element_type=f32,
                )
                total = term if total is None else total + term
        term = lax.dot_general(
            total.astype(bf16),
            grads[x][...],
            (((0,), (0,)), ((), ())),
            preferred_element_type=f32,
        )
        if x == 0:
            grad[...] = term
        else:
            grad[...] += term
    for i in range(lay.n // 2):
        kept[i] = grad[pl.ds(pl.multiple_of((2 * i + core) * owned, owned), owned), :]
        given[i] = grad[pl.ds(pl.multiple_of((2 * i + 1 - core) * owned, owned), owned), :].astype(bf16)


def fold_kernel(bit, radix, came, *refs):
    kept, arrived, outs = refs[0], refs[1 : 1 + came], refs[1 + came :]
    digit = (lax.axis_index("dp") // bit) % radix

    def block(i):
        total = kept[i]
        for piece in arrived:
            total = total + piece[i].astype(f32)
        return total

    for i in range(kept.shape[0] // radix):
        for j in range(radix):
            other = digit
            for b in (1, 2):
                if j & b:
                    other = flip(other, b)
            value = block(i * radix + other)
            outs[j][i] = value.astype(outs[j].dtype)


def square_kernel(came, lines, *refs):
    kept, arrived, (owned, message) = refs[0], refs[1 : 1 + came], refs[1 + came :]
    total = kept[0]
    for piece in arrived:
        total = total + piece[0].astype(f32)
    owned[...] = total
    count = total.shape[0]
    square = jnp.full((16, total.shape[1]), jnp.sum(total * total), f32)
    first = square.astype(bf16).astype(f32)
    second = (square - first).astype(bf16).astype(f32)
    third = square - first - second
    row = lax.broadcasted_iota(jnp.int32, square.shape, 0)
    terms = jnp.where(row == 0, first, jnp.where(row == 1, second, jnp.where(row == 2, third, 0.0)))
    if count < lines:
        total = jnp.concatenate([total, jnp.zeros((lines - count, total.shape[1]), f32)], axis=0)
    message[0, :lines, :] = total.astype(bf16)
    message[0, lines:, :] = terms.astype(bf16)


def gathered_kernel(messages, square):
    lines = messages.shape[1] - 16
    total = jnp.zeros((16, 128), f32)
    for j in range(messages.shape[0]):
        total = total + messages[j, lines:, 0:128].astype(f32)
    square[...] = jnp.full(square.shape, jnp.sum(total[:, 0:1]), f32)


def moment_kernel(lay, rows, *refs):
    squares, refs = refs[: lay.members], refs[lay.members :]
    basis, refs = refs[: lay.ring], refs[lay.ring :]
    owned, first, second, messages, new_first, new_second, update = refs
    total = squares[0][...]
    for square in squares[1:]:
        total = total + square[...]
    factor = jnp.minimum(1.0, clip_total / (jnp.sqrt(total) + 1e-06))[0:1, 0:1]

    def advance(gradient, one, two):
        clipped = gradient * factor
        one = 0.9 * one + 0.1 * clipped
        two = 0.99 * two + 0.01 * clipped * clipped
        return one, two

    one, two = advance(owned[...], first[...], second[...])
    new_first[...] = one
    new_second[...] = two
    count = owned.shape[0]
    half = owned.shape[1] // 2
    index = lax.axis_index("dp")
    for s in range(lay.ring):
        xor = lax.bitwise_xor(lay.source(index, s), index // lay.members)
        slot = place_slot(lay, xor)
        for k in range(2):
            low = rows + k * 2 * count
            moments = basis[s][low : low + 2 * count, :].astype(f32)
            gradient = messages[slot, :, k * half : (k + 1) * half].astype(f32)[:count]
            one, two = advance(gradient, moments[:count], moments[count:])
            update[slot, :, k * half : (k + 1) * half] = (
                one / first_fix / (jnp.sqrt(two / second_fix) + 1e-08)
            ).astype(bf16)


def place_slot(lay, xor):
    slot, scale = 0, 1
    for bit, radix in reversed(lay.rounds):
        if bit >= lay.members:
            slot = slot + scale * ((xor // (bit // lay.members)) % radix)
            scale *= radix
    return slot


def place(lay, s, side, low, width, rows, source, out, sems):
    index = lax.axis_index("dp")
    core = index % 2
    chip = lay.source(index, s) * lay.sides + side
    copies = []
    for k, owner in enumerate((core, 1 - core)):
        start = pl.multiple_of((chip * 2 + owner) * rows + low, width)
        copies.append(
            pltpu.make_async_copy(
                source.at[:, pl.ds(k * width, width)],
                out.at[:, pl.ds(start, width)],
                sems.at[k],
            )
        )
    return copies


def weight_kernel(lay, rows, s, low, parts, came, first, *refs):
    sides = lay.sides
    mine, refs = refs[:parts], refs[parts:]
    theirs, refs = refs[:parts], refs[parts:]
    grads, refs = refs[:sides], refs[sides:]
    if came is not None:
        arrived, refs = refs[0], refs[1:]
    if not first:
        refs = refs[1:]
    out, refs = refs[0], refs[1:]
    if sides == 2:
        far, refs = refs[0], refs[1:]
    own, sems, came_sems = refs
    height = mine[0].shape[0]
    width = parts * height
    side = (lax.axis_index("dp") // 2) % sides
    copies = []
    if came is not None:
        copies = place(
            lay, came[0], 1 - side, came[1], arrived.shape[1] // 2, rows, arrived, out, came_sems
        )
        for copy in copies:
            copy.start()
    for x in reversed(range(sides)):
        target = own if x == 0 else far
        for k, group in enumerate((mine, theirs)):
            for p, piece in enumerate(group):
                target[:, k * width + p * height : k * width + (p + 1) * height] = lax.dot_general(
                    grads[x][...],
                    piece[...],
                    (((1,), (1,)), ((), ())),
                    preferred_element_type=f32,
                ).astype(bf16)
    owns = place(lay, s, side, low, width, rows, own, out, sems)
    for copy in owns:
        copy.start()
    for copy in owns + copies:
        copy.wait()


def last_kernel(lay, rows, blocks, *refs):
    arrived, (before, out, sems) = refs[: len(blocks)], refs[len(blocks) :]
    side = (lax.axis_index("dp") // 2) % lay.sides
    copies = []
    for k, (s, low) in enumerate(blocks):
        wide = arrived[k].shape[1] // 2
        copies += place(lay, s, 1 - side, low, wide, rows, arrived[k], out, sems.at[k])
    for copy in copies:
        copy.start()
    for copy in copies:
        copy.wait()


def back_kernel(lay, owned, basis, near, other, master, out, update):
    index = lax.axis_index("dp")
    half = lay.n // 2
    for j in range(lay.n):
        owner = index
        for bit in [1 << b for b in range(lay.n.bit_length() - 1)]:
            if slot_to_xor(lay, j) & bit:
                owner = flip(owner, bit)
        piece = near[j] if j < half else other[j - half]
        update[pl.ds(pl.multiple_of(owner * owned, owned), owned), :] = piece.astype(f32)
    out[...] = master[...] - step_size * jnp.dot(
        basis[...], update[...].astype(bf16), preferred_element_type=f32
    )


def slot_to_xor(lay, j):
    xor = 0
    for bit, radix in reversed(lay.rounds):
        xor += (j % radix) * bit
        j //= radix
    return xor


def call(kernel, name, shapes, args, in_specs=None, out_specs=None, scratch=(), flops=0, moved=2**20, **more):
    return pl.pallas_call(
        kernel,
        name=name,
        out_shape=[jax.ShapeDtypeStruct(shape, dtype) for shape, dtype in shapes],
        in_specs=in_specs or [VMEM] * len(args),
        out_specs=out_specs or [VMEM] * len(shapes),
        scratch_shapes=list(scratch),
        compiler_params=PARAMS,
        cost_estimate=pl.CostEstimate(flops=flops, bytes_accessed=moved, transcendentals=0),
        **more,
    )(*args)


def make_per_device(n):
    lay = Layout(n)
    sides, members, ring, rounds = lay.sides, lay.members, lay.ring, lay.rounds
    swap, onward = lay.swap, lay.onward

    def per_device(activations, key_grad, proj_basis, master_weight, first_moment, second_moment):
        tokens, width = activations.shape
        rows, rank = proj_basis.shape
        outs = key_grad.shape[1]
        owned = rank // n
        lines = -(-owned // 16) * 16
        parts = 2 if rows % 256 == 0 else 1
        height = rows // parts

        plan = [(x, 0, ring) for x in range(members)]
        wides = [ring * rows + (outs if x == 2 else 0) for x in range(members)]
        cut = call(
            functools.partial(cut_kernel, lay, rows, plan),
            "cut",
            [((tokens, wide), bf16) for wide in wides],
            [activations, key_grad],
            in_specs=[HBM, HBM],
            scratch=[pltpu.SemaphoreType.DMA((members * ring + 1,))],
            moved=4 * tokens * ring * rows * members,
        )

        acts = [cut[0]] + [swap(cut[x], x) for x in range(1, members)]
        moments = jnp.concatenate([first_moment, second_moment], axis=0).astype(bf16)
        folded = [moments[:, k * rank : (k + 1) * rank] for k in range(outs // rank)]
        basis = [after(jnp.concatenate([proj_basis] + folded, axis=0), cut[0])]
        for s in range(1, ring):
            basis.append(onward(basis[-1]))
        weight = [master_weight.astype(bf16)]
        weight.append(onward(after(weight[0], basis[-1])))

        if sides == 2:
            far_grad = acts[2][:, ring * rows :]
            near = swap(jnp.concatenate([key_grad, far_grad], axis=0), 1)
            grads = [key_grad, near[:tokens], far_grad, near[tokens:]]
        else:
            near = swap(key_grad, 1)
            grads = [key_grad, near]
        theirs = [swap(after(weight[0], basis[1]), 1)]

        side_grads = [key_grad, far_grad] if sides == 2 else [key_grad]
        state = {"out": None}
        waiting = []

        def multiply(s, mine, theirs, low=0, gate=None):
            args = [mine if gate is None else after(mine, gate), theirs] + side_grads
            in_specs = [VMEM] * len(args)
            wide = mine.shape[0]
            came = None
            if len(waiting) > 1:
                (came, block) = waiting.pop(0)
                args.append(block)
                in_specs.append(VMEM)
            first = state["out"] is None
            if not first:
                args.append(state["out"])
                in_specs.append(HBM)
            shapes, out_specs = [((tokens, width), bf16)], [HBM]
            if sides == 2:
                shapes.append(((tokens, 2 * wide), bf16))
                out_specs.append(VMEM)
            result = call(
                functools.partial(weight_kernel, lay, rows, s, low, 1, came, first),
                "weight",
                shapes,
                args,
                in_specs,
                out_specs,
                scratch=[
                    pltpu.VMEM((tokens, 2 * wide), bf16),
                    pltpu.SemaphoreType.DMA((2,)),
                    pltpu.SemaphoreType.DMA((2,)),
                ],
                flops=4 * sides * tokens * wide * outs,
                moved=6 * 2**20,
                input_output_aliases={} if first else {len(args) - 1: 0},
            )
            state["out"] = result[0]
            return result[1] if sides == 2 else result[0]

        def give_back(s, block, low=0, gate=None):
            if sides == 1:
                return block
            waiting.append(((s, low), swap(block if gate is None else after(block, gate), 2)))
            return waiting[-1][1]

        first_block = multiply(0, weight[0], theirs[0])
        total, *gives = call(
            functools.partial(project_kernel, lay, owned, plan),
            "project",
            [((n // 2, owned, outs), f32), ((n // 2, owned, outs), bf16)],
            [after(acts[0], first_block)] + acts[1:] + basis + grads,
            scratch=[pltpu.VMEM((rank, outs), f32)],
            flops=2 * tokens * members * rank * (ring * rows + outs),
            moved=12 * 2**20,
        )
        weight.append(onward(weight[1]))
        theirs.append(swap(weight[1], 1))

        for k, (bit, radix) in enumerate(rounds):
            if bit == members:
                gives = [after(give, weight[2], sent if sides == 2 else block) for give in gives]
            came = [swap(give, j * bit) for j, give in zip(range(1, radix), gives)]
            if k == len(rounds) - 1:
                break
            next_bit, next_radix = rounds[k + 1]
            shape = (total.shape[0] // next_radix, owned, outs)
            total, *gives = call(
                functools.partial(fold_kernel, next_bit, next_radix, len(came)),
                "fold",
                [(shape, f32)] + [(shape, bf16)] * (next_radix - 1),
                [total] + came,
                moved=4 * total.size,
            )
            if bit == 1:
                block = multiply(1, weight[1], theirs[1], gate=total)
            if bit == 2:
                sent = give_back(0, first_block, gate=total)
                later = give_back(1, block, gate=total)
                weight[2] = after(weight[2], total)

        split = [weight[2][p * height : (p + 1) * height] for p in range(parts)] if ring == 4 else []
        last = []
        if split:
            last.append(onward(after(split[0], *came)))
        owned_rows, message = call(
            functools.partial(square_kernel, len(came), lines),
            "square",
            [((owned, outs), f32), ((1, lines + 16, outs), bf16)],
            [total] + came,
        )
        block = multiply(2, weight[2], swap(weight[2], 1), gate=owned_rows)
        messages = after(message, last[0], block) if split else message
        for bit, radix in reversed(rounds):
            if bit >= members:
                came = [swap(messages, j * bit) for j in range(1, radix)]
                messages = jnp.concatenate([messages] + came, axis=0)
        for p in range(1, len(split)):
            last.append(onward(after(split[p], *came)))
        (square,) = call(gathered_kernel, "gathered", [((8, 128), f32)], [messages])
        if sides == 2:
            sent = give_back(2, block, gate=later)
            square = after(square, sent)
        squares = [square] + [swap(square, x) for x in range(1, members)]
        new_first, new_second, whole = call(
            functools.partial(moment_kernel, lay, rows),
            "moment",
            [((owned, outs), f32), ((owned, outs), f32), ((ring, owned, outs), bf16)],
            squares + basis + [owned_rows, first_moment, second_moment, messages],
        )
        blocks = []
        if split:
            block = multiply(3, last[0], swap(last[0], 1), 0, squares[0])
            sent = give_back(3, after(block, *squares), 0)

        for bit, radix in reversed(rounds[1:]):
            if bit < members:
                whole = after(whole, sent)
                whole = jnp.concatenate(
                    [whole] + [swap(whole, j * bit) for j in range(1, radix)], axis=0
                )
        (new_master,) = call(
            functools.partial(back_kernel, lay, owned),
            "back",
            [(master_weight.shape, f32)],
            [proj_basis, whole, swap(whole, 1), master_weight],
            scratch=[pltpu.VMEM((rank, outs), f32)],
            flops=2 * rows * rank * outs,
            moved=8 * 2**20,
        )

        for p in range(1, len(split)):
            give_back(3, multiply(3, last[p], swap(last[p], 1), p * height), p * height)
        if not split:
            for s in range(3, ring):
                weight.append(onward(weight[s - 1]))
                give_back(s, multiply(s, weight[s], swap(weight[s], 1)))
        activation_grad = state["out"]
        if waiting:
            (activation_grad,) = call(
                functools.partial(last_kernel, lay, rows, [spot for spot, block in waiting]),
                "last",
                [((tokens, width), bf16)],
                [after(block, new_master) for spot, block in waiting] + [activation_grad],
                [VMEM] * len(waiting) + [HBM],
                [HBM],
                scratch=[pltpu.SemaphoreType.DMA((len(waiting), 2))],
                input_output_aliases={len(waiting): 0},
            )
        return (activation_grad, new_master, new_first, new_second)

    return per_device


def solution(mesh):
    spec = P(("groups", "dp"), None)
    return jax.shard_map(
        make_per_device(mesh.shape["dp"]),
        mesh=mesh,
        in_specs=(spec,) * 6,
        out_specs=(spec,) * 4,
        check_vma=False,
    )
```

```python
import functools
import jax
import jax.numpy as jnp
from jax import lax
from jax.experimental import pallas as pl
from jax.experimental.pallas import tpu as pltpu
from jax.sharding import PartitionSpec as P

clip_total = 512.0
step_size = 0.01
first_fix = 1.0 - 0.9**10
second_fix = 1.0 - 0.99**10

f32 = jnp.float32
bf16 = jnp.bfloat16
HBM = pl.BlockSpec(memory_space=pl.ANY)
VMEM = pl.BlockSpec(memory_space=pltpu.VMEM)
PARAMS = pltpu.CompilerParams(vmem_limit_bytes=40 * 2**20)


def after(value, *others):
    return lax.optimization_barrier((value,) + others)[0]


class Layout:
    def __init__(self, n):
        self.n = n
        self.sides = 2 if n == 16 else 1
        self.members = 2 * self.sides
        self.ring = n // self.members
        ring, members = self.ring, self.members
        order = [0, 1, 3, 2] if ring == 4 else list(range(ring))
        self.forward = [
            (order[k] * members + m, order[(k + 1) % ring] * members + m)
            for k in range(ring)
            for m in range(members)
        ]
        self.rounds = [(1, 2)]
        bit = 2
        if self.sides == 2:
            self.rounds.append((2, 2))
            bit = 4
        while bit < n:
            radix = 4 if 2 * bit < n else 2
            self.rounds.append((bit, radix))
            bit *= radix

    def swap(self, value, bit):
        return lax.ppermute(value, "dp", [(i, i ^ bit) for i in range(self.n)])

    def onward(self, value):
        return lax.ppermute(value, "dp", self.forward)

    def source(self, index, s):
        z = index // self.members
        if self.ring != 4:
            return (z - s + self.ring) % self.ring
        k = (z + z // 2 * (5 - 2 * z) - s + 4) % 4
        return k + k // 2 * (5 - 2 * k)


def flip(value, bit):
    return value + bit - 2 * bit * ((value // bit) % 2)


def cut_kernel(lay, rows, plan, act, key_grad, *refs):
    pieces, sems = refs[:-1], refs[-1]
    index = lax.axis_index("dp")
    member = index % lay.members
    copies = []
    for (x, first, count), piece in zip(plan, pieces):
        owner = member
        for bit in (1, 2):
            if x & bit:
                owner = flip(owner, bit)
        for s in range(first, first + count):
            start = pl.multiple_of((lay.source(index, s) * lay.members + owner) * rows, rows)
            copies.append(
                pltpu.make_async_copy(
                    act.at[:, pl.ds(start, rows)],
                    piece.at[:, pl.ds((s - first) * rows, rows)],
                    sems.at[len(copies)],
                )
            )
    if lay.sides == 2:
        copies.append(
            pltpu.make_async_copy(
                key_grad,
                pieces[2].at[:, pl.ds(lay.ring * rows, key_grad.shape[1])],
                sems.at[len(copies)],
            )
        )
    for copy in copies:
        copy.start()
    for copy in copies:
        copy.wait()


def project_kernel(lay, owned, plan, *refs):
    members, ring = lay.members, lay.ring
    acts, refs = refs[: len(plan)], refs[len(plan) :]
    basis, refs = refs[:ring], refs[ring:]
    grads, refs = refs[:members], refs[members:]
    kept, given, grad = refs
    rows = acts[0].shape[1] // ring
    core = lax.axis_index("dp") % 2
    for x in range(members):
        total = None
        for (x_, first, count), piece in zip(plan, acts):
            if x_ != x:
                continue
            for s in range(first, first + count):
                term = jnp.dot(
                    piece[:, (s - first) * rows : (s - first + 1) * rows],
                    basis[s][:rows, :],
                    preferred_element_type=f32,
                )
                total = term if total is None else total + term
        term = lax.dot_general(
            total.astype(bf16),
            grads[x][...],
            (((0,), (0,)), ((), ())),
            preferred_element_type=f32,
        )
        if x == 0:
            grad[...] = term
        else:
            grad[...] += term
    for i in range(lay.n // 2):
        kept[i] = grad[pl.ds(pl.multiple_of((2 * i + core) * owned, owned), owned), :]
        given[i] = grad[pl.ds(pl.multiple_of((2 * i + 1 - core) * owned, owned), owned), :].astype(bf16)


def fold_kernel(bit, radix, came, *refs):
    kept, arrived, outs = refs[0], refs[1 : 1 + came], refs[1 + came :]
    digit = (lax.axis_index("dp") // bit) % radix

    def block(i):
        total = kept[i]
        for piece in arrived:
            total = total + piece[i].astype(f32)
        return total

    for i in range(kept.shape[0] // radix):
        for j in range(radix):
            other = digit
            for b in (1, 2):
                if j & b:
                    other = flip(other, b)
            value = block(i * radix + other)
            outs[j][i] = value.astype(outs[j].dtype)


def square_kernel(came, lines, *refs):
    kept, arrived, (owned, message) = refs[0], refs[1 : 1 + came], refs[1 + came :]
    total = kept[0]
    for piece in arrived:
        total = total + piece[0].astype(f32)
    owned[...] = total
    count = total.shape[0]
    square = jnp.full((16, total.shape[1]), jnp.sum(total * total), f32)
    first = square.astype(bf16).astype(f32)
    second = (square - first).astype(bf16).astype(f32)
    third = square - first - second
    row = lax.broadcasted_iota(jnp.int32, square.shape, 0)
    terms = jnp.where(row == 0, first, jnp.where(row == 1, second, jnp.where(row == 2, third, 0.0)))
    if count < lines:
        total = jnp.concatenate([total, jnp.zeros((lines - count, total.shape[1]), f32)], axis=0)
    message[0, :lines, :] = total.astype(bf16)
    message[0, lines:, :] = terms.astype(bf16)


def gathered_kernel(messages, square):
    lines = messages.shape[1] - 16
    total = jnp.zeros((16, 128), f32)
    for j in range(messages.shape[0]):
        total = total + messages[j, lines:, 0:128].astype(f32)
    square[...] = jnp.full(square.shape, jnp.sum(total[:, 0:1]), f32)


def moment_kernel(lay, rows, *refs):
    squares, refs = refs[: lay.members], refs[lay.members :]
    basis, refs = refs[: lay.ring], refs[lay.ring :]
    owned, first, second, messages, new_first, new_second, update = refs
    total = squares[0][...]
    for square in squares[1:]:
        total = total + square[...]
    factor = jnp.minimum(1.0, clip_total / (jnp.sqrt(total) + 1e-06))[0:1, 0:1]

    def advance(gradient, one, two):
        clipped = gradient * factor
        one = 0.9 * one + 0.1 * clipped
        two = 0.99 * two + 0.01 * clipped * clipped
        return one, two

    one, two = advance(owned[...], first[...], second[...])
    new_first[...] = one
    new_second[...] = two
    count = owned.shape[0]
    half = owned.shape[1] // 2
    index = lax.axis_index("dp")
    for s in range(lay.ring):
        xor = lax.bitwise_xor(lay.source(index, s), index // lay.members)
        slot = place_slot(lay, xor)
        for k in range(2):
            low = rows + k * 2 * count
            moments = basis[s][low : low + 2 * count, :].astype(f32)
            gradient = messages[slot, :, k * half : (k + 1) * half].astype(f32)[:count]
            one, two = advance(gradient, moments[:count], moments[count:])
            update[slot, :, k * half : (k + 1) * half] = (
                one / first_fix / (jnp.sqrt(two / second_fix) + 1e-08)
            ).astype(bf16)


def place_slot(lay, xor):
    slot, scale = 0, 1
    for bit, radix in reversed(lay.rounds):
        if bit >= lay.members:
            slot = slot + scale * ((xor // (bit // lay.members)) % radix)
            scale *= radix
    return slot


def place(lay, s, side, low, width, rows, source, out, sems):
    index = lax.axis_index("dp")
    core = index % 2
    chip = lay.source(index, s) * lay.sides + side
    copies = []
    for k, owner in enumerate((core, 1 - core)):
        start = pl.multiple_of((chip * 2 + owner) * rows + low, width)
        copies.append(
            pltpu.make_async_copy(
                source.at[:, pl.ds(k * width, width)],
                out.at[:, pl.ds(start, width)],
                sems.at[k],
            )
        )
    return copies


def weight_kernel(lay, rows, s, low, parts, came, first, *refs):
    sides = lay.sides
    mine, refs = refs[:parts], refs[parts:]
    theirs, refs = refs[:parts], refs[parts:]
    grads, refs = refs[:sides], refs[sides:]
    if came is not None:
        arrived, refs = refs[0], refs[1:]
    if not first:
        refs = refs[1:]
    out, refs = refs[0], refs[1:]
    if sides == 2:
        far, refs = refs[0], refs[1:]
    own, sems, came_sems = refs
    height = mine[0].shape[0]
    width = parts * height
    side = (lax.axis_index("dp") // 2) % sides
    copies = []
    if came is not None:
        copies = place(
            lay, came[0], 1 - side, came[1], arrived.shape[1] // 2, rows, arrived, out, came_sems
        )
        for copy in copies:
            copy.start()
    for x in reversed(range(sides)):
        target = own if x == 0 else far
        for k, group in enumerate((mine, theirs)):
            for p, piece in enumerate(group):
                target[:, k * width + p * height : k * width + (p + 1) * height] = lax.dot_general(
                    grads[x][...],
                    piece[...],
                    (((1,), (1,)), ((), ())),
                    preferred_element_type=f32,
                ).astype(bf16)
    owns = place(lay, s, side, low, width, rows, own, out, sems)
    for copy in owns:
        copy.start()
    for copy in owns + copies:
        copy.wait()


def last_kernel(lay, rows, blocks, *refs):
    arrived, (before, out, sems) = refs[: len(blocks)], refs[len(blocks) :]
    side = (lax.axis_index("dp") // 2) % lay.sides
    copies = []
    for k, (s, low) in enumerate(blocks):
        wide = arrived[k].shape[1] // 2
        copies += place(lay, s, 1 - side, low, wide, rows, arrived[k], out, sems.at[k])
    for copy in copies:
        copy.start()
    for copy in copies:
        copy.wait()


def back_kernel(lay, owned, basis, near, other, master, out, update):
    index = lax.axis_index("dp")
    half = lay.n // 2
    for j in range(lay.n):
        owner = index
        for bit in [1 << b for b in range(lay.n.bit_length() - 1)]:
            if slot_to_xor(lay, j) & bit:
                owner = flip(owner, bit)
        piece = near[j] if j < half else other[j - half]
        update[pl.ds(pl.multiple_of(owner * owned, owned), owned), :] = piece.astype(f32)
    out[...] = master[...] - step_size * jnp.dot(
        basis[...], update[...].astype(bf16), preferred_element_type=f32
    )


def slot_to_xor(lay, j):
    xor = 0
    for bit, radix in reversed(lay.rounds):
        xor += (j % radix) * bit
        j //= radix
    return xor


def call(kernel, name, shapes, args, in_specs=None, out_specs=None, scratch=(), flops=0, moved=2**20, **more):
    return pl.pallas_call(
        kernel,
        name=name,
        out_shape=[jax.ShapeDtypeStruct(shape, dtype) for shape, dtype in shapes],
        in_specs=in_specs or [VMEM] * len(args),
        out_specs=out_specs or [VMEM] * len(shapes),
        scratch_shapes=list(scratch),
        compiler_params=PARAMS,
        cost_estimate=pl.CostEstimate(flops=flops, bytes_accessed=moved, transcendentals=0),
        **more,
    )(*args)


def make_per_device(n):
    lay = Layout(n)
    sides, members, ring, rounds = lay.sides, lay.members, lay.ring, lay.rounds
    swap, onward = lay.swap, lay.onward

    def per_device(activations, key_grad, proj_basis, master_weight, first_moment, second_moment):
        tokens, width = activations.shape
        rows, rank = proj_basis.shape
        outs = key_grad.shape[1]
        owned = rank // n
        lines = -(-owned // 16) * 16
        parts = 2 if rows % 256 == 0 else 1
        height = rows // parts

        plan = [(x, 0, ring) for x in range(members)]
        wides = [ring * rows + (outs if x == 2 else 0) for x in range(members)]
        cut = call(
            functools.partial(cut_kernel, lay, rows, plan),
            "cut",
            [((tokens, wide), bf16) for wide in wides],
            [activations, key_grad],
            in_specs=[HBM, HBM],
            scratch=[pltpu.SemaphoreType.DMA((members * ring + 1,))],
            moved=4 * tokens * ring * rows * members,
        )

        acts = [cut[0]] + [swap(cut[x], x) for x in range(1, members)]
        moments = jnp.concatenate([first_moment, second_moment], axis=0).astype(bf16)
        folded = [moments[:, k * rank : (k + 1) * rank] for k in range(outs // rank)]
        basis = [jnp.concatenate([proj_basis] + folded, axis=0)]
        for s in range(1, ring):
            basis.append(onward(basis[-1]))
        whole_weight = master_weight.astype(bf16)
        next_weight = onward(after(whole_weight, basis[-1]))

        if sides == 2:
            far_grad = acts[2][:, ring * rows :]
            near = swap(jnp.concatenate([key_grad, far_grad], axis=0), 1)
            grads = [key_grad, near[:tokens], far_grad, near[tokens:]]
        else:
            near = swap(key_grad, 1)
            grads = [key_grad, near]
        their_weight = swap(after(whole_weight, basis[1]), 1)

        side_grads = [key_grad, far_grad] if sides == 2 else [key_grad]
        state = {"out": None}
        waiting = []

        def multiply(s, mine, theirs, low=0, gate=None):
            if gate is not None:
                mine = [after(mine[0], gate)] + mine[1:]
            args = mine + theirs + side_grads
            in_specs = [VMEM] * len(args)
            wide = sum(piece.shape[0] for piece in mine)
            came = None
            if len(waiting) > 1:
                (came, block) = waiting.pop(0)
                args.append(block)
                in_specs.append(VMEM)
            first = state["out"] is None
            if not first:
                args.append(state["out"])
                in_specs.append(HBM)
            shapes, out_specs = [((tokens, width), bf16)], [HBM]
            if sides == 2:
                shapes.append(((tokens, 2 * wide), bf16))
                out_specs.append(VMEM)
            result = call(
                functools.partial(weight_kernel, lay, rows, s, low, len(mine), came, first),
                "weight",
                shapes,
                args,
                in_specs,
                out_specs,
                scratch=[
                    pltpu.VMEM((tokens, 2 * wide), bf16),
                    pltpu.SemaphoreType.DMA((2,)),
                    pltpu.SemaphoreType.DMA((2,)),
                ],
                flops=4 * sides * tokens * wide * outs,
                moved=6 * 2**20,
                input_output_aliases={} if first else {len(args) - 1: 0},
            )
            state["out"] = result[0]
            return result[1] if sides == 2 else result[0]

        def give_back(s, block, low=0, gate=None):
            if sides == 1:
                return block
            waiting.append(((s, low), swap(block if gate is None else after(block, gate), 2)))
            return waiting[-1][1]

        def core_swap(pieces):
            return [swap(piece, 1) for piece in pieces]

        first_block = multiply(0, [whole_weight], [their_weight])

        total, *gives = call(
            functools.partial(project_kernel, lay, owned, plan),
            "project",
            [((n // 2, owned, outs), f32), ((n // 2, owned, outs), bf16)],
            [after(acts[0], first_block)] + acts[1:] + basis + grads,
            scratch=[pltpu.VMEM((rank, outs), f32)],
            flops=2 * tokens * members * rank * (ring * rows + outs),
            moved=12 * 2**20,
        )
        for k, (bit, radix) in enumerate(rounds):
            if bit == members:
                gives = [after(give, weight[2][0]) for give in gives]
            came = [swap(give, j * bit) for j, give in zip(range(1, radix), gives)]
            if k == len(rounds) - 1:
                break
            next_bit, next_radix = rounds[k + 1]
            shape = (total.shape[0] // next_radix, owned, outs)
            total, *gives = call(
                functools.partial(fold_kernel, next_bit, next_radix, len(came)),
                "fold",
                [(shape, f32)] + [(shape, bf16)] * (next_radix - 1),
                [total] + came,
                moved=4 * total.size,
            )
            if bit == 1:
                next_weight = after(next_weight, total)
                weight = [None, [next_weight[p * height : (p + 1) * height] for p in range(parts)]]
                weight.append([onward(weight[1][0])])
                block = multiply(1, [next_weight], core_swap([next_weight]))
            if bit == 2 and sides == 2:
                both = jnp.concatenate([first_block, block], axis=1)
                sent = swap(after(both, total), 2)
                waiting.append(((0, 0), sent[:, : 2 * rows]))
                waiting.append(((1, 0), sent[:, 2 * rows :]))
        if sides == 1:
            sent = block
        for p in range(1, parts):
            weight[2].append(onward(after(weight[1][p], *came)))
        if ring == 4:
            weight.append([onward(after(weight[2][0], *came))])
        owned_rows, message = call(
            functools.partial(square_kernel, len(came), lines),
            "square",
            [((owned, outs), f32), ((1, lines + 16, outs), bf16)],
            [after(total, sent)] + came,
        )

        their_half = swap(weight[2][0], 1)
        messages = after(message, weight[3][0]) if ring == 4 else message
        for bit, radix in reversed(rounds):
            if bit >= members:
                came = [swap(messages, j * bit) for j in range(1, radix)]
                messages = jnp.concatenate([messages] + came, axis=0)
        if ring == 4:
            for p in range(1, parts):
                weight[3].append(onward(after(weight[2][p], *came)))
        (square,) = call(gathered_kernel, "gathered", [((8, 128), f32)], [messages])
        block = multiply(2, weight[2][:1], [their_half], 0, owned_rows)
        sent = give_back(2, block, 0)
        for p in range(1, parts):
            block = multiply(2, weight[2][p:], core_swap(weight[2][p:]), p * height, owned_rows)
            sent = give_back(2, block, p * height)
        square = after(square, sent)
        squares = [square] + [swap(square, x) for x in range(1, members)]
        new_first, new_second, whole = call(
            functools.partial(moment_kernel, lay, rows),
            "moment",
            [((owned, outs), f32), ((owned, outs), f32), ((ring, owned, outs), bf16)],
            squares + basis + [owned_rows, first_moment, second_moment, messages],
        )
        if ring == 4:
            pieces = weight[3][:1]
            block = multiply(3, pieces, core_swap(pieces))
            sent = give_back(3, block)

        for bit, radix in reversed(rounds[1:]):
            if bit < members:
                whole = after(whole, sent)
                whole = jnp.concatenate(
                    [whole] + [swap(whole, j * bit) for j in range(1, radix)], axis=0
                )
        (new_master,) = call(
            functools.partial(back_kernel, lay, owned),
            "back",
            [(master_weight.shape, f32)],
            [proj_basis, whole, swap(whole, 1), master_weight],
            scratch=[pltpu.VMEM((rank, outs), f32)],
            flops=2 * rows * rank * outs,
            moved=8 * 2**20,
        )

        for s in range(3, ring):
            if len(weight) <= s:
                weight.append([onward(piece) for piece in weight[s - 1]])
            for p in range(1 if ring == 4 else 0, parts):
                pieces = weight[s][p : p + 1]
                give_back(s, multiply(s, pieces, core_swap(pieces), p * height), p * height)
        activation_grad = state["out"]
        if waiting:
            (activation_grad,) = call(
                functools.partial(last_kernel, lay, rows, [spot for spot, block in waiting]),
                "last",
                [((tokens, width), bf16)],
                [after(block, new_master) for spot, block in waiting] + [activation_grad],
                [VMEM] * len(waiting) + [HBM],
                [HBM],
                scratch=[pltpu.SemaphoreType.DMA((len(waiting), 2))],
                input_output_aliases={len(waiting): 0},
            )
        return (activation_grad, new_master, new_first, new_second)

    return per_device


def solution(mesh):
    spec = P(("groups", "dp"), None)
    return jax.shard_map(
        make_per_device(mesh.shape["dp"]),
        mesh=mesh,
        in_specs=(spec,) * 6,
        out_specs=(spec,) * 4,
        check_vma=False,
    )
```

```python
import functools
import jax
import jax.numpy as jnp
from jax import lax
from jax.experimental import pallas as pl
from jax.experimental.pallas import tpu as pltpu
from jax.sharding import PartitionSpec as P

clip_total = 512.0
step_size = 0.01
first_fix = 1.0 - 0.9**10
second_fix = 1.0 - 0.99**10

f32 = jnp.float32
bf16 = jnp.bfloat16
HBM = pl.BlockSpec(memory_space=pl.ANY)
VMEM = pl.BlockSpec(memory_space=pltpu.VMEM)
PARAMS = pltpu.CompilerParams(vmem_limit_bytes=40 * 2**20)


def after(value, *others):
    return lax.optimization_barrier((value,) + others)[0]


class Layout:
    def __init__(self, n):
        self.n = n
        self.sides = 2 if n == 16 else 1
        self.members = 2 * self.sides
        self.ring = n // self.members
        ring, members = self.ring, self.members
        order = [0, 1, 3, 2] if ring == 4 else list(range(ring))
        self.forward = [
            (order[k] * members + m, order[(k + 1) % ring] * members + m)
            for k in range(ring)
            for m in range(members)
        ]
        self.rounds = [(1, 2)]
        bit = 2
        if self.sides == 2:
            self.rounds.append((2, 2))
            bit = 4
        while bit < n:
            radix = 4 if 2 * bit < n else 2
            self.rounds.append((bit, radix))
            bit *= radix

    def swap(self, value, bit):
        return lax.ppermute(value, "dp", [(i, i ^ bit) for i in range(self.n)])

    def onward(self, value):
        return lax.ppermute(value, "dp", self.forward)

    def source(self, index, s):
        z = index // self.members
        if self.ring != 4:
            return (z - s + self.ring) % self.ring
        k = (z + z // 2 * (5 - 2 * z) - s + 4) % 4
        return k + k // 2 * (5 - 2 * k)


def flip(value, bit):
    return value + bit - 2 * bit * ((value // bit) % 2)


def cut_kernel(lay, rows, plan, act, key_grad, *refs):
    pieces, sems = refs[:-1], refs[-1]
    index = lax.axis_index("dp")
    member = index % lay.members
    copies = []
    for (x, first, count), piece in zip(plan, pieces):
        owner = member
        for bit in (1, 2):
            if x & bit:
                owner = flip(owner, bit)
        for s in range(first, first + count):
            start = pl.multiple_of((lay.source(index, s) * lay.members + owner) * rows, rows)
            copies.append(
                pltpu.make_async_copy(
                    act.at[:, pl.ds(start, rows)],
                    piece.at[:, pl.ds((s - first) * rows, rows)],
                    sems.at[len(copies)],
                )
            )
    if lay.sides == 2:
        copies.append(
            pltpu.make_async_copy(
                key_grad,
                pieces[2].at[:, pl.ds(lay.ring * rows, key_grad.shape[1])],
                sems.at[len(copies)],
            )
        )
    for copy in copies:
        copy.start()
    for copy in copies:
        copy.wait()


def project_kernel(lay, owned, plan, *refs):
    members, ring = lay.members, lay.ring
    acts, refs = refs[: len(plan)], refs[len(plan) :]
    basis, refs = refs[:ring], refs[ring:]
    grads, refs = refs[:members], refs[members:]
    kept, given, grad = refs
    rows = acts[0].shape[1] // ring
    core = lax.axis_index("dp") % 2
    for x in range(members):
        total = None
        for (x_, first, count), piece in zip(plan, acts):
            if x_ != x:
                continue
            for s in range(first, first + count):
                term = jnp.dot(
                    piece[:, (s - first) * rows : (s - first + 1) * rows],
                    basis[s][:rows, :],
                    preferred_element_type=f32,
                )
                total = term if total is None else total + term
        term = lax.dot_general(
            total.astype(bf16),
            grads[x][...],
            (((0,), (0,)), ((), ())),
            preferred_element_type=f32,
        )
        if x == 0:
            grad[...] = term
        else:
            grad[...] += term
    for i in range(lay.n // 2):
        kept[i] = grad[pl.ds(pl.multiple_of((2 * i + core) * owned, owned), owned), :]
        given[i] = grad[pl.ds(pl.multiple_of((2 * i + 1 - core) * owned, owned), owned), :].astype(bf16)


def fold_kernel(bit, radix, came, *refs):
    kept, arrived, outs = refs[0], refs[1 : 1 + came], refs[1 + came :]
    digit = (lax.axis_index("dp") // bit) % radix

    def block(i):
        total = kept[i]
        for piece in arrived:
            total = total + piece[i].astype(f32)
        return total

    for i in range(kept.shape[0] // radix):
        for j in range(radix):
            other = digit
            for b in (1, 2):
                if j & b:
                    other = flip(other, b)
            value = block(i * radix + other)
            outs[j][i] = value.astype(outs[j].dtype)


def square_kernel(came, lines, *refs):
    kept, arrived, (owned, message) = refs[0], refs[1 : 1 + came], refs[1 + came :]
    total = kept[0]
    for piece in arrived:
        total = total + piece[0].astype(f32)
    owned[...] = total
    count = total.shape[0]
    square = jnp.full((16, total.shape[1]), jnp.sum(total * total), f32)
    first = square.astype(bf16).astype(f32)
    second = (square - first).astype(bf16).astype(f32)
    third = square - first - second
    row = lax.broadcasted_iota(jnp.int32, square.shape, 0)
    terms = jnp.where(row == 0, first, jnp.where(row == 1, second, jnp.where(row == 2, third, 0.0)))
    if count < lines:
        total = jnp.concatenate([total, jnp.zeros((lines - count, total.shape[1]), f32)], axis=0)
    message[0, :lines, :] = total.astype(bf16)
    message[0, lines:, :] = terms.astype(bf16)


def gathered_kernel(messages, square):
    lines = messages.shape[1] - 16
    total = jnp.zeros((16, 128), f32)
    for j in range(messages.shape[0]):
        total = total + messages[j, lines:, 0:128].astype(f32)
    square[...] = jnp.full(square.shape, jnp.sum(total[:, 0:1]), f32)


def moment_kernel(lay, rows, *refs):
    squares, refs = refs[: lay.members], refs[lay.members :]
    basis, refs = refs[: lay.ring], refs[lay.ring :]
    owned, first, second, messages, new_first, new_second, update = refs
    total = squares[0][...]
    for square in squares[1:]:
        total = total + square[...]
    factor = jnp.minimum(1.0, clip_total / (jnp.sqrt(total) + 1e-06))[0:1, 0:1]

    def advance(gradient, one, two):
        clipped = gradient * factor
        one = 0.9 * one + 0.1 * clipped
        two = 0.99 * two + 0.01 * clipped * clipped
        return one, two

    one, two = advance(owned[...], first[...], second[...])
    new_first[...] = one
    new_second[...] = two
    count = owned.shape[0]
    half = owned.shape[1] // 2
    index = lax.axis_index("dp")
    for s in range(lay.ring):
        xor = lax.bitwise_xor(lay.source(index, s), index // lay.members)
        slot = place_slot(lay, xor)
        for k in range(2):
            low = rows + k * 2 * count
            moments = basis[s][low : low + 2 * count, :].astype(f32)
            gradient = messages[slot, :, k * half : (k + 1) * half].astype(f32)[:count]
            one, two = advance(gradient, moments[:count], moments[count:])
            update[slot, :, k * half : (k + 1) * half] = (
                one / first_fix / (jnp.sqrt(two / second_fix) + 1e-08)
            ).astype(bf16)


def place_slot(lay, xor):
    slot, scale = 0, 1
    for bit, radix in reversed(lay.rounds):
        if bit >= lay.members:
            slot = slot + scale * ((xor // (bit // lay.members)) % radix)
            scale *= radix
    return slot


def place(lay, s, side, low, width, rows, source, out, sems):
    index = lax.axis_index("dp")
    core = index % 2
    chip = lay.source(index, s) * lay.sides + side
    copies = []
    for k, owner in enumerate((core, 1 - core)):
        start = pl.multiple_of((chip * 2 + owner) * rows + low, width)
        copies.append(
            pltpu.make_async_copy(
                source.at[:, pl.ds(k * width, width)],
                out.at[:, pl.ds(start, width)],
                sems.at[k],
            )
        )
    return copies


def weight_kernel(lay, rows, s, low, parts, came, first, *refs):
    sides = lay.sides
    mine, refs = refs[:parts], refs[parts:]
    theirs, refs = refs[:parts], refs[parts:]
    grads, refs = refs[:sides], refs[sides:]
    if came is not None:
        arrived, refs = refs[0], refs[1:]
    if not first:
        refs = refs[1:]
    out, refs = refs[0], refs[1:]
    if sides == 2:
        far, refs = refs[0], refs[1:]
    own, sems, came_sems = refs
    height = mine[0].shape[0]
    width = parts * height
    side = (lax.axis_index("dp") // 2) % sides
    copies = []
    if came is not None:
        copies = place(
            lay, came[0], 1 - side, came[1], arrived.shape[1] // 2, rows, arrived, out, came_sems
        )
        for copy in copies:
            copy.start()
    for x in reversed(range(sides)):
        target = own if x == 0 else far
        for k, group in enumerate((mine, theirs)):
            for p, piece in enumerate(group):
                target[:, k * width + p * height : k * width + (p + 1) * height] = lax.dot_general(
                    grads[x][...],
                    piece[...],
                    (((1,), (1,)), ((), ())),
                    preferred_element_type=f32,
                ).astype(bf16)
    owns = place(lay, s, side, low, width, rows, own, out, sems)
    for copy in owns:
        copy.start()
    for copy in owns + copies:
        copy.wait()


def last_kernel(lay, rows, blocks, *refs):
    arrived, (before, out, sems) = refs[: len(blocks)], refs[len(blocks) :]
    side = (lax.axis_index("dp") // 2) % lay.sides
    copies = []
    for k, (s, low) in enumerate(blocks):
        wide = arrived[k].shape[1] // 2
        copies += place(lay, s, 1 - side, low, wide, rows, arrived[k], out, sems.at[k])
    for copy in copies:
        copy.start()
    for copy in copies:
        copy.wait()


def back_kernel(lay, owned, basis, near, other, master, out, update):
    index = lax.axis_index("dp")
    half = lay.n // 2
    for j in range(lay.n):
        owner = index
        for bit in [1 << b for b in range(lay.n.bit_length() - 1)]:
            if slot_to_xor(lay, j) & bit:
                owner = flip(owner, bit)
        piece = near[j] if j < half else other[j - half]
        update[pl.ds(pl.multiple_of(owner * owned, owned), owned), :] = piece.astype(f32)
    out[...] = master[...] - step_size * jnp.dot(
        basis[...], update[...].astype(bf16), preferred_element_type=f32
    )


def slot_to_xor(lay, j):
    xor = 0
    for bit, radix in reversed(lay.rounds):
        xor += (j % radix) * bit
        j //= radix
    return xor


def call(kernel, name, shapes, args, in_specs=None, out_specs=None, scratch=(), flops=0, moved=2**20, **more):
    return pl.pallas_call(
        kernel,
        name=name,
        out_shape=[jax.ShapeDtypeStruct(shape, dtype) for shape, dtype in shapes],
        in_specs=in_specs or [VMEM] * len(args),
        out_specs=out_specs or [VMEM] * len(shapes),
        scratch_shapes=list(scratch),
        compiler_params=PARAMS,
        cost_estimate=pl.CostEstimate(flops=flops, bytes_accessed=moved, transcendentals=0),
        **more,
    )(*args)


def make_per_device(n):
    lay = Layout(n)
    sides, members, ring, rounds = lay.sides, lay.members, lay.ring, lay.rounds
    swap, onward = lay.swap, lay.onward

    def per_device(activations, key_grad, proj_basis, master_weight, first_moment, second_moment):
        tokens, width = activations.shape
        rows, rank = proj_basis.shape
        outs = key_grad.shape[1]
        owned = rank // n
        lines = -(-owned // 16) * 16
        parts = 2 if rows % 256 == 0 else 1
        height = rows // parts

        plan = [(x, 0, ring) for x in range(members)]
        wides = [ring * rows + (outs if x == 2 else 0) for x in range(members)]
        cut = call(
            functools.partial(cut_kernel, lay, rows, plan),
            "cut",
            [((tokens, wide), bf16) for wide in wides],
            [activations, key_grad],
            in_specs=[HBM, HBM],
            scratch=[pltpu.SemaphoreType.DMA((members * ring + 1,))],
            moved=4 * tokens * ring * rows * members,
        )

        acts = [cut[0]] + [swap(cut[x], x) for x in range(1, members)]
        moments = jnp.concatenate([first_moment, second_moment], axis=0).astype(bf16)
        folded = [moments[:, k * rank : (k + 1) * rank] for k in range(outs // rank)]
        basis = [after(jnp.concatenate([proj_basis] + folded, axis=0), cut[0])]
        for s in range(1, ring):
            basis.append(onward(basis[-1]))
        weight = [master_weight.astype(bf16)]
        weight.append(onward(after(weight[0], basis[-1])))

        if sides == 2:
            far_grad = acts[2][:, ring * rows :]
            near = swap(jnp.concatenate([key_grad, far_grad], axis=0), 1)
            grads = [key_grad, near[:tokens], far_grad, near[tokens:]]
        else:
            near = swap(key_grad, 1)
            grads = [key_grad, near]
        theirs = [swap(after(weight[0], basis[1]), 1)]

        side_grads = [key_grad, far_grad] if sides == 2 else [key_grad]
        state = {"out": None}
        waiting = []

        def multiply(s, mine, theirs, low=0, gate=None):
            args = [mine if gate is None else after(mine, gate), theirs] + side_grads
            in_specs = [VMEM] * len(args)
            wide = mine.shape[0]
            came = None
            if len(waiting) > 1:
                (came, block) = waiting.pop(0)
                args.append(block)
                in_specs.append(VMEM)
            first = state["out"] is None
            if not first:
                args.append(state["out"])
                in_specs.append(HBM)
            shapes, out_specs = [((tokens, width), bf16)], [HBM]
            if sides == 2:
                shapes.append(((tokens, 2 * wide), bf16))
                out_specs.append(VMEM)
            result = call(
                functools.partial(weight_kernel, lay, rows, s, low, 1, came, first),
                "weight",
                shapes,
                args,
                in_specs,
                out_specs,
                scratch=[
                    pltpu.VMEM((tokens, 2 * wide), bf16),
                    pltpu.SemaphoreType.DMA((2,)),
                    pltpu.SemaphoreType.DMA((2,)),
                ],
                flops=4 * sides * tokens * wide * outs,
                moved=6 * 2**20,
                input_output_aliases={} if first else {len(args) - 1: 0},
            )
            state["out"] = result[0]
            return result[1] if sides == 2 else result[0]

        def give_back(s, block, low=0, gate=None):
            if sides == 1:
                return block
            waiting.append(((s, low), swap(block if gate is None else after(block, gate), 2)))
            return waiting[-1][1]

        first_block = multiply(0, weight[0], theirs[0])
        total, *gives = call(
            functools.partial(project_kernel, lay, owned, plan),
            "project",
            [((n // 2, owned, outs), f32), ((n // 2, owned, outs), bf16)],
            [after(acts[0], first_block)] + acts[1:] + basis + grads,
            scratch=[pltpu.VMEM((rank, outs), f32)],
            flops=2 * tokens * members * rank * (ring * rows + outs),
            moved=12 * 2**20,
        )
        weight[1] = after(weight[1], total)
        weight.append(onward(weight[1]))
        theirs.append(swap(weight[1], 1))

        for k, (bit, radix) in enumerate(rounds):
            if bit == members:
                gives = [after(give, weight[2], block, sent if sides == 2 else block) for give in gives]
            came = [swap(give, j * bit) for j, give in zip(range(1, radix), gives)]
            if k == len(rounds) - 1:
                break
            next_bit, next_radix = rounds[k + 1]
            shape = (total.shape[0] // next_radix, owned, outs)
            total, *gives = call(
                functools.partial(fold_kernel, next_bit, next_radix, len(came)),
                "fold",
                [(shape, f32)] + [(shape, bf16)] * (next_radix - 1),
                [total] + came,
                moved=4 * total.size,
            )
            if bit == 1:
                block = multiply(1, weight[1], theirs[1], gate=total)
            if bit == 2:
                sent = give_back(0, first_block, gate=total)
                later = give_back(1, block, gate=total)
                weight[2] = after(weight[2], total, sent)

        owned_rows, message = call(
            functools.partial(square_kernel, len(came), lines),
            "square",
            [((owned, outs), f32), ((1, lines + 16, outs), bf16)],
            [total] + came,
        )
        their_step = swap(weight[2], 1)
        messages = message
        for bit, radix in reversed(rounds):
            if bit >= members:
                came = [swap(messages, j * bit) for j in range(1, radix)]
                messages = jnp.concatenate([messages] + came, axis=0)

        split = [weight[2][p * height : (p + 1) * height] for p in range(parts)] if ring == 4 else []
        last = [onward(after(piece, *came)) for piece in split[:1]]
        block = multiply(2, weight[2], their_step, gate=owned_rows)
        (square,) = call(gathered_kernel, "gathered", [((8, 128), f32)], [messages])
        if sides == 2:
            sent = give_back(2, block, gate=later)
            square = after(square, sent)
        squares = [square] + [swap(square, x) for x in range(1, members)]
        last += [onward(after(piece, square)) for piece in split[1:]]
        new_first, new_second, update = call(
            functools.partial(moment_kernel, lay, rows),
            "moment",
            [((owned, outs), f32), ((owned, outs), f32), ((ring, owned, outs), bf16)],
            squares + basis + [owned_rows, first_moment, second_moment, messages],
        )
        whole = update
        for bit, radix in reversed(rounds[1:]):
            if bit < members:
                whole = jnp.concatenate(
                    [whole] + [swap(whole, j * bit) for j in range(1, radix)], axis=0
                )
        (new_master,) = call(
            functools.partial(back_kernel, lay, owned),
            "back",
            [(master_weight.shape, f32)],
            [proj_basis, whole, swap(whole, 1), master_weight],
            scratch=[pltpu.VMEM((rank, outs), f32)],
            flops=2 * rows * rank * outs,
            moved=8 * 2**20,
        )

        for p in range(len(split)):
            piece = after(last[p], update if p == 0 else sent)
            block = multiply(3, piece, swap(piece, 1), p * height)
            sent = give_back(3, block, p * height)
        if not split:
            for s in range(3, ring):
                weight.append(onward(weight[s - 1]))
                give_back(s, multiply(s, weight[s], swap(weight[s], 1)))
        activation_grad = state["out"]
        if waiting:
            (activation_grad,) = call(
                functools.partial(last_kernel, lay, rows, [spot for spot, block in waiting]),
                "last",
                [((tokens, width), bf16)],
                [after(block, new_master) for spot, block in waiting] + [activation_grad],
                [VMEM] * len(waiting) + [HBM],
                [HBM],
                scratch=[pltpu.SemaphoreType.DMA((len(waiting), 2))],
                input_output_aliases={len(waiting): 0},
            )
        return (activation_grad, new_master, new_first, new_second)

    return per_device


def solution(mesh):
    spec = P(("groups", "dp"), None)
    return jax.shard_map(
        make_per_device(mesh.shape["dp"]),
        mesh=mesh,
        in_specs=(spec,) * 6,
        out_specs=(spec,) * 4,
        check_vma=False,
    )
```

```python
import functools
import jax
import jax.numpy as jnp
from jax import lax
from jax.experimental import pallas as pl
from jax.experimental.pallas import tpu as pltpu
from jax.sharding import PartitionSpec as P

clip_total = 512.0
step_size = 0.01
first_fix = 1.0 - 0.9**10
second_fix = 1.0 - 0.99**10

f32 = jnp.float32
bf16 = jnp.bfloat16
HBM = pl.BlockSpec(memory_space=pl.ANY)
VMEM = pl.BlockSpec(memory_space=pltpu.VMEM)
PARAMS = pltpu.CompilerParams(vmem_limit_bytes=40 * 2**20)


def after(value, *others):
    return lax.optimization_barrier((value,) + others)[0]


class Layout:
    def __init__(self, n):
        self.n = n
        self.sides = 2 if n == 16 else 1
        self.members = 2 * self.sides
        self.ring = n // self.members
        ring, members = self.ring, self.members
        order = [0, 1, 3, 2] if ring == 4 else list(range(ring))
        self.forward = [
            (order[k] * members + m, order[(k + 1) % ring] * members + m)
            for k in range(ring)
            for m in range(members)
        ]
        self.rounds = [(1, 2)]
        bit = 2
        if self.sides == 2:
            self.rounds.append((2, 2))
            bit = 4
        while bit < n:
            radix = 4 if 2 * bit < n else 2
            self.rounds.append((bit, radix))
            bit *= radix

    def swap(self, value, bit):
        return lax.ppermute(value, "dp", [(i, i ^ bit) for i in range(self.n)])

    def onward(self, value):
        return lax.ppermute(value, "dp", self.forward)

    def source(self, index, s):
        z = index // self.members
        if self.ring != 4:
            return (z - s + self.ring) % self.ring
        k = (z + z // 2 * (5 - 2 * z) - s + 4) % 4
        return k + k // 2 * (5 - 2 * k)


def flip(value, bit):
    return value + bit - 2 * bit * ((value // bit) % 2)


def cut_kernel(lay, rows, plan, act, key_grad, *refs):
    pieces, sems = refs[:-1], refs[-1]
    index = lax.axis_index("dp")
    member = index % lay.members
    copies = []
    for (x, first, count), piece in zip(plan, pieces):
        owner = member
        for bit in (1, 2):
            if x & bit:
                owner = flip(owner, bit)
        for s in range(first, first + count):
            start = pl.multiple_of((lay.source(index, s) * lay.members + owner) * rows, rows)
            copies.append(
                pltpu.make_async_copy(
                    act.at[:, pl.ds(start, rows)],
                    piece.at[:, pl.ds((s - first) * rows, rows)],
                    sems.at[len(copies)],
                )
            )
    if lay.sides == 2:
        copies.append(
            pltpu.make_async_copy(
                key_grad,
                pieces[2].at[:, pl.ds(lay.ring * rows, key_grad.shape[1])],
                sems.at[len(copies)],
            )
        )
    for copy in copies:
        copy.start()
    for copy in copies:
        copy.wait()


def project_kernel(lay, owned, plan, *refs):
    members, ring = lay.members, lay.ring
    acts, refs = refs[: len(plan)], refs[len(plan) :]
    basis, refs = refs[:ring], refs[ring:]
    grads, refs = refs[:members], refs[members:]
    kept, given, grad = refs
    rows = acts[0].shape[1] // ring
    core = lax.axis_index("dp") % 2
    for x in range(members):
        total = None
        for (x_, first, count), piece in zip(plan, acts):
            if x_ != x:
                continue
            for s in range(first, first + count):
                term = jnp.dot(
                    piece[:, (s - first) * rows : (s - first + 1) * rows],
                    basis[s][:rows, :],
                    preferred_element_type=f32,
                )
                total = term if total is None else total + term
        term = lax.dot_general(
            total.astype(bf16),
            grads[x][...],
            (((0,), (0,)), ((), ())),
            preferred_element_type=f32,
        )
        if x == 0:
            grad[...] = term
        else:
            grad[...] += term
    for i in range(lay.n // 2):
        kept[i] = grad[pl.ds(pl.multiple_of((2 * i + core) * owned, owned), owned), :]
        given[i] = grad[pl.ds(pl.multiple_of((2 * i + 1 - core) * owned, owned), owned), :].astype(bf16)


def fold_kernel(bit, radix, came, *refs):
    kept, arrived, outs = refs[0], refs[1 : 1 + came], refs[1 + came :]
    digit = (lax.axis_index("dp") // bit) % radix

    def block(i):
        total = kept[i]
        for piece in arrived:
            total = total + piece[i].astype(f32)
        return total

    for i in range(kept.shape[0] // radix):
        for j in range(radix):
            other = digit
            for b in (1, 2):
                if j & b:
                    other = flip(other, b)
            value = block(i * radix + other)
            outs[j][i] = value.astype(outs[j].dtype)


def square_kernel(came, lines, *refs):
    kept, arrived, (owned, message) = refs[0], refs[1 : 1 + came], refs[1 + came :]
    total = kept[0]
    for piece in arrived:
        total = total + piece[0].astype(f32)
    owned[...] = total
    count = total.shape[0]
    square = jnp.full((16, total.shape[1]), jnp.sum(total * total), f32)
    first = square.astype(bf16).astype(f32)
    second = (square - first).astype(bf16).astype(f32)
    third = square - first - second
    row = lax.broadcasted_iota(jnp.int32, square.shape, 0)
    terms = jnp.where(row == 0, first, jnp.where(row == 1, second, jnp.where(row == 2, third, 0.0)))
    if count < lines:
        total = jnp.concatenate([total, jnp.zeros((lines - count, total.shape[1]), f32)], axis=0)
    message[0, :lines, :] = total.astype(bf16)
    message[0, lines:, :] = terms.astype(bf16)


def gathered_kernel(messages, square):
    lines = messages.shape[1] - 16
    total = jnp.zeros((16, 128), f32)
    for j in range(messages.shape[0]):
        total = total + messages[j, lines:, 0:128].astype(f32)
    square[...] = jnp.full(square.shape, jnp.sum(total[:, 0:1]), f32)


def moment_kernel(lay, rows, *refs):
    squares, refs = refs[: lay.members], refs[lay.members :]
    basis, refs = refs[: lay.ring], refs[lay.ring :]
    owned, first, second, messages, new_first, new_second, update = refs
    total = squares[0][...]
    for square in squares[1:]:
        total = total + square[...]
    factor = jnp.minimum(1.0, clip_total / (jnp.sqrt(total) + 1e-06))[0:1, 0:1]

    def advance(gradient, one, two):
        clipped = gradient * factor
        one = 0.9 * one + 0.1 * clipped
        two = 0.99 * two + 0.01 * clipped * clipped
        return one, two

    one, two = advance(owned[...], first[...], second[...])
    new_first[...] = one
    new_second[...] = two
    count = owned.shape[0]
    half = owned.shape[1] // 2
    index = lax.axis_index("dp")
    for s in range(lay.ring):
        xor = lax.bitwise_xor(lay.source(index, s), index // lay.members)
        slot = place_slot(lay, xor)
        for k in range(2):
            low = rows + k * 2 * count
            moments = basis[s][low : low + 2 * count, :].astype(f32)
            gradient = messages[slot, :, k * half : (k + 1) * half].astype(f32)[:count]
            one, two = advance(gradient, moments[:count], moments[count:])
            update[slot, :, k * half : (k + 1) * half] = (
                one / first_fix / (jnp.sqrt(two / second_fix) + 1e-08)
            ).astype(bf16)


def place_slot(lay, xor):
    slot, scale = 0, 1
    for bit, radix in reversed(lay.rounds):
        if bit >= lay.members:
            slot = slot + scale * ((xor // (bit // lay.members)) % radix)
            scale *= radix
    return slot


def place(lay, s, side, low, width, rows, source, out, sems):
    index = lax.axis_index("dp")
    core = index % 2
    chip = lay.source(index, s) * lay.sides + side
    copies = []
    for k, owner in enumerate((core, 1 - core)):
        start = pl.multiple_of((chip * 2 + owner) * rows + low, width)
        copies.append(
            pltpu.make_async_copy(
                source.at[:, pl.ds(k * width, width)],
                out.at[:, pl.ds(start, width)],
                sems.at[k],
            )
        )
    return copies


def weight_kernel(lay, rows, s, low, parts, came, first, *refs):
    sides = lay.sides
    mine, refs = refs[:parts], refs[parts:]
    theirs, refs = refs[:parts], refs[parts:]
    grads, refs = refs[:sides], refs[sides:]
    if came is not None:
        arrived, refs = refs[0], refs[1:]
    if not first:
        refs = refs[1:]
    out, refs = refs[0], refs[1:]
    if sides == 2:
        far, refs = refs[0], refs[1:]
    own, sems, came_sems = refs
    height = mine[0].shape[0]
    width = parts * height
    side = (lax.axis_index("dp") // 2) % sides
    copies = []
    if came is not None:
        copies = place(
            lay, came[0], 1 - side, came[1], arrived.shape[1] // 2, rows, arrived, out, came_sems
        )
        for copy in copies:
            copy.start()
    for x in reversed(range(sides)):
        target = own if x == 0 else far
        for k, group in enumerate((mine, theirs)):
            for p, piece in enumerate(group):
                target[:, k * width + p * height : k * width + (p + 1) * height] = lax.dot_general(
                    grads[x][...],
                    piece[...],
                    (((1,), (1,)), ((), ())),
                    preferred_element_type=f32,
                ).astype(bf16)
    owns = place(lay, s, side, low, width, rows, own, out, sems)
    for copy in owns:
        copy.start()
    for copy in owns + copies:
        copy.wait()


def last_kernel(lay, rows, blocks, *refs):
    arrived, (before, out, sems) = refs[: len(blocks)], refs[len(blocks) :]
    side = (lax.axis_index("dp") // 2) % lay.sides
    copies = []
    for k, (s, low) in enumerate(blocks):
        wide = arrived[k].shape[1] // 2
        copies += place(lay, s, 1 - side, low, wide, rows, arrived[k], out, sems.at[k])
    for copy in copies:
        copy.start()
    for copy in copies:
        copy.wait()


def back_kernel(lay, owned, basis, near, other, master, out, update):
    index = lax.axis_index("dp")
    half = lay.n // 2
    for j in range(lay.n):
        owner = index
        for bit in [1 << b for b in range(lay.n.bit_length() - 1)]:
            if slot_to_xor(lay, j) & bit:
                owner = flip(owner, bit)
        piece = near[j] if j < half else other[j - half]
        update[pl.ds(pl.multiple_of(owner * owned, owned), owned), :] = piece.astype(f32)
    out[...] = master[...] - step_size * jnp.dot(
        basis[...], update[...].astype(bf16), preferred_element_type=f32
    )


def slot_to_xor(lay, j):
    xor = 0
    for bit, radix in reversed(lay.rounds):
        xor += (j % radix) * bit
        j //= radix
    return xor


def call(kernel, name, shapes, args, in_specs=None, out_specs=None, scratch=(), flops=0, moved=2**20, **more):
    return pl.pallas_call(
        kernel,
        name=name,
        out_shape=[jax.ShapeDtypeStruct(shape, dtype) for shape, dtype in shapes],
        in_specs=in_specs or [VMEM] * len(args),
        out_specs=out_specs or [VMEM] * len(shapes),
        scratch_shapes=list(scratch),
        compiler_params=PARAMS,
        cost_estimate=pl.CostEstimate(flops=flops, bytes_accessed=moved, transcendentals=0),
        **more,
    )(*args)


def make_per_device(n):
    lay = Layout(n)
    sides, members, ring, rounds = lay.sides, lay.members, lay.ring, lay.rounds
    swap, onward = lay.swap, lay.onward

    def per_device(activations, key_grad, proj_basis, master_weight, first_moment, second_moment):
        tokens, width = activations.shape
        rows, rank = proj_basis.shape
        outs = key_grad.shape[1]
        owned = rank // n
        lines = -(-owned // 16) * 16
        parts = 2 if rows % 256 == 0 else 1
        height = rows // parts

        plan = [(x, 0, ring) for x in range(members)]
        wides = [ring * rows + (outs if x == 2 else 0) for x in range(members)]
        cut = call(
            functools.partial(cut_kernel, lay, rows, plan),
            "cut",
            [((tokens, wide), bf16) for wide in wides],
            [activations, key_grad],
            in_specs=[HBM, HBM],
            scratch=[pltpu.SemaphoreType.DMA((members * ring + 1,))],
            moved=4 * tokens * ring * rows * members,
        )

        acts = [cut[0]] + [swap(cut[x], x) for x in range(1, members)]
        moments = jnp.concatenate([first_moment, second_moment], axis=0).astype(bf16)
        folded = [moments[:, k * rank : (k + 1) * rank] for k in range(outs // rank)]
        basis = [after(jnp.concatenate([proj_basis] + folded, axis=0), cut[0])]
        for s in range(1, ring):
            basis.append(onward(basis[-1]))
        weight = [master_weight.astype(bf16)]
        weight.append(onward(after(weight[0], basis[-1])))

        if sides == 2:
            far_grad = acts[2][:, ring * rows :]
            near = swap(jnp.concatenate([key_grad, far_grad], axis=0), 1)
            grads = [key_grad, near[:tokens], far_grad, near[tokens:]]
        else:
            near = swap(key_grad, 1)
            grads = [key_grad, near]
        theirs = [swap(after(weight[0], basis[1]), 1)]

        side_grads = [key_grad, far_grad] if sides == 2 else [key_grad]
        state = {"out": None}
        waiting = []

        def multiply(s, mine, theirs, low=0, gate=None):
            args = [mine if gate is None else after(mine, gate), theirs] + side_grads
            in_specs = [VMEM] * len(args)
            wide = mine.shape[0]
            came = None
            if len(waiting) > 1:
                (came, block) = waiting.pop(0)
                args.append(block)
                in_specs.append(VMEM)
            first = state["out"] is None
            if not first:
                args.append(state["out"])
                in_specs.append(HBM)
            shapes, out_specs = [((tokens, width), bf16)], [HBM]
            if sides == 2:
                shapes.append(((tokens, 2 * wide), bf16))
                out_specs.append(VMEM)
            result = call(
                functools.partial(weight_kernel, lay, rows, s, low, 1, came, first),
                "weight",
                shapes,
                args,
                in_specs,
                out_specs,
                scratch=[
                    pltpu.VMEM((tokens, 2 * wide), bf16),
                    pltpu.SemaphoreType.DMA((2,)),
                    pltpu.SemaphoreType.DMA((2,)),
                ],
                flops=4 * sides * tokens * wide * outs,
                moved=6 * 2**20,
                input_output_aliases={} if first else {len(args) - 1: 0},
            )
            state["out"] = result[0]
            return result[1] if sides == 2 else result[0]

        def give_back(s, block, low=0, gate=None):
            if sides == 1:
                return block
            waiting.append(((s, low), swap(block if gate is None else after(block, gate), 2)))
            return waiting[-1][1]

        first_block = multiply(0, weight[0], theirs[0])
        total, *gives = call(
            functools.partial(project_kernel, lay, owned, plan),
            "project",
            [((n // 2, owned, outs), f32), ((n // 2, owned, outs), bf16)],
            [after(acts[0], first_block)] + acts[1:] + basis + grads,
            scratch=[pltpu.VMEM((rank, outs), f32)],
            flops=2 * tokens * members * rank * (ring * rows + outs),
            moved=12 * 2**20,
        )
        weight.append(onward(weight[1]))
        theirs.append(swap(weight[1], 1))

        for k, (bit, radix) in enumerate(rounds):
            if bit == members:
                gives = [after(give, weight[2], sent if sides == 2 else block) for give in gives]
            came = [swap(give, j * bit) for j, give in zip(range(1, radix), gives)]
            if k == len(rounds) - 1:
                break
            next_bit, next_radix = rounds[k + 1]
            shape = (total.shape[0] // next_radix, owned, outs)
            total, *gives = call(
                functools.partial(fold_kernel, next_bit, next_radix, len(came)),
                "fold",
                [(shape, f32)] + [(shape, bf16)] * (next_radix - 1),
                [total] + came,
                moved=4 * total.size,
            )
            if bit == 1:
                block = multiply(1, weight[1], theirs[1], gate=total)
            if bit == 2:
                sent = give_back(0, first_block, gate=total)
                later = give_back(1, block, gate=total)
                weight[2] = after(weight[2], total)

        split = [weight[2][p * height : (p + 1) * height] for p in range(parts)] if ring == 4 else []
        last = []
        if split:
            last.append(onward(after(split[0], *came)))
        owned_rows, message = call(
            functools.partial(square_kernel, len(came), lines),
            "square",
            [((owned, outs), f32), ((1, lines + 16, outs), bf16)],
            [total] + came,
        )
        block = multiply(2, weight[2], swap(weight[2], 1), gate=owned_rows)
        messages = after(message, last[0], block) if split else message
        for bit, radix in reversed(rounds):
            if bit >= members:
                came = [swap(messages, j * bit) for j in range(1, radix)]
                messages = jnp.concatenate([messages] + came, axis=0)
        for p in range(1, len(split)):
            last.append(onward(after(split[p], *came)))
        (square,) = call(gathered_kernel, "gathered", [((8, 128), f32)], [messages])
        if sides == 2:
            sent = give_back(2, block, gate=later)
            square = after(square, sent)
        squares = [square] + [swap(square, x) for x in range(1, members)]
        new_first, new_second, whole = call(
            functools.partial(moment_kernel, lay, rows),
            "moment",
            [((owned, outs), f32), ((owned, outs), f32), ((ring, owned, outs), bf16)],
            squares + basis + [owned_rows, first_moment, second_moment, messages],
        )
        blocks = []
        if split:
            block = multiply(3, last[0], swap(last[0], 1), 0, squares[0])
            sent = give_back(3, after(block, *squares), 0)

        for p in range(1, len(split)):
            piece = after(last[p], sent)
            block = multiply(3, piece, swap(piece, 1), p * height)
            sent = give_back(3, block, p * height)

        for bit, radix in reversed(rounds[1:]):
            if bit < members:
                whole = jnp.concatenate([whole, after(swap(whole, bit), block)], axis=0)
        (new_master,) = call(
            functools.partial(back_kernel, lay, owned),
            "back",
            [(master_weight.shape, f32)],
            [proj_basis, whole, swap(whole, 1), master_weight],
            scratch=[pltpu.VMEM((rank, outs), f32)],
            flops=2 * rows * rank * outs,
            moved=8 * 2**20,
        )

        if not split:
            for s in range(3, ring):
                weight.append(onward(weight[s - 1]))
                give_back(s, multiply(s, weight[s], swap(weight[s], 1)))
        activation_grad = state["out"]
        if waiting:
            (activation_grad,) = call(
                functools.partial(last_kernel, lay, rows, [spot for spot, block in waiting]),
                "last",
                [((tokens, width), bf16)],
                [after(block, new_master) for spot, block in waiting] + [activation_grad],
                [VMEM] * len(waiting) + [HBM],
                [HBM],
                scratch=[pltpu.SemaphoreType.DMA((len(waiting), 2))],
                input_output_aliases={len(waiting): 0},
            )
        return (activation_grad, new_master, new_first, new_second)

    return per_device


def solution(mesh):
    spec = P(("groups", "dp"), None)
    return jax.shard_map(
        make_per_device(mesh.shape["dp"]),
        mesh=mesh,
        in_specs=(spec,) * 6,
        out_specs=(spec,) * 4,
        check_vma=False,
    )
```

```python
import functools
import jax
import jax.numpy as jnp
from jax import lax
from jax.experimental import pallas as pl
from jax.experimental.pallas import tpu as pltpu
from jax.sharding import PartitionSpec as P

clip_total = 512.0
step_size = 0.01
first_fix = 1.0 - 0.9**10
second_fix = 1.0 - 0.99**10

f32 = jnp.float32
bf16 = jnp.bfloat16
HBM = pl.BlockSpec(memory_space=pl.ANY)
VMEM = pl.BlockSpec(memory_space=pltpu.VMEM)
PARAMS = pltpu.CompilerParams(vmem_limit_bytes=40 * 2**20)


def after(value, *others):
    return lax.optimization_barrier((value,) + others)[0]


class Layout:
    def __init__(self, n):
        self.n = n
        self.sides = 2 if n == 16 else 1
        self.members = 2 * self.sides
        self.ring = n // self.members
        ring, members = self.ring, self.members
        order = [0, 1, 3, 2] if ring == 4 else list(range(ring))
        self.forward = [
            (order[k] * members + m, order[(k + 1) % ring] * members + m)
            for k in range(ring)
            for m in range(members)
        ]
        self.rounds = [(1, 2)]
        bit = 2
        if self.sides == 2:
            self.rounds.append((2, 2))
            bit = 4
        while bit < n:
            radix = 4 if 2 * bit < n else 2
            self.rounds.append((bit, radix))
            bit *= radix

    def swap(self, value, bit):
        return lax.ppermute(value, "dp", [(i, i ^ bit) for i in range(self.n)])

    def onward(self, value):
        return lax.ppermute(value, "dp", self.forward)

    def source(self, index, s):
        z = index // self.members
        if self.ring != 4:
            return (z - s + self.ring) % self.ring
        k = (z + z // 2 * (5 - 2 * z) - s + 4) % 4
        return k + k // 2 * (5 - 2 * k)


def flip(value, bit):
    return value + bit - 2 * bit * ((value // bit) % 2)


def cut_kernel(lay, rows, plan, act, key_grad, *refs):
    pieces, sems = refs[:-1], refs[-1]
    index = lax.axis_index("dp")
    member = index % lay.members
    copies = []
    for (x, first, count), piece in zip(plan, pieces):
        owner = member
        for bit in (1, 2):
            if x & bit:
                owner = flip(owner, bit)
        for s in range(first, first + count):
            start = pl.multiple_of((lay.source(index, s) * lay.members + owner) * rows, rows)
            copies.append(
                pltpu.make_async_copy(
                    act.at[:, pl.ds(start, rows)],
                    piece.at[:, pl.ds((s - first) * rows, rows)],
                    sems.at[len(copies)],
                )
            )
    if lay.sides == 2:
        copies.append(
            pltpu.make_async_copy(
                key_grad,
                pieces[2].at[:, pl.ds(lay.ring * rows, key_grad.shape[1])],
                sems.at[len(copies)],
            )
        )
    for copy in copies:
        copy.start()
    for copy in copies:
        copy.wait()


def project_kernel(lay, owned, plan, *refs):
    members, ring = lay.members, lay.ring
    acts, refs = refs[: len(plan)], refs[len(plan) :]
    basis, refs = refs[:ring], refs[ring:]
    grads, refs = refs[:members], refs[members:]
    kept, given, grad = refs
    rows = acts[0].shape[1] // ring
    core = lax.axis_index("dp") % 2
    for x in range(members):
        total = None
        for (x_, first, count), piece in zip(plan, acts):
            if x_ != x:
                continue
            for s in range(first, first + count):
                term = jnp.dot(
                    piece[:, (s - first) * rows : (s - first + 1) * rows],
                    basis[s][:rows, :],
                    preferred_element_type=f32,
                )
                total = term if total is None else total + term
        term = lax.dot_general(
            total.astype(bf16),
            grads[x][...],
            (((0,), (0,)), ((), ())),
            preferred_element_type=f32,
        )
        if x == 0:
            grad[...] = term
        else:
            grad[...] += term
    for i in range(lay.n // 2):
        kept[i] = grad[pl.ds(pl.multiple_of((2 * i + core) * owned, owned), owned), :]
        given[i] = grad[pl.ds(pl.multiple_of((2 * i + 1 - core) * owned, owned), owned), :].astype(bf16)


def fold_kernel(bit, radix, came, *refs):
    kept, arrived, outs = refs[0], refs[1 : 1 + came], refs[1 + came :]
    digit = (lax.axis_index("dp") // bit) % radix

    def block(i):
        total = kept[i]
        for piece in arrived:
            total = total + piece[i].astype(f32)
        return total

    for i in range(kept.shape[0] // radix):
        for j in range(radix):
            other = digit
            for b in (1, 2):
                if j & b:
                    other = flip(other, b)
            value = block(i * radix + other)
            outs[j][i] = value.astype(outs[j].dtype)


def square_kernel(came, lines, *refs):
    kept, arrived, (owned, message) = refs[0], refs[1 : 1 + came], refs[1 + came :]
    total = kept[0]
    for piece in arrived:
        total = total + piece[0].astype(f32)
    owned[...] = total
    count = total.shape[0]
    square = jnp.full((16, total.shape[1]), jnp.sum(total * total), f32)
    first = square.astype(bf16).astype(f32)
    second = (square - first).astype(bf16).astype(f32)
    third = square - first - second
    row = lax.broadcasted_iota(jnp.int32, square.shape, 0)
    terms = jnp.where(row == 0, first, jnp.where(row == 1, second, jnp.where(row == 2, third, 0.0)))
    if count < lines:
        total = jnp.concatenate([total, jnp.zeros((lines - count, total.shape[1]), f32)], axis=0)
    message[0, :lines, :] = total.astype(bf16)
    message[0, lines:, :] = terms.astype(bf16)


def gathered_kernel(messages, square):
    lines = messages.shape[1] - 16
    total = jnp.zeros((16, 128), f32)
    for j in range(messages.shape[0]):
        total = total + messages[j, lines:, 0:128].astype(f32)
    square[...] = jnp.full(square.shape, jnp.sum(total[:, 0:1]), f32)


def moment_kernel(lay, rows, *refs):
    squares, refs = refs[: lay.members], refs[lay.members :]
    basis, refs = refs[: lay.ring], refs[lay.ring :]
    owned, first, second, messages, new_first, new_second, update = refs
    total = squares[0][...]
    for square in squares[1:]:
        total = total + square[...]
    factor = jnp.minimum(1.0, clip_total / (jnp.sqrt(total) + 1e-06))[0:1, 0:1]

    def advance(gradient, one, two):
        clipped = gradient * factor
        one = 0.9 * one + 0.1 * clipped
        two = 0.99 * two + 0.01 * clipped * clipped
        return one, two

    one, two = advance(owned[...], first[...], second[...])
    new_first[...] = one
    new_second[...] = two
    count = owned.shape[0]
    half = owned.shape[1] // 2
    index = lax.axis_index("dp")
    for s in range(lay.ring):
        xor = lax.bitwise_xor(lay.source(index, s), index // lay.members)
        slot = place_slot(lay, xor)
        for k in range(2):
            low = rows + k * 2 * count
            moments = basis[s][low : low + 2 * count, :].astype(f32)
            gradient = messages[slot, :, k * half : (k + 1) * half].astype(f32)[:count]
            one, two = advance(gradient, moments[:count], moments[count:])
            update[slot, :, k * half : (k + 1) * half] = (
                one / first_fix / (jnp.sqrt(two / second_fix) + 1e-08)
            ).astype(bf16)


def place_slot(lay, xor):
    slot, scale = 0, 1
    for bit, radix in reversed(lay.rounds):
        if bit >= lay.members:
            slot = slot + scale * ((xor // (bit // lay.members)) % radix)
            scale *= radix
    return slot


def place(lay, s, side, low, width, rows, source, out, sems):
    index = lax.axis_index("dp")
    core = index % 2
    chip = lay.source(index, s) * lay.sides + side
    copies = []
    for k, owner in enumerate((core, 1 - core)):
        start = pl.multiple_of((chip * 2 + owner) * rows + low, width)
        copies.append(
            pltpu.make_async_copy(
                source.at[:, pl.ds(k * width, width)],
                out.at[:, pl.ds(start, width)],
                sems.at[k],
            )
        )
    return copies


def weight_kernel(lay, rows, s, low, parts, came, first, *refs):
    sides = lay.sides
    mine, refs = refs[:parts], refs[parts:]
    theirs, refs = refs[:parts], refs[parts:]
    grads, refs = refs[:sides], refs[sides:]
    if came is not None:
        arrived, refs = refs[0], refs[1:]
    if not first:
        refs = refs[1:]
    out, refs = refs[0], refs[1:]
    if sides == 2:
        far, refs = refs[0], refs[1:]
    own, sems, came_sems = refs
    height = mine[0].shape[0]
    width = parts * height
    side = (lax.axis_index("dp") // 2) % sides
    copies = []
    if came is not None:
        copies = place(
            lay, came[0], 1 - side, came[1], arrived.shape[1] // 2, rows, arrived, out, came_sems
        )
        for copy in copies:
            copy.start()
    for x in reversed(range(sides)):
        target = own if x == 0 else far
        for k, group in enumerate((mine, theirs)):
            for p, piece in enumerate(group):
                target[:, k * width + p * height : k * width + (p + 1) * height] = lax.dot_general(
                    grads[x][...],
                    piece[...],
                    (((1,), (1,)), ((), ())),
                    preferred_element_type=f32,
                ).astype(bf16)
    owns = place(lay, s, side, low, width, rows, own, out, sems)
    for copy in owns:
        copy.start()
    for copy in owns + copies:
        copy.wait()


def last_kernel(lay, rows, blocks, *refs):
    arrived, (before, out, sems) = refs[: len(blocks)], refs[len(blocks) :]
    side = (lax.axis_index("dp") // 2) % lay.sides
    copies = []
    for k, (s, low) in enumerate(blocks):
        wide = arrived[k].shape[1] // 2
        copies += place(lay, s, 1 - side, low, wide, rows, arrived[k], out, sems.at[k])
    for copy in copies:
        copy.start()
    for copy in copies:
        copy.wait()


def back_kernel(lay, owned, basis, near, other, master, out, update):
    index = lax.axis_index("dp")
    half = lay.n // 2
    for j in range(lay.n):
        owner = index
        for bit in [1 << b for b in range(lay.n.bit_length() - 1)]:
            if slot_to_xor(lay, j) & bit:
                owner = flip(owner, bit)
        piece = near[j] if j < half else other[j - half]
        update[pl.ds(pl.multiple_of(owner * owned, owned), owned), :] = piece.astype(f32)
    out[...] = master[...] - step_size * jnp.dot(
        basis[...], update[...].astype(bf16), preferred_element_type=f32
    )


def slot_to_xor(lay, j):
    xor = 0
    for bit, radix in reversed(lay.rounds):
        xor += (j % radix) * bit
        j //= radix
    return xor


def call(kernel, name, shapes, args, in_specs=None, out_specs=None, scratch=(), flops=0, moved=2**20, **more):
    return pl.pallas_call(
        kernel,
        name=name,
        out_shape=[jax.ShapeDtypeStruct(shape, dtype) for shape, dtype in shapes],
        in_specs=in_specs or [VMEM] * len(args),
        out_specs=out_specs or [VMEM] * len(shapes),
        scratch_shapes=list(scratch),
        compiler_params=PARAMS,
        cost_estimate=pl.CostEstimate(flops=flops, bytes_accessed=moved, transcendentals=0),
        **more,
    )(*args)


def make_per_device(n):
    lay = Layout(n)
    sides, members, ring, rounds = lay.sides, lay.members, lay.ring, lay.rounds
    swap, onward = lay.swap, lay.onward

    def per_device(activations, key_grad, proj_basis, master_weight, first_moment, second_moment):
        tokens, width = activations.shape
        rows, rank = proj_basis.shape
        outs = key_grad.shape[1]
        owned = rank // n
        lines = -(-owned // 16) * 16
        parts = 2 if rows % 256 == 0 else 1
        height = rows // parts

        plan = [(x, 0, ring) for x in range(members)]
        wides = [ring * rows + (outs if x == 2 else 0) for x in range(members)]
        cut = call(
            functools.partial(cut_kernel, lay, rows, plan),
            "cut",
            [((tokens, wide), bf16) for wide in wides],
            [activations, key_grad],
            in_specs=[HBM, HBM],
            scratch=[pltpu.SemaphoreType.DMA((members * ring + 1,))],
            moved=4 * tokens * ring * rows * members,
        )

        acts = [cut[0]] + [swap(cut[x], x) for x in range(1, members)]
        moments = jnp.concatenate([first_moment, second_moment], axis=0).astype(bf16)
        folded = [moments[:, k * rank : (k + 1) * rank] for k in range(outs // rank)]
        basis = [after(jnp.concatenate([proj_basis] + folded, axis=0), cut[0])]
        for s in range(1, ring):
            basis.append(onward(basis[-1]))
        weight = [master_weight.astype(bf16)]
        weight.append(onward(after(weight[0], basis[-1])))

        if sides == 2:
            far_grad = acts[2][:, ring * rows :]
            near = swap(jnp.concatenate([key_grad, far_grad], axis=0), 1)
            grads = [key_grad, near[:tokens], far_grad, near[tokens:]]
        else:
            near = swap(key_grad, 1)
            grads = [key_grad, near]
        theirs = [swap(after(weight[0], basis[1]), 1)]

        side_grads = [key_grad, far_grad] if sides == 2 else [key_grad]
        state = {"out": None}
        waiting = []

        def multiply(s, mine, theirs, low=0, gate=None):
            args = [mine if gate is None else after(mine, gate), theirs] + side_grads
            in_specs = [VMEM] * len(args)
            wide = mine.shape[0]
            came = None
            if len(waiting) > 1:
                (came, block) = waiting.pop(0)
                args.append(block)
                in_specs.append(VMEM)
            first = state["out"] is None
            if not first:
                args.append(state["out"])
                in_specs.append(HBM)
            shapes, out_specs = [((tokens, width), bf16)], [HBM]
            if sides == 2:
                shapes.append(((tokens, 2 * wide), bf16))
                out_specs.append(VMEM)
            result = call(
                functools.partial(weight_kernel, lay, rows, s, low, 1, came, first),
                "weight",
                shapes,
                args,
                in_specs,
                out_specs,
                scratch=[
                    pltpu.VMEM((tokens, 2 * wide), bf16),
                    pltpu.SemaphoreType.DMA((2,)),
                    pltpu.SemaphoreType.DMA((2,)),
                ],
                flops=4 * sides * tokens * wide * outs,
                moved=6 * 2**20,
                input_output_aliases={} if first else {len(args) - 1: 0},
            )
            state["out"] = result[0]
            return result[1] if sides == 2 else result[0]

        def give_back(s, block, low=0, gate=None):
            if sides == 1:
                return block
            waiting.append(((s, low), swap(block if gate is None else after(block, gate), 2)))
            return waiting[-1][1]

        first_block = multiply(0, weight[0], theirs[0])
        total, *gives = call(
            functools.partial(project_kernel, lay, owned, plan),
            "project",
            [((n // 2, owned, outs), f32), ((n // 2, owned, outs), bf16)],
            [after(acts[0], first_block)] + acts[1:] + basis + grads,
            scratch=[pltpu.VMEM((rank, outs), f32)],
            flops=2 * tokens * members * rank * (ring * rows + outs),
            moved=12 * 2**20,
        )
        weight[1] = after(weight[1], total)
        halves = [weight[1][p * height : (p + 1) * height] for p in range(parts)]
        second = [onward(halves[0])]
        theirs.append(swap(weight[1], 1))

        for k, (bit, radix) in enumerate(rounds):
            if bit == members:
                gives = [after(give, second[0]) for give in gives]
            came = [swap(give, j * bit) for j, give in zip(range(1, radix), gives)]
            if k == len(rounds) - 1:
                break
            next_bit, next_radix = rounds[k + 1]
            shape = (total.shape[0] // next_radix, owned, outs)
            total, *gives = call(
                functools.partial(fold_kernel, next_bit, next_radix, len(came)),
                "fold",
                [(shape, f32)] + [(shape, bf16)] * (next_radix - 1),
                [total] + came,
                moved=4 * total.size,
            )
            if bit == 1:
                block = multiply(1, weight[1], theirs[1], gate=total)
            if bit == 2:
                sent = give_back(0, first_block, gate=total)
                later = give_back(1, block, gate=total)
        owned_rows, message = call(
            functools.partial(square_kernel, len(came), lines),
            "square",
            [((owned, outs), f32), ((1, lines + 16, outs), bf16)],
            [total] + came,
        )

        messages = after(message, sent) if sides == 2 else message
        for bit, radix in reversed(rounds):
            if bit >= members:
                came = [swap(messages, j * bit) for j in range(1, radix)]
                messages = jnp.concatenate([messages] + came, axis=0)
        second += [onward(after(half, *came)) for half in halves[1:]]
        third = []
        if ring == 4:
            third = [onward(after(piece, *came) if p == 0 else piece) for p, piece in enumerate(second)]
        (square,) = call(gathered_kernel, "gathered", [((8, 128), f32)], [messages])
        if sides == 2:
            square = after(square, later)
        squares = [square] + [swap(square, x) for x in range(1, members)]
        new_first, new_second, update = call(
            functools.partial(moment_kernel, lay, rows),
            "moment",
            [((owned, outs), f32), ((owned, outs), f32), ((ring, owned, outs), bf16)],
            squares + basis + [owned_rows, first_moment, second_moment, messages],
        )
        piece = after(second[0], owned_rows)
        block = multiply(2, piece, swap(piece, 1))
        sent = give_back(2, block, gate=update)

        whole = update
        for bit, radix in reversed(rounds[1:]):
            if bit < members:
                whole = jnp.concatenate([whole, swap(whole, bit)], axis=0)
        (new_master,) = call(
            functools.partial(back_kernel, lay, owned),
            "back",
            [(master_weight.shape, f32)],
            [proj_basis, whole, swap(whole, 1), master_weight],
            scratch=[pltpu.VMEM((rank, outs), f32)],
            flops=2 * rows * rank * outs,
            moved=8 * 2**20,
        )

        spots = [(2, p, second[p]) for p in range(1, parts)]
        spots += [(3, p, third[p]) for p in range(len(third))]
        if ring != 4:
            spots = []
            for s in range(3, ring):
                second = [onward(piece) for piece in second]
                spots += [(s, p, piece) for p, piece in enumerate(second)]
        for s, p, piece in spots:
            piece = after(piece, sent, new_master) if (s, p) == (3, parts - 1) else after(piece, sent)
            block = multiply(s, piece, swap(piece, 1), p * height)
            sent = give_back(s, block, p * height)
        activation_grad = state["out"]
        if waiting:
            (activation_grad,) = call(
                functools.partial(last_kernel, lay, rows, [spot for spot, block in waiting]),
                "last",
                [((tokens, width), bf16)],
                [block for spot, block in waiting] + [activation_grad],
                [VMEM] * len(waiting) + [HBM],
                [HBM],
                scratch=[pltpu.SemaphoreType.DMA((len(waiting), 2))],
                input_output_aliases={len(waiting): 0},
            )
        return (activation_grad, new_master, new_first, new_second)

    return per_device


def solution(mesh):
    spec = P(("groups", "dp"), None)
    return jax.shard_map(
        make_per_device(mesh.shape["dp"]),
        mesh=mesh,
        in_specs=(spec,) * 6,
        out_specs=(spec,) * 4,
        check_vma=False,
    )
```

```python
import functools
import jax
import jax.numpy as jnp
from jax import lax
from jax.experimental import pallas as pl
from jax.experimental.pallas import tpu as pltpu
from jax.sharding import PartitionSpec as P

clip_total = 512.0
step_size = 0.01
first_fix = 1.0 - 0.9**10
second_fix = 1.0 - 0.99**10

f32 = jnp.float32
bf16 = jnp.bfloat16
HBM = pl.BlockSpec(memory_space=pl.ANY)
VMEM = pl.BlockSpec(memory_space=pltpu.VMEM)
PARAMS = pltpu.CompilerParams(vmem_limit_bytes=40 * 2**20)


def after(value, *others):
    return lax.optimization_barrier((value,) + others)[0]


class Layout:
    def __init__(self, n):
        self.n = n
        self.sides = 2 if n == 16 else 1
        self.members = 2 * self.sides
        self.ring = n // self.members
        ring, members = self.ring, self.members
        order = [0, 1, 3, 2] if ring == 4 else list(range(ring))
        self.forward = [
            (order[k] * members + m, order[(k + 1) % ring] * members + m)
            for k in range(ring)
            for m in range(members)
        ]
        self.rounds = [(1, 2)]
        bit = 2
        if self.sides == 2:
            self.rounds.append((2, 2))
            bit = 4
        while bit < n:
            radix = 4 if 2 * bit < n else 2
            self.rounds.append((bit, radix))
            bit *= radix

    def swap(self, value, bit):
        return lax.ppermute(value, "dp", [(i, i ^ bit) for i in range(self.n)])

    def onward(self, value):
        return lax.ppermute(value, "dp", self.forward)

    def source(self, index, s):
        z = index // self.members
        if self.ring != 4:
            return (z - s + self.ring) % self.ring
        k = (z + z // 2 * (5 - 2 * z) - s + 4) % 4
        return k + k // 2 * (5 - 2 * k)


def flip(value, bit):
    return value + bit - 2 * bit * ((value // bit) % 2)


def cut_kernel(lay, rows, plan, act, key_grad, *refs):
    pieces, sems = refs[:-1], refs[-1]
    index = lax.axis_index("dp")
    member = index % lay.members
    copies = []
    for (x, first, count), piece in zip(plan, pieces):
        owner = member
        for bit in (1, 2):
            if x & bit:
                owner = flip(owner, bit)
        for s in range(first, first + count):
            start = pl.multiple_of((lay.source(index, s) * lay.members + owner) * rows, rows)
            copies.append(
                pltpu.make_async_copy(
                    act.at[:, pl.ds(start, rows)],
                    piece.at[:, pl.ds((s - first) * rows, rows)],
                    sems.at[len(copies)],
                )
            )
    if lay.sides == 2:
        copies.append(
            pltpu.make_async_copy(
                key_grad,
                pieces[2].at[:, pl.ds(lay.ring * rows, key_grad.shape[1])],
                sems.at[len(copies)],
            )
        )
    for copy in copies:
        copy.start()
    for copy in copies:
        copy.wait()


def project_kernel(lay, owned, plan, *refs):
    members, ring = lay.members, lay.ring
    acts, refs = refs[: len(plan)], refs[len(plan) :]
    basis, refs = refs[:ring], refs[ring:]
    grads, refs = refs[:members], refs[members:]
    kept, given, grad = refs
    rows = acts[0].shape[1] // ring
    core = lax.axis_index("dp") % 2
    for x in range(members):
        total = None
        for (x_, first, count), piece in zip(plan, acts):
            if x_ != x:
                continue
            for s in range(first, first + count):
                term = jnp.dot(
                    piece[:, (s - first) * rows : (s - first + 1) * rows],
                    basis[s][:rows, :],
                    preferred_element_type=f32,
                )
                total = term if total is None else total + term
        term = lax.dot_general(
            total.astype(bf16),
            grads[x][...],
            (((0,), (0,)), ((), ())),
            preferred_element_type=f32,
        )
        if x == 0:
            grad[...] = term
        else:
            grad[...] += term
    for i in range(lay.n // 2):
        kept[i] = grad[pl.ds(pl.multiple_of((2 * i + core) * owned, owned), owned), :]
        given[i] = grad[pl.ds(pl.multiple_of((2 * i + 1 - core) * owned, owned), owned), :].astype(bf16)


def fold_kernel(bit, radix, came, *refs):
    kept, arrived, outs = refs[0], refs[1 : 1 + came], refs[1 + came :]
    digit = (lax.axis_index("dp") // bit) % radix

    def block(i):
        total = kept[i]
        for piece in arrived:
            total = total + piece[i].astype(f32)
        return total

    for i in range(kept.shape[0] // radix):
        for j in range(radix):
            other = digit
            for b in (1, 2):
                if j & b:
                    other = flip(other, b)
            value = block(i * radix + other)
            outs[j][i] = value.astype(outs[j].dtype)


def square_kernel(came, lines, *refs):
    kept, arrived, (owned, message) = refs[0], refs[1 : 1 + came], refs[1 + came :]
    total = kept[0]
    for piece in arrived:
        total = total + piece[0].astype(f32)
    owned[...] = total
    count = total.shape[0]
    square = jnp.full((16, total.shape[1]), jnp.sum(total * total), f32)
    first = square.astype(bf16).astype(f32)
    second = (square - first).astype(bf16).astype(f32)
    third = square - first - second
    row = lax.broadcasted_iota(jnp.int32, square.shape, 0)
    terms = jnp.where(row == 0, first, jnp.where(row == 1, second, jnp.where(row == 2, third, 0.0)))
    if count < lines:
        total = jnp.concatenate([total, jnp.zeros((lines - count, total.shape[1]), f32)], axis=0)
    message[0, :lines, :] = total.astype(bf16)
    message[0, lines:, :] = terms.astype(bf16)


def gathered_kernel(messages, square):
    lines = messages.shape[1] - 16
    total = jnp.zeros((16, 128), f32)
    for j in range(messages.shape[0]):
        total = total + messages[j, lines:, 0:128].astype(f32)
    square[...] = jnp.full(square.shape, jnp.sum(total[:, 0:1]), f32)


def moment_kernel(lay, rows, *refs):
    squares, refs = refs[: lay.members], refs[lay.members :]
    basis, refs = refs[: lay.ring], refs[lay.ring :]
    owned, first, second, messages, new_first, new_second, update = refs
    total = squares[0][...]
    for square in squares[1:]:
        total = total + square[...]
    factor = jnp.minimum(1.0, clip_total / (jnp.sqrt(total) + 1e-06))[0:1, 0:1]

    def advance(gradient, one, two):
        clipped = gradient * factor
        one = 0.9 * one + 0.1 * clipped
        two = 0.99 * two + 0.01 * clipped * clipped
        return one, two

    one, two = advance(owned[...], first[...], second[...])
    new_first[...] = one
    new_second[...] = two
    count = owned.shape[0]
    half = owned.shape[1] // 2
    index = lax.axis_index("dp")
    for s in range(lay.ring):
        xor = lax.bitwise_xor(lay.source(index, s), index // lay.members)
        slot = place_slot(lay, xor)
        for k in range(2):
            low = rows + k * 2 * count
            moments = basis[s][low : low + 2 * count, :].astype(f32)
            gradient = messages[slot, :, k * half : (k + 1) * half].astype(f32)[:count]
            one, two = advance(gradient, moments[:count], moments[count:])
            update[slot, :, k * half : (k + 1) * half] = (
                one / first_fix / (jnp.sqrt(two / second_fix) + 1e-08)
            ).astype(bf16)


def place_slot(lay, xor):
    slot, scale = 0, 1
    for bit, radix in reversed(lay.rounds):
        if bit >= lay.members:
            slot = slot + scale * ((xor // (bit // lay.members)) % radix)
            scale *= radix
    return slot


def place(lay, s, side, low, width, rows, source, out, sems):
    index = lax.axis_index("dp")
    core = index % 2
    chip = lay.source(index, s) * lay.sides + side
    copies = []
    for k, owner in enumerate((core, 1 - core)):
        start = pl.multiple_of((chip * 2 + owner) * rows + low, width)
        copies.append(
            pltpu.make_async_copy(
                source.at[:, pl.ds(k * width, width)],
                out.at[:, pl.ds(start, width)],
                sems.at[k],
            )
        )
    return copies


def weight_kernel(lay, rows, s, low, parts, came, first, *refs):
    sides = lay.sides
    mine, refs = refs[:parts], refs[parts:]
    theirs, refs = refs[:parts], refs[parts:]
    grads, refs = refs[:sides], refs[sides:]
    if came is not None:
        arrived, refs = refs[0], refs[1:]
    if not first:
        refs = refs[1:]
    out, refs = refs[0], refs[1:]
    if sides == 2:
        far, refs = refs[0], refs[1:]
    own, sems, came_sems = refs
    height = mine[0].shape[0]
    width = parts * height
    side = (lax.axis_index("dp") // 2) % sides
    copies = []
    if came is not None:
        copies = place(
            lay, came[0], 1 - side, came[1], arrived.shape[1] // 2, rows, arrived, out, came_sems
        )
        for copy in copies:
            copy.start()
    for x in reversed(range(sides)):
        target = own if x == 0 else far
        for k, group in enumerate((mine, theirs)):
            for p, piece in enumerate(group):
                target[:, k * width + p * height : k * width + (p + 1) * height] = lax.dot_general(
                    grads[x][...],
                    piece[...],
                    (((1,), (1,)), ((), ())),
                    preferred_element_type=f32,
                ).astype(bf16)
    owns = place(lay, s, side, low, width, rows, own, out, sems)
    for copy in owns:
        copy.start()
    for copy in owns + copies:
        copy.wait()


def last_kernel(lay, rows, blocks, *refs):
    arrived, (before, out, sems) = refs[: len(blocks)], refs[len(blocks) :]
    side = (lax.axis_index("dp") // 2) % lay.sides
    copies = []
    for k, (s, low) in enumerate(blocks):
        wide = arrived[k].shape[1] // 2
        copies += place(lay, s, 1 - side, low, wide, rows, arrived[k], out, sems.at[k])
    for copy in copies:
        copy.start()
    for copy in copies:
        copy.wait()


def back_kernel(lay, owned, basis, near, other, master, out, update):
    index = lax.axis_index("dp")
    half = lay.n // 2
    for j in range(lay.n):
        owner = index
        for bit in [1 << b for b in range(lay.n.bit_length() - 1)]:
            if slot_to_xor(lay, j) & bit:
                owner = flip(owner, bit)
        piece = near[j] if j < half else other[j - half]
        update[pl.ds(pl.multiple_of(owner * owned, owned), owned), :] = piece.astype(f32)
    out[...] = master[...] - step_size * jnp.dot(
        basis[...], update[...].astype(bf16), preferred_element_type=f32
    )


def slot_to_xor(lay, j):
    xor = 0
    for bit, radix in reversed(lay.rounds):
        xor += (j % radix) * bit
        j //= radix
    return xor


def call(kernel, name, shapes, args, in_specs=None, out_specs=None, scratch=(), flops=0, moved=2**20, **more):
    return pl.pallas_call(
        kernel,
        name=name,
        out_shape=[jax.ShapeDtypeStruct(shape, dtype) for shape, dtype in shapes],
        in_specs=in_specs or [VMEM] * len(args),
        out_specs=out_specs or [VMEM] * len(shapes),
        scratch_shapes=list(scratch),
        compiler_params=PARAMS,
        cost_estimate=pl.CostEstimate(flops=flops, bytes_accessed=moved, transcendentals=0),
        **more,
    )(*args)


def make_per_device(n):
    lay = Layout(n)
    sides, members, ring, rounds = lay.sides, lay.members, lay.ring, lay.rounds
    swap, onward = lay.swap, lay.onward

    def per_device(activations, key_grad, proj_basis, master_weight, first_moment, second_moment):
        tokens, width = activations.shape
        rows, rank = proj_basis.shape
        outs = key_grad.shape[1]
        owned = rank // n
        lines = -(-owned // 16) * 16
        parts = 2 if rows % 256 == 0 else 1
        height = rows // parts

        plan = [(x, 0, ring) for x in range(members)]
        wides = [ring * rows + (outs if x == 2 else 0) for x in range(members)]
        cut = call(
            functools.partial(cut_kernel, lay, rows, plan),
            "cut",
            [((tokens, wide), bf16) for wide in wides],
            [activations, key_grad],
            in_specs=[HBM, HBM],
            scratch=[pltpu.SemaphoreType.DMA((members * ring + 1,))],
            moved=4 * tokens * ring * rows * members,
        )

        acts = [cut[0]] + [swap(cut[x], x) for x in range(1, members)]
        moments = jnp.concatenate([first_moment, second_moment], axis=0).astype(bf16)
        folded = [moments[:, k * rank : (k + 1) * rank] for k in range(outs // rank)]
        basis = [after(jnp.concatenate([proj_basis] + folded, axis=0), cut[0])]
        for s in range(1, ring):
            basis.append(onward(basis[-1]))
        weight = [master_weight.astype(bf16)]
        weight.append(onward(after(weight[0], basis[-1])))

        if sides == 2:
            acts[2] = after(acts[2], basis[2])
            far_grad = acts[2][:, ring * rows :]
            near = swap(jnp.concatenate([key_grad, far_grad], axis=0), 1)
            grads = [key_grad, near[:tokens], far_grad, near[tokens:]]
        else:
            near = swap(key_grad, 1)
            grads = [key_grad, near]
        theirs = [swap(after(weight[0], basis[1]), 1)]

        side_grads = [key_grad, far_grad] if sides == 2 else [key_grad]
        state = {"out": None}
        waiting = []

        def multiply(s, mine, theirs, low=0, gate=None):
            args = [mine if gate is None else after(mine, gate), theirs] + side_grads
            in_specs = [VMEM] * len(args)
            wide = mine.shape[0]
            came = None
            if len(waiting) > 1:
                (came, block) = waiting.pop(0)
                args.append(block)
                in_specs.append(VMEM)
            first = state["out"] is None
            if not first:
                args.append(state["out"])
                in_specs.append(HBM)
            shapes, out_specs = [((tokens, width), bf16)], [HBM]
            if sides == 2:
                shapes.append(((tokens, 2 * wide), bf16))
                out_specs.append(VMEM)
            result = call(
                functools.partial(weight_kernel, lay, rows, s, low, 1, came, first),
                "weight",
                shapes,
                args,
                in_specs,
                out_specs,
                scratch=[
                    pltpu.VMEM((tokens, 2 * wide), bf16),
                    pltpu.SemaphoreType.DMA((2,)),
                    pltpu.SemaphoreType.DMA((2,)),
                ],
                flops=4 * sides * tokens * wide * outs,
                moved=6 * 2**20,
                input_output_aliases={} if first else {len(args) - 1: 0},
            )
            state["out"] = result[0]
            return result[1] if sides == 2 else result[0]

        def give_back(s, block, low=0, gate=None):
            if sides == 1:
                return block
            waiting.append(((s, low), swap(block if gate is None else after(block, gate), 2)))
            return waiting[-1][1]

        first_block = multiply(0, weight[0], theirs[0])
        total, *gives = call(
            functools.partial(project_kernel, lay, owned, plan),
            "project",
            [((n // 2, owned, outs), f32), ((n // 2, owned, outs), bf16)],
            [after(acts[0], first_block)] + acts[1:] + basis + grads,
            scratch=[pltpu.VMEM((rank, outs), f32)],
            flops=2 * tokens * members * rank * (ring * rows + outs),
            moved=12 * 2**20,
        )
        weight[1] = after(weight[1], total)
        weight.append(onward(weight[1]))
        theirs.append(swap(weight[1], 1))

        for k, (bit, radix) in enumerate(rounds):
            if bit == members:
                gives = [after(give, weight[2], sent if sides == 2 else block) for give in gives]
            came = [swap(give, j * bit) for j, give in zip(range(1, radix), gives)]
            if k == len(rounds) - 1:
                break
            next_bit, next_radix = rounds[k + 1]
            shape = (total.shape[0] // next_radix, owned, outs)
            total, *gives = call(
                functools.partial(fold_kernel, next_bit, next_radix, len(came)),
                "fold",
                [(shape, f32)] + [(shape, bf16)] * (next_radix - 1),
                [after(total, block) if bit == 2 else total] + came,
                moved=4 * total.size,
            )
            if bit == 1:
                block = multiply(1, weight[1], theirs[1], gate=total)
            if bit == 2:
                sent = give_back(0, first_block, gate=total)
                later = give_back(1, block, gate=total)
                weight[2] = after(weight[2], total, sent)

        owned_rows, message = call(
            functools.partial(square_kernel, len(came), lines),
            "square",
            [((owned, outs), f32), ((1, lines + 16, outs), bf16)],
            [total] + came,
        )
        their_step = swap(weight[2], 1)
        messages = message
        for bit, radix in reversed(rounds):
            if bit >= members:
                came = [swap(messages, j * bit) for j in range(1, radix)]
                messages = jnp.concatenate([messages] + came, axis=0)

        split = [weight[2][p * height : (p + 1) * height] for p in range(parts)] if ring == 4 else []
        last = [onward(after(piece, *came)) for piece in split[:1]]
        block = multiply(2, weight[2], their_step, gate=owned_rows)
        (square,) = call(gathered_kernel, "gathered", [((8, 128), f32)], [messages])
        if sides == 2:
            sent = give_back(2, block, gate=later)
            square = after(square, sent)
        squares = [square] + [swap(square, x) for x in range(1, members)]
        last += [onward(after(piece, square)) for piece in split[1:]]
        new_first, new_second, update = call(
            functools.partial(moment_kernel, lay, rows),
            "moment",
            [((owned, outs), f32), ((owned, outs), f32), ((ring, owned, outs), bf16)],
            squares + basis + [owned_rows, first_moment, second_moment, messages],
        )
        whole = update
        for bit, radix in reversed(rounds[1:]):
            if bit < members:
                whole = jnp.concatenate(
                    [whole] + [swap(whole, j * bit) for j in range(1, radix)], axis=0
                )
        (new_master,) = call(
            functools.partial(back_kernel, lay, owned),
            "back",
            [(master_weight.shape, f32)],
            [proj_basis, whole, swap(whole, 1), master_weight],
            scratch=[pltpu.VMEM((rank, outs), f32)],
            flops=2 * rows * rank * outs,
            moved=8 * 2**20,
        )

        for p in range(len(split)):
            piece = after(last[p], update if p == 0 else sent)
            block = multiply(3, piece, swap(piece, 1), p * height)
            sent = give_back(3, block, p * height, whole if p == 0 else None)
        if not split:
            for s in range(3, ring):
                weight.append(onward(weight[s - 1]))
                give_back(s, multiply(s, weight[s], swap(weight[s], 1)))
        activation_grad = state["out"]
        if waiting:
            (activation_grad,) = call(
                functools.partial(last_kernel, lay, rows, [spot for spot, block in waiting]),
                "last",
                [((tokens, width), bf16)],
                [after(block, new_master) for spot, block in waiting] + [activation_grad],
                [VMEM] * len(waiting) + [HBM],
                [HBM],
                scratch=[pltpu.SemaphoreType.DMA((len(waiting), 2))],
                input_output_aliases={len(waiting): 0},
            )
        return (activation_grad, new_master, new_first, new_second)

    return per_device


def solution(mesh):
    spec = P(("groups", "dp"), None)
    return jax.shard_map(
        make_per_device(mesh.shape["dp"]),
        mesh=mesh,
        in_specs=(spec,) * 6,
        out_specs=(spec,) * 4,
        check_vma=False,
    )
```

```python
import functools
import jax
import jax.numpy as jnp
from jax import lax
from jax.experimental import pallas as pl
from jax.experimental.pallas import tpu as pltpu
from jax.sharding import PartitionSpec as P

clip_total = 512.0
step_size = 0.01
first_fix = 1.0 - 0.9**10
second_fix = 1.0 - 0.99**10

f32 = jnp.float32
bf16 = jnp.bfloat16
HBM = pl.BlockSpec(memory_space=pl.ANY)
VMEM = pl.BlockSpec(memory_space=pltpu.VMEM)
PARAMS = pltpu.CompilerParams(vmem_limit_bytes=40 * 2**20)


def after(value, *others):
    return lax.optimization_barrier((value,) + others)[0]


class Layout:
    def __init__(self, n):
        self.n = n
        self.sides = 2 if n == 16 else 1
        self.members = 2 * self.sides
        self.ring = n // self.members
        ring, members = self.ring, self.members
        order = [0, 1, 3, 2] if ring == 4 else list(range(ring))
        self.forward = [
            (order[k] * members + m, order[(k + 1) % ring] * members + m)
            for k in range(ring)
            for m in range(members)
        ]
        self.rounds = [(1, 2)]
        bit = 2
        if self.sides == 2:
            self.rounds.append((2, 2))
            bit = 4
        while bit < n:
            radix = 4 if 2 * bit < n else 2
            self.rounds.append((bit, radix))
            bit *= radix

    def swap(self, value, bit):
        return lax.ppermute(value, "dp", [(i, i ^ bit) for i in range(self.n)])

    def onward(self, value):
        return lax.ppermute(value, "dp", self.forward)

    def source(self, index, s):
        z = index // self.members
        if self.ring != 4:
            return (z - s + self.ring) % self.ring
        k = (z + z // 2 * (5 - 2 * z) - s + 4) % 4
        return k + k // 2 * (5 - 2 * k)


def flip(value, bit):
    return value + bit - 2 * bit * ((value // bit) % 2)


def cut_kernel(lay, rows, plan, act, key_grad, *refs):
    pieces, sems = refs[:-1], refs[-1]
    index = lax.axis_index("dp")
    member = index % lay.members
    copies = []
    for (x, first, count), piece in zip(plan, pieces):
        owner = member
        for bit in (1, 2):
            if x & bit:
                owner = flip(owner, bit)
        for s in range(first, first + count):
            start = pl.multiple_of((lay.source(index, s) * lay.members + owner) * rows, rows)
            copies.append(
                pltpu.make_async_copy(
                    act.at[:, pl.ds(start, rows)],
                    piece.at[:, pl.ds((s - first) * rows, rows)],
                    sems.at[len(copies)],
                )
            )
    if lay.sides == 2:
        copies.append(
            pltpu.make_async_copy(
                key_grad,
                pieces[2].at[:, pl.ds(lay.ring * rows, key_grad.shape[1])],
                sems.at[len(copies)],
            )
        )
    for copy in copies:
        copy.start()
    for copy in copies:
        copy.wait()


def project_kernel(lay, owned, plan, *refs):
    members, ring = lay.members, lay.ring
    acts, refs = refs[: len(plan)], refs[len(plan) :]
    basis, refs = refs[:ring], refs[ring:]
    grads, refs = refs[:members], refs[members:]
    kept, given, grad = refs
    rows = acts[0].shape[1] // ring
    core = lax.axis_index("dp") % 2
    for x in range(members):
        total = None
        for (x_, first, count), piece in zip(plan, acts):
            if x_ != x:
                continue
            for s in range(first, first + count):
                term = jnp.dot(
                    piece[:, (s - first) * rows : (s - first + 1) * rows],
                    basis[s][:rows, :],
                    preferred_element_type=f32,
                )
                total = term if total is None else total + term
        term = lax.dot_general(
            total.astype(bf16),
            grads[x][...],
            (((0,), (0,)), ((), ())),
            preferred_element_type=f32,
        )
        if x == 0:
            grad[...] = term
        else:
            grad[...] += term
    for i in range(lay.n // 2):
        kept[i] = grad[pl.ds(pl.multiple_of((2 * i + core) * owned, owned), owned), :]
        given[i] = grad[pl.ds(pl.multiple_of((2 * i + 1 - core) * owned, owned), owned), :].astype(bf16)


def fold_kernel(bit, radix, came, *refs):
    kept, arrived, outs = refs[0], refs[1 : 1 + came], refs[1 + came :]
    digit = (lax.axis_index("dp") // bit) % radix

    def block(i):
        total = kept[i]
        for piece in arrived:
            total = total + piece[i].astype(f32)
        return total

    for i in range(kept.shape[0] // radix):
        for j in range(radix):
            other = digit
            for b in (1, 2):
                if j & b:
                    other = flip(other, b)
            value = block(i * radix + other)
            outs[j][i] = value.astype(outs[j].dtype)


def square_kernel(came, lines, *refs):
    kept, arrived, (owned, message) = refs[0], refs[1 : 1 + came], refs[1 + came :]
    total = kept[0]
    for piece in arrived:
        total = total + piece[0].astype(f32)
    owned[...] = total
    count = total.shape[0]
    square = jnp.full((16, total.shape[1]), jnp.sum(total * total), f32)
    first = square.astype(bf16).astype(f32)
    second = (square - first).astype(bf16).astype(f32)
    third = square - first - second
    row = lax.broadcasted_iota(jnp.int32, square.shape, 0)
    terms = jnp.where(row == 0, first, jnp.where(row == 1, second, jnp.where(row == 2, third, 0.0)))
    if count < lines:
        total = jnp.concatenate([total, jnp.zeros((lines - count, total.shape[1]), f32)], axis=0)
    message[0, :lines, :] = total.astype(bf16)
    message[0, lines:, :] = terms.astype(bf16)


def gathered_kernel(messages, square):
    lines = messages.shape[1] - 16
    total = jnp.zeros((16, 128), f32)
    for j in range(messages.shape[0]):
        total = total + messages[j, lines:, 0:128].astype(f32)
    square[...] = jnp.full(square.shape, jnp.sum(total[:, 0:1]), f32)


def moment_kernel(lay, rows, *refs):
    squares, refs = refs[: lay.members], refs[lay.members :]
    basis, refs = refs[: lay.ring], refs[lay.ring :]
    owned, first, second, messages, new_first, new_second, update = refs
    total = squares[0][...]
    for square in squares[1:]:
        total = total + square[...]
    factor = jnp.minimum(1.0, clip_total / (jnp.sqrt(total) + 1e-06))[0:1, 0:1]

    def advance(gradient, one, two):
        clipped = gradient * factor
        one = 0.9 * one + 0.1 * clipped
        two = 0.99 * two + 0.01 * clipped * clipped
        return one, two

    one, two = advance(owned[...], first[...], second[...])
    new_first[...] = one
    new_second[...] = two
    count = owned.shape[0]
    half = owned.shape[1] // 2
    index = lax.axis_index("dp")
    for s in range(lay.ring):
        xor = lax.bitwise_xor(lay.source(index, s), index // lay.members)
        slot = place_slot(lay, xor)
        for k in range(2):
            low = rows + k * 2 * count
            moments = basis[s][low : low + 2 * count, :].astype(f32)
            gradient = messages[slot, :, k * half : (k + 1) * half].astype(f32)[:count]
            one, two = advance(gradient, moments[:count], moments[count:])
            update[slot, :, k * half : (k + 1) * half] = (
                one / first_fix / (jnp.sqrt(two / second_fix) + 1e-08)
            ).astype(bf16)


def place_slot(lay, xor):
    slot, scale = 0, 1
    for bit, radix in reversed(lay.rounds):
        if bit >= lay.members:
            slot = slot + scale * ((xor // (bit // lay.members)) % radix)
            scale *= radix
    return slot


def place(lay, s, side, low, width, rows, source, out, sems):
    index = lax.axis_index("dp")
    core = index % 2
    chip = lay.source(index, s) * lay.sides + side
    copies = []
    for k, owner in enumerate((core, 1 - core)):
        start = pl.multiple_of((chip * 2 + owner) * rows + low, width)
        copies.append(
            pltpu.make_async_copy(
                source.at[:, pl.ds(k * width, width)],
                out.at[:, pl.ds(start, width)],
                sems.at[k],
            )
        )
    return copies


def weight_kernel(lay, rows, s, low, parts, came, first, *refs):
    sides = lay.sides
    mine, refs = refs[:parts], refs[parts:]
    theirs, refs = refs[:parts], refs[parts:]
    grads, refs = refs[:sides], refs[sides:]
    if came is not None:
        arrived, refs = refs[0], refs[1:]
    if not first:
        refs = refs[1:]
    out, refs = refs[0], refs[1:]
    if sides == 2:
        far, refs = refs[0], refs[1:]
    own, sems, came_sems = refs
    height = mine[0].shape[0]
    width = parts * height
    side = (lax.axis_index("dp") // 2) % sides
    copies = []
    if came is not None:
        copies = place(
            lay, came[0], 1 - side, came[1], arrived.shape[1] // 2, rows, arrived, out, came_sems
        )
        for copy in copies:
            copy.start()
    for x in reversed(range(sides)):
        target = own if x == 0 else far
        for k, group in enumerate((mine, theirs)):
            for p, piece in enumerate(group):
                target[:, k * width + p * height : k * width + (p + 1) * height] = lax.dot_general(
                    grads[x][...],
                    piece[...],
                    (((1,), (1,)), ((), ())),
                    preferred_element_type=f32,
                ).astype(bf16)
    owns = place(lay, s, side, low, width, rows, own, out, sems)
    for copy in owns:
        copy.start()
    for copy in owns + copies:
        copy.wait()


def last_kernel(lay, rows, blocks, *refs):
    arrived, (before, out, sems) = refs[: len(blocks)], refs[len(blocks) :]
    side = (lax.axis_index("dp") // 2) % lay.sides
    copies = []
    for k, (s, low) in enumerate(blocks):
        wide = arrived[k].shape[1] // 2
        copies += place(lay, s, 1 - side, low, wide, rows, arrived[k], out, sems.at[k])
    for copy in copies:
        copy.start()
    for copy in copies:
        copy.wait()


def back_kernel(lay, owned, basis, near, other, master, out, update):
    index = lax.axis_index("dp")
    half = lay.n // 2
    for j in range(lay.n):
        owner = index
        for bit in [1 << b for b in range(lay.n.bit_length() - 1)]:
            if slot_to_xor(lay, j) & bit:
                owner = flip(owner, bit)
        piece = near[j] if j < half else other[j - half]
        update[pl.ds(pl.multiple_of(owner * owned, owned), owned), :] = piece.astype(f32)
    out[...] = master[...] - step_size * jnp.dot(
        basis[...], update[...].astype(bf16), preferred_element_type=f32
    )


def slot_to_xor(lay, j):
    xor = 0
    for bit, radix in reversed(lay.rounds):
        xor += (j % radix) * bit
        j //= radix
    return xor


def call(kernel, name, shapes, args, in_specs=None, out_specs=None, scratch=(), flops=0, moved=2**20, **more):
    return pl.pallas_call(
        kernel,
        name=name,
        out_shape=[jax.ShapeDtypeStruct(shape, dtype) for shape, dtype in shapes],
        in_specs=in_specs or [VMEM] * len(args),
        out_specs=out_specs or [VMEM] * len(shapes),
        scratch_shapes=list(scratch),
        compiler_params=PARAMS,
        cost_estimate=pl.CostEstimate(flops=flops, bytes_accessed=moved, transcendentals=0),
        **more,
    )(*args)


def make_per_device(n):
    lay = Layout(n)
    sides, members, ring, rounds = lay.sides, lay.members, lay.ring, lay.rounds
    swap, onward = lay.swap, lay.onward

    def per_device(activations, key_grad, proj_basis, master_weight, first_moment, second_moment):
        tokens, width = activations.shape
        rows, rank = proj_basis.shape
        outs = key_grad.shape[1]
        owned = rank // n
        lines = -(-owned // 16) * 16
        parts = 2 if rows % 256 == 0 else 1
        height = rows // parts

        plan = [(x, 0, ring) for x in range(members)]
        wides = [ring * rows + (outs if x == 2 else 0) for x in range(members)]
        cut = call(
            functools.partial(cut_kernel, lay, rows, plan),
            "cut",
            [((tokens, wide), bf16) for wide in wides],
            [activations, key_grad],
            in_specs=[HBM, HBM],
            scratch=[pltpu.SemaphoreType.DMA((members * ring + 1,))],
            moved=4 * tokens * ring * rows * members,
        )

        acts = [cut[0]] + [swap(cut[x], x) for x in range(1, members)]
        moments = jnp.concatenate([first_moment, second_moment], axis=0).astype(bf16)
        folded = [moments[:, k * rank : (k + 1) * rank] for k in range(outs // rank)]
        basis = [after(jnp.concatenate([proj_basis] + folded, axis=0), cut[0])]
        for s in range(1, ring):
            basis.append(onward(basis[-1]))
        weight = [master_weight.astype(bf16)]
        weight.append(onward(after(weight[0], basis[-1])))

        if sides == 2:
            acts[2] = after(acts[2], basis[2])
            far_grad = acts[2][:, ring * rows :]
            near = swap(jnp.concatenate([key_grad, far_grad], axis=0), 1)
            grads = [key_grad, near[:tokens], far_grad, near[tokens:]]
        else:
            near = swap(key_grad, 1)
            grads = [key_grad, near]
        theirs = [swap(after(weight[0], basis[1]), 1)]

        side_grads = [key_grad, far_grad] if sides == 2 else [key_grad]
        state = {"out": None}
        waiting = []

        def multiply(s, mine, theirs, low=0, gate=None):
            args = [mine if gate is None else after(mine, gate), theirs] + side_grads
            in_specs = [VMEM] * len(args)
            wide = mine.shape[0]
            came = None
            if len(waiting) > 1:
                (came, block) = waiting.pop(0)
                args.append(block)
                in_specs.append(VMEM)
            first = state["out"] is None
            if not first:
                args.append(state["out"])
                in_specs.append(HBM)
            shapes, out_specs = [((tokens, width), bf16)], [HBM]
            if sides == 2:
                shapes.append(((tokens, 2 * wide), bf16))
                out_specs.append(VMEM)
            result = call(
                functools.partial(weight_kernel, lay, rows, s, low, 1, came, first),
                "weight",
                shapes,
                args,
                in_specs,
                out_specs,
                scratch=[
                    pltpu.VMEM((tokens, 2 * wide), bf16),
                    pltpu.SemaphoreType.DMA((2,)),
                    pltpu.SemaphoreType.DMA((2,)),
                ],
                flops=4 * sides * tokens * wide * outs,
                moved=6 * 2**20,
                input_output_aliases={} if first else {len(args) - 1: 0},
            )
            state["out"] = result[0]
            return result[1] if sides == 2 else result[0]

        def give_back(s, block, low=0, gate=None):
            if sides == 1:
                return block
            waiting.append(((s, low), swap(block if gate is None else after(block, gate), 2)))
            return waiting[-1][1]

        first_block = multiply(0, weight[0], theirs[0])
        total, *gives = call(
            functools.partial(project_kernel, lay, owned, plan),
            "project",
            [((n // 2, owned, outs), f32), ((n // 2, owned, outs), bf16)],
            [after(acts[0], first_block)] + acts[1:] + basis + grads,
            scratch=[pltpu.VMEM((rank, outs), f32)],
            flops=2 * tokens * members * rank * (ring * rows + outs),
            moved=12 * 2**20,
        )
        weight[1] = after(weight[1], total)
        weight.append(onward(weight[1]))
        theirs.append(swap(weight[1], 1))

        for k, (bit, radix) in enumerate(rounds):
            if bit == members:
                gives = [after(give, weight[2], sent if sides == 2 else block) for give in gives]
            came = [swap(give, j * bit) for j, give in zip(range(1, radix), gives)]
            if k == len(rounds) - 1:
                break
            next_bit, next_radix = rounds[k + 1]
            shape = (total.shape[0] // next_radix, owned, outs)
            total, *gives = call(
                functools.partial(fold_kernel, next_bit, next_radix, len(came)),
                "fold",
                [(shape, f32)] + [(shape, bf16)] * (next_radix - 1),
                [after(total, block) if bit == 2 else total] + came,
                moved=4 * total.size,
            )
            if bit == 1:
                block = multiply(1, weight[1], theirs[1], gate=total)
            if bit == 2:
                sent = give_back(0, first_block, gate=total)
                later = give_back(1, block, gate=total)
                weight[2] = after(weight[2], total, sent)

        owned_rows, message = call(
            functools.partial(square_kernel, len(came), lines),
            "square",
            [((owned, outs), f32), ((1, lines + 16, outs), bf16)],
            [total] + came,
        )
        their_step = swap(weight[2], 1)
        messages = message
        for bit, radix in reversed(rounds):
            if bit >= members:
                came = [swap(messages, j * bit) for j in range(1, radix)]
                messages = jnp.concatenate([messages] + came, axis=0)

        split = [weight[2][p * height : (p + 1) * height] for p in range(parts)] if ring == 4 else []
        last = [onward(after(piece, *came)) for piece in split[:1]]
        block = multiply(2, weight[2], their_step, gate=gives[0])
        (square,) = call(gathered_kernel, "gathered", [((8, 128), f32)], [messages])
        last += [onward(after(piece, square)) for piece in split[1:]]
        if sides == 2:
            sent = give_back(2, block, gate=later)
            square = after(square, sent)
        squares = [square] + [swap(square, x) for x in range(1, members)]
        new_first, new_second, update = call(
            functools.partial(moment_kernel, lay, rows),
            "moment",
            [((owned, outs), f32), ((owned, outs), f32), ((ring, owned, outs), bf16)],
            squares + basis + [owned_rows, first_moment, second_moment, messages],
        )
        if split:
            piece = after(last[0], update)
            block = multiply(3, piece, swap(piece, 1))
        whole = update
        for bit, radix in reversed(rounds[1:]):
            if bit < members:
                whole = jnp.concatenate([whole, after(swap(whole, bit), block)], axis=0)
        if split:
            sent = give_back(3, block, 0, whole)
        (new_master,) = call(
            functools.partial(back_kernel, lay, owned),
            "back",
            [(master_weight.shape, f32)],
            [proj_basis, whole, swap(whole, 1), master_weight],
            scratch=[pltpu.VMEM((rank, outs), f32)],
            flops=2 * rows * rank * outs,
            moved=8 * 2**20,
        )

        for p in range(1, len(split)):
            piece = after(last[p], sent)
            block = multiply(3, piece, swap(piece, 1), p * height)
            sent = give_back(3, block, p * height)
        if not split:
            for s in range(3, ring):
                weight.append(onward(weight[s - 1]))
                give_back(s, multiply(s, weight[s], swap(weight[s], 1)))
        activation_grad = state["out"]
        if waiting:
            (activation_grad,) = call(
                functools.partial(last_kernel, lay, rows, [spot for spot, block in waiting]),
                "last",
                [((tokens, width), bf16)],
                [after(block, new_master) for spot, block in waiting] + [activation_grad],
                [VMEM] * len(waiting) + [HBM],
                [HBM],
                scratch=[pltpu.SemaphoreType.DMA((len(waiting), 2))],
                input_output_aliases={len(waiting): 0},
            )
        return (activation_grad, new_master, new_first, new_second)

    return per_device


def solution(mesh):
    spec = P(("groups", "dp"), None)
    return jax.shard_map(
        make_per_device(mesh.shape["dp"]),
        mesh=mesh,
        in_specs=(spec,) * 6,
        out_specs=(spec,) * 4,
        check_vma=False,
    )
```

```python
import functools
import jax
import jax.numpy as jnp
from jax import lax
from jax.experimental import pallas as pl
from jax.experimental.pallas import tpu as pltpu
from jax.sharding import PartitionSpec as P

clip_total = 512.0
step_size = 0.01
first_fix = 1.0 - 0.9**10
second_fix = 1.0 - 0.99**10

f32 = jnp.float32
bf16 = jnp.bfloat16
HBM = pl.BlockSpec(memory_space=pl.ANY)
VMEM = pl.BlockSpec(memory_space=pltpu.VMEM)
PARAMS = pltpu.CompilerParams(vmem_limit_bytes=40 * 2**20)


def after(value, *others):
    return lax.optimization_barrier((value,) + others)[0]


class Layout:
    def __init__(self, n):
        self.n = n
        self.sides = 2 if n == 16 else 1
        self.members = 2 * self.sides
        self.ring = n // self.members
        ring, members = self.ring, self.members
        order = [0, 1, 3, 2] if ring == 4 else list(range(ring))
        self.forward = [
            (order[k] * members + m, order[(k + 1) % ring] * members + m)
            for k in range(ring)
            for m in range(members)
        ]
        self.rounds = [(1, 2)]
        bit = 2
        if self.sides == 2:
            self.rounds.append((2, 2))
            bit = 4
        while bit < n:
            radix = 4 if 2 * bit < n else 2
            self.rounds.append((bit, radix))
            bit *= radix

    def swap(self, value, bit):
        return lax.ppermute(value, "dp", [(i, i ^ bit) for i in range(self.n)])

    def onward(self, value):
        return lax.ppermute(value, "dp", self.forward)

    def source(self, index, s):
        z = index // self.members
        if self.ring != 4:
            return (z - s + self.ring) % self.ring
        k = (z + z // 2 * (5 - 2 * z) - s + 4) % 4
        return k + k // 2 * (5 - 2 * k)


def flip(value, bit):
    return value + bit - 2 * bit * ((value // bit) % 2)


def cut_kernel(lay, rows, plan, act, key_grad, *refs):
    pieces, sems = refs[:-1], refs[-1]
    index = lax.axis_index("dp")
    member = index % lay.members
    copies = []
    for (x, first, count), piece in zip(plan, pieces):
        owner = member
        for bit in (1, 2):
            if x & bit:
                owner = flip(owner, bit)
        for s in range(first, first + count):
            start = pl.multiple_of((lay.source(index, s) * lay.members + owner) * rows, rows)
            copies.append(
                pltpu.make_async_copy(
                    act.at[:, pl.ds(start, rows)],
                    piece.at[:, pl.ds((s - first) * rows, rows)],
                    sems.at[len(copies)],
                )
            )
    if lay.sides == 2:
        copies.append(
            pltpu.make_async_copy(
                key_grad,
                pieces[2].at[:, pl.ds(lay.ring * rows, key_grad.shape[1])],
                sems.at[len(copies)],
            )
        )
    for copy in copies:
        copy.start()
    for copy in copies:
        copy.wait()


def project_kernel(lay, owned, plan, *refs):
    members, ring = lay.members, lay.ring
    acts, refs = refs[: len(plan)], refs[len(plan) :]
    basis, refs = refs[:ring], refs[ring:]
    grads, refs = refs[:members], refs[members:]
    kept, given, grad = refs
    rows = acts[0].shape[1] // ring
    core = lax.axis_index("dp") % 2
    for x in range(members):
        total = None
        for (x_, first, count), piece in zip(plan, acts):
            if x_ != x:
                continue
            for s in range(first, first + count):
                term = jnp.dot(
                    piece[:, (s - first) * rows : (s - first + 1) * rows],
                    basis[s][:rows, :],
                    preferred_element_type=f32,
                )
                total = term if total is None else total + term
        term = lax.dot_general(
            total.astype(bf16),
            grads[x][...],
            (((0,), (0,)), ((), ())),
            preferred_element_type=f32,
        )
        if x == 0:
            grad[...] = term
        else:
            grad[...] += term
    for i in range(lay.n // 2):
        kept[i] = grad[pl.ds(pl.multiple_of((2 * i + core) * owned, owned), owned), :]
        given[i] = grad[pl.ds(pl.multiple_of((2 * i + 1 - core) * owned, owned), owned), :].astype(bf16)


def fold_kernel(bit, radix, came, *refs):
    kept, arrived, outs = refs[0], refs[1 : 1 + came], refs[1 + came :]
    digit = (lax.axis_index("dp") // bit) % radix

    def block(i):
        total = kept[i]
        for piece in arrived:
            total = total + piece[i].astype(f32)
        return total

    for i in range(kept.shape[0] // radix):
        for j in range(radix):
            other = digit
            for b in (1, 2):
                if j & b:
                    other = flip(other, b)
            value = block(i * radix + other)
            outs[j][i] = value.astype(outs[j].dtype)


def square_kernel(came, lines, *refs):
    kept, arrived, (owned, message) = refs[0], refs[1 : 1 + came], refs[1 + came :]
    total = kept[0]
    for piece in arrived:
        total = total + piece[0].astype(f32)
    owned[...] = total
    count = total.shape[0]
    square = jnp.full((16, total.shape[1]), jnp.sum(total * total), f32)
    first = square.astype(bf16).astype(f32)
    second = (square - first).astype(bf16).astype(f32)
    third = square - first - second
    row = lax.broadcasted_iota(jnp.int32, square.shape, 0)
    terms = jnp.where(row == 0, first, jnp.where(row == 1, second, jnp.where(row == 2, third, 0.0)))
    if count < lines:
        total = jnp.concatenate([total, jnp.zeros((lines - count, total.shape[1]), f32)], axis=0)
    message[0, :lines, :] = total.astype(bf16)
    message[0, lines:, :] = terms.astype(bf16)


def gathered_kernel(messages, square):
    lines = messages.shape[1] - 16
    total = jnp.zeros((16, 128), f32)
    for j in range(messages.shape[0]):
        total = total + messages[j, lines:, 0:128].astype(f32)
    square[...] = jnp.full(square.shape, jnp.sum(total[:, 0:1]), f32)


def moment_kernel(lay, rows, *refs):
    squares, refs = refs[: lay.members], refs[lay.members :]
    basis, refs = refs[: lay.ring], refs[lay.ring :]
    owned, first, second, messages, new_first, new_second, update = refs
    total = squares[0][...]
    for square in squares[1:]:
        total = total + square[...]
    factor = jnp.minimum(1.0, clip_total / (jnp.sqrt(total) + 1e-06))[0:1, 0:1]

    def advance(gradient, one, two):
        clipped = gradient * factor
        one = 0.9 * one + 0.1 * clipped
        two = 0.99 * two + 0.01 * clipped * clipped
        return one, two

    one, two = advance(owned[...], first[...], second[...])
    new_first[...] = one
    new_second[...] = two
    count = owned.shape[0]
    half = owned.shape[1] // 2
    index = lax.axis_index("dp")
    for s in range(lay.ring):
        xor = lax.bitwise_xor(lay.source(index, s), index // lay.members)
        slot = place_slot(lay, xor)
        for k in range(2):
            low = rows + k * 2 * count
            moments = basis[s][low : low + 2 * count, :].astype(f32)
            gradient = messages[slot, :, k * half : (k + 1) * half].astype(f32)[:count]
            one, two = advance(gradient, moments[:count], moments[count:])
            update[slot, :, k * half : (k + 1) * half] = (
                one / first_fix / (jnp.sqrt(two / second_fix) + 1e-08)
            ).astype(bf16)


def place_slot(lay, xor):
    slot, scale = 0, 1
    for bit, radix in reversed(lay.rounds):
        if bit >= lay.members:
            slot = slot + scale * ((xor // (bit // lay.members)) % radix)
            scale *= radix
    return slot


def place(lay, s, side, low, width, rows, source, out, sems):
    index = lax.axis_index("dp")
    core = index % 2
    chip = lay.source(index, s) * lay.sides + side
    copies = []
    for k, owner in enumerate((core, 1 - core)):
        start = pl.multiple_of((chip * 2 + owner) * rows + low, width)
        copies.append(
            pltpu.make_async_copy(
                source.at[:, pl.ds(k * width, width)],
                out.at[:, pl.ds(start, width)],
                sems.at[k],
            )
        )
    return copies


def weight_kernel(lay, rows, s, low, height, parts, came, first, *refs):
    sides = lay.sides
    mine, refs = refs[:parts], refs[parts:]
    theirs, refs = refs[:parts], refs[parts:]
    grads, refs = refs[:sides], refs[sides:]
    if came is not None:
        arrived, refs = refs[0], refs[1:]
    if not first:
        refs = refs[1:]
    out, refs = refs[0], refs[1:]
    if sides == 2:
        far, refs = refs[0], refs[1:]
    own, sems, came_sems = refs
    width = parts * height
    side = (lax.axis_index("dp") // 2) % sides
    copies = []
    if came is not None:
        copies = place(
            lay, came[0], 1 - side, came[1], arrived.shape[1] // 2, rows, arrived, out, came_sems
        )
        for copy in copies:
            copy.start()
    for x in reversed(range(sides)):
        target = own if x == 0 else far
        for k, group in enumerate((mine, theirs)):
            for p, piece in enumerate(group):
                target[:, k * width + p * height : k * width + (p + 1) * height] = lax.dot_general(
                    grads[x][...],
                    piece[...] if piece.shape[0] == height else piece[low : low + height, :],
                    (((1,), (1,)), ((), ())),
                    preferred_element_type=f32,
                ).astype(bf16)
    owns = place(lay, s, side, low, width, rows, own, out, sems)
    for copy in owns:
        copy.start()
    for copy in owns + copies:
        copy.wait()


def last_kernel(lay, rows, blocks, *refs):
    arrived, (before, out, sems) = refs[: len(blocks)], refs[len(blocks) :]
    side = (lax.axis_index("dp") // 2) % lay.sides
    copies = []
    for k, (s, low) in enumerate(blocks):
        wide = arrived[k].shape[1] // 2
        copies += place(lay, s, 1 - side, low, wide, rows, arrived[k], out, sems.at[k])
    for copy in copies:
        copy.start()
    for copy in copies:
        copy.wait()


def back_kernel(lay, owned, basis, near, other, master, out, update):
    index = lax.axis_index("dp")
    half = lay.n // 2
    for j in range(lay.n):
        owner = index
        for bit in [1 << b for b in range(lay.n.bit_length() - 1)]:
            if slot_to_xor(lay, j) & bit:
                owner = flip(owner, bit)
        piece = near[j] if j < half else other[j - half]
        update[pl.ds(pl.multiple_of(owner * owned, owned), owned), :] = piece.astype(f32)
    out[...] = master[...] - step_size * jnp.dot(
        basis[...], update[...].astype(bf16), preferred_element_type=f32
    )


def slot_to_xor(lay, j):
    xor = 0
    for bit, radix in reversed(lay.rounds):
        xor += (j % radix) * bit
        j //= radix
    return xor


def call(kernel, name, shapes, args, in_specs=None, out_specs=None, scratch=(), flops=0, moved=2**20, **more):
    return pl.pallas_call(
        kernel,
        name=name,
        out_shape=[jax.ShapeDtypeStruct(shape, dtype) for shape, dtype in shapes],
        in_specs=in_specs or [VMEM] * len(args),
        out_specs=out_specs or [VMEM] * len(shapes),
        scratch_shapes=list(scratch),
        compiler_params=PARAMS,
        cost_estimate=pl.CostEstimate(flops=flops, bytes_accessed=moved, transcendentals=0),
        **more,
    )(*args)


def make_per_device(n):
    lay = Layout(n)
    sides, members, ring, rounds = lay.sides, lay.members, lay.ring, lay.rounds
    swap, onward = lay.swap, lay.onward

    def per_device(activations, key_grad, proj_basis, master_weight, first_moment, second_moment):
        tokens, width = activations.shape
        rows, rank = proj_basis.shape
        outs = key_grad.shape[1]
        owned = rank // n
        lines = -(-owned // 16) * 16
        parts = 2 if rows % 256 == 0 else 1
        height = rows // parts

        plan = [(x, 0, ring) for x in range(members)]
        wides = [ring * rows + (outs if x == 2 else 0) for x in range(members)]
        cut = call(
            functools.partial(cut_kernel, lay, rows, plan),
            "cut",
            [((tokens, wide), bf16) for wide in wides],
            [activations, key_grad],
            in_specs=[HBM, HBM],
            scratch=[pltpu.SemaphoreType.DMA((members * ring + 1,))],
            moved=4 * tokens * ring * rows * members,
        )

        acts = [cut[0]] + [swap(cut[x], x) for x in range(1, members)]
        moments = jnp.concatenate([first_moment, second_moment], axis=0).astype(bf16)
        folded = [moments[:, k * rank : (k + 1) * rank] for k in range(outs // rank)]
        basis = [after(jnp.concatenate([proj_basis] + folded, axis=0), cut[0])]
        for s in range(1, ring):
            basis.append(onward(basis[-1]))
        weight = [master_weight.astype(bf16)]
        weight.append(onward(after(weight[0], basis[-1])))

        if sides == 2:
            acts[2] = after(acts[2], basis[2])
            far_grad = acts[2][:, ring * rows :]
            near = swap(jnp.concatenate([key_grad, far_grad], axis=0), 1)
            grads = [key_grad, near[:tokens], far_grad, near[tokens:]]
        else:
            near = swap(key_grad, 1)
            grads = [key_grad, near]
        theirs = [swap(after(weight[0], basis[1]), 1)]

        side_grads = [key_grad, far_grad] if sides == 2 else [key_grad]
        state = {"out": None}
        waiting = []

        def multiply(s, mine, theirs, low=0, gate=None, wide=rows):
            args = [mine if gate is None else after(mine, gate), theirs] + side_grads
            in_specs = [VMEM] * len(args)
            came = None
            if len(waiting) > 1:
                (came, block) = waiting.pop(0)
                args.append(block)
                in_specs.append(VMEM)
            first = state["out"] is None
            if not first:
                args.append(state["out"])
                in_specs.append(HBM)
            shapes, out_specs = [((tokens, width), bf16)], [HBM]
            if sides == 2:
                shapes.append(((tokens, 2 * wide), bf16))
                out_specs.append(VMEM)
            result = call(
                functools.partial(weight_kernel, lay, rows, s, low, wide, 1, came, first),
                "weight",
                shapes,
                args,
                in_specs,
                out_specs,
                scratch=[
                    pltpu.VMEM((tokens, 2 * wide), bf16),
                    pltpu.SemaphoreType.DMA((2,)),
                    pltpu.SemaphoreType.DMA((2,)),
                ],
                flops=4 * sides * tokens * wide * outs,
                moved=6 * 2**20,
                input_output_aliases={} if first else {len(args) - 1: 0},
            )
            state["out"] = result[0]
            return result[1] if sides == 2 else result[0]

        def give_back(s, block, low=0, gate=None):
            if sides == 1:
                return block
            waiting.append(((s, low), swap(block if gate is None else after(block, gate), 2)))
            return waiting[-1][1]

        first_block = multiply(0, weight[0], theirs[0])
        total, *gives = call(
            functools.partial(project_kernel, lay, owned, plan),
            "project",
            [((n // 2, owned, outs), f32), ((n // 2, owned, outs), bf16)],
            [after(acts[0], first_block)] + acts[1:] + basis + grads,
            scratch=[pltpu.VMEM((rank, outs), f32)],
            flops=2 * tokens * members * rank * (ring * rows + outs),
            moved=12 * 2**20,
        )
        weight[1] = after(weight[1], total)
        weight.append(onward(weight[1]))
        theirs.append(swap(weight[1], 1))

        for k, (bit, radix) in enumerate(rounds):
            if bit == members:
                gives = [after(give, weight[2], sent if sides == 2 else block) for give in gives]
            came = [swap(give, j * bit) for j, give in zip(range(1, radix), gives)]
            if k == len(rounds) - 1:
                break
            next_bit, next_radix = rounds[k + 1]
            shape = (total.shape[0] // next_radix, owned, outs)
            total, *gives = call(
                functools.partial(fold_kernel, next_bit, next_radix, len(came)),
                "fold",
                [(shape, f32)] + [(shape, bf16)] * (next_radix - 1),
                [after(total, block) if bit == 2 else total] + came,
                moved=4 * total.size,
            )
            if bit == 1:
                block = multiply(1, weight[1], theirs[1], gate=total)
            if bit == 2:
                sent = give_back(0, first_block, gate=total)
                later = give_back(1, block, gate=total)
                weight[2] = after(weight[2], total, sent)

        owned_rows, message = call(
            functools.partial(square_kernel, len(came), lines),
            "square",
            [((owned, outs), f32), ((1, lines + 16, outs), bf16)],
            [total] + came,
        )
        their_step = swap(weight[2], 1)
        messages = after(message, later) if sides == 2 else message
        for bit, radix in reversed(rounds):
            if bit >= members:
                came = [swap(messages, j * bit) for j in range(1, radix)]
                messages = jnp.concatenate([messages] + came, axis=0)

        block = multiply(2, weight[2], their_step, gate=gives[0])
        if ring == 4:
            weight.append(onward(after(weight[2], *came)))
        (square,) = call(gathered_kernel, "gathered", [((8, 128), f32)], [messages])
        if sides == 2:
            square = after(square, block)
        squares = [square] + [swap(square, x) for x in range(1, members)]
        new_first, new_second, update = call(
            functools.partial(moment_kernel, lay, rows),
            "moment",
            [((owned, outs), f32), ((owned, outs), f32), ((ring, owned, outs), bf16)],
            squares + basis + [owned_rows, first_moment, second_moment, messages],
        )
        sent = give_back(2, block, gate=squares[-1])
        whole = update
        for bit, radix in reversed(rounds[1:]):
            if bit < members:
                whole = jnp.concatenate([whole, swap(whole, bit)], axis=0)
        (new_master,) = call(
            functools.partial(back_kernel, lay, owned),
            "back",
            [(master_weight.shape, f32)],
            [proj_basis, whole, swap(whole, 1), master_weight],
            scratch=[pltpu.VMEM((rank, outs), f32)],
            flops=2 * rows * rank * outs,
            moved=8 * 2**20,
        )

        for s in range(3, ring):
            if len(weight) <= s:
                weight.append(onward(weight[s - 1]))
            mine = after(weight[s], whole, sent)
            other = swap(mine, 1)
            for p in range(parts):
                block = multiply(s, mine, other, p * height, wide=height)
                give_back(s, block, p * height)
        activation_grad = state["out"]
        if waiting:
            (activation_grad,) = call(
                functools.partial(last_kernel, lay, rows, [spot for spot, block in waiting]),
                "last",
                [((tokens, width), bf16)],
                [after(block, new_master) for spot, block in waiting] + [activation_grad],
                [VMEM] * len(waiting) + [HBM],
                [HBM],
                scratch=[pltpu.SemaphoreType.DMA((len(waiting), 2))],
                input_output_aliases={len(waiting): 0},
            )
        return (activation_grad, new_master, new_first, new_second)

    return per_device


def solution(mesh):
    spec = P(("groups", "dp"), None)
    return jax.shard_map(
        make_per_device(mesh.shape["dp"]),
        mesh=mesh,
        in_specs=(spec,) * 6,
        out_specs=(spec,) * 4,
        check_vma=False,
    )
```
